32 devices in a mesh: seq: 8 (over y, x, core), batch: 4 (over z).
Axes of the slice: x: 2, y: 2, z: 4, core: 2. Of those that a mesh axis runs over, the one named last changes fastest.
Arguments:
- hidden_in: bfloat16 [8, 1024, 768], P('batch', 'seq'), may hold values from -6 to 6
- lengths: int32 [8], P('batch'), may hold values from 1 to 1024, as said below
- attn_weight: bfloat16 [768, 2304], P(('seq', 'batch')), may hold values from -0.21875 to 0.21875
- attn_bias: bfloat16 [2304], P(('seq', 'batch')), may hold values from -0.4375 to 0.4375
- proj_weight: bfloat16 [768, 768], P(('seq', 'batch')), may hold values from -6 to 6
- proj_bias: bfloat16 [768], P(('seq', 'batch')), may hold values from -4 to 4
- first_gain: bfloat16 [768], P(('seq', 'batch')), may hold values from 0.5 to 1.5
- first_shift: bfloat16 [768], P(('seq', 'batch')), may hold values from -4 to 4
- up_weight: bfloat16 [768, 3072], P(('seq', 'batch')), may hold values from -0.21875 to 0.21875
- up_bias: bfloat16 [3072], P(('seq', 'batch')), may hold values from -4 to 4
- down_weight: bfloat16 [3072, 768], P(('seq', 'batch')), may hold values from -0.109375 to 0.109375
- down_bias: bfloat16 [768], P(('seq', 'batch')), may hold values from -4 to 4
- second_gain: bfloat16 [768], P(('seq', 'batch')), may hold values from 0.5 to 1.5
- second_shift: bfloat16 [768], P(('seq', 'batch')), may hold values from -4 to 4
- grad_out: bfloat16 [8, 1024, 768], P('batch', 'seq'), may hold values from -6 to 6
Outputs:
- layer_out: bfloat16 [8, 1024, 768], P('batch', 'seq')
- grad_hidden: float32 [8, 1024, 768], P('batch', 'seq')
- grad_attn_weight: float32 [768, 2304], P(('seq', 'batch'))
- grad_attn_bias: float32 [1536], P(('seq', 'batch'))
- grad_value_bias: float32 [768], P(('seq', 'batch'))
- grad_proj_weight: float32 [768, 768], P(('seq', 'batch'))
- grad_proj_bias: float32 [768], P(('seq', 'batch'))
- grad_first_gain: float32 [768], P(('seq', 'batch'))
- grad_first_shift: float32 [768], P(('seq', 'batch'))
- grad_up_weight: float32 [768, 3072], P(('seq', 'batch'))
- grad_up_bias: float32 [3072], P(('seq', 'batch'))
- grad_down_weight: float32 [3072, 768], P(('seq', 'batch'))
- grad_down_bias: float32 [768], P(('seq', 'batch'))
- grad_second_gain: float32 [768], P(('seq', 'batch'))
- grad_second_shift: float32 [768], P(('seq', 'batch'))
The draws below stay inside these ranges and needn't reach their ends.
Inputs may be any that keep to these rules, and one draw needn't show every extreme that they name: `lengths`: within the 2 entries of each index of batch at least one equals 1024; some entry equals 1.
All inputs are finite; a program needn't handle non-finite values.
Results may differ from the reference program's by a relative error of at most 0.02.
Values may be sent and summed in bfloat16 or wider, within the bound.
No kernel may reach another device: no remote copies, remote signals or barrier semaphores. Data moves between devices by JAX's collectives and lax.ppermute only.
A program may use at most 128 MiB of HBM per device.

```python
import math
import jax
import jax.numpy as jnp
from jax import lax

HEADS = 12
HEAD_DIM = 64
D = 768
FF = 3072
SEQS = 2
LEN = 1024
SEQ_ALL = 8


def draw_lengths(key, part):
    key = jax.random.fold_in(key, 11)
    groups = SEQ_ALL // SEQS
    split_one, split_two = jax.random.split(key)
    drawn = jax.random.randint(split_one, (groups, SEQS), 1, LEN + 1)
    full_slot = jax.random.randint(split_two, (groups,), 0, SEQS)
    slots = jnp.arange(SEQS, dtype=jnp.int32)[None, :]
    drawn = jnp.where(slots == full_slot[:, None], LEN, drawn)
    short_slot = (full_slot[0] + 1) % SEQS
    drawn = drawn.at[0, short_slot].set(1)
    return drawn.reshape(SEQ_ALL).astype(jnp.int32)


def levels(key, dims, pieces, least, largest):
    level = 1.0
    for position, blocks in pieces:
        draws = jax.random.uniform(jax.random.fold_in(jax.random.fold_in(key, 6), position), (blocks,), jnp.float32, least / len(pieces), largest / len(pieces))
        level = level * jnp.repeat(jnp.exp(draws), dims[position] // blocks).reshape((-1,) + (1,) * (len(dims) - 1 - position))
    return level


def centred(stream_key, shape, width, bound, pieces=(), kind=jnp.bfloat16):
    values = width * jax.random.normal(stream_key, shape, jnp.float32)
    if pieces:
        values = values * levels(stream_key, shape, pieces, -0.22, 0.18)
    return jnp.clip(values, -bound, bound).astype(kind)


def setup_inputs(seed: int = 0) -> dict:
    key_list = jax.random.split(jax.random.key(seed), 16)
    hidden_in = centred(key_list[0], (SEQ_ALL, LEN, D), 1.0, 6.0, ((0, 4), (1, 8)))
    lengths = draw_lengths(jax.random.fold_in(key_list[15], 71), 0)
    attn_weight = centred(key_list[2], (D, 3 * D), D ** -0.5, 0.21875, ((0, 32),))
    attn_bias = centred(key_list[3], (3 * D,), 0.03, 0.4375, ((0, 32),))
    proj_weight = centred(key_list[4], (D, D), (((LEN // 2) ** 0.5) * D ** -0.5), 6.0, ((0, 32),))
    proj_bias = centred(key_list[5], (D,), 0.3, 4.0, ((0, 32),))
    first_gain = jnp.clip(1.0 + 0.1 * jax.random.normal(key_list[6], (D,), jnp.float32), 0.5, 1.5).astype(jnp.bfloat16)
    first_shift = centred(key_list[7], (D,), 0.3, 4.0, ((0, 32),))
    up_weight = centred(key_list[8], (D, FF), D ** -0.5, 0.21875, ((0, 32),))
    up_bias = centred(key_list[9], (FF,), 0.3, 4.0, ((0, 32),))
    down_weight = centred(key_list[10], (FF, D), FF ** -0.5, 0.109375, ((0, 32),))
    down_bias = centred(key_list[11], (D,), 0.3, 4.0, ((0, 32),))
    second_gain = jnp.clip(1.0 + 0.1 * jax.random.normal(key_list[12], (D,), jnp.float32), 0.5, 1.5).astype(jnp.bfloat16)
    second_shift = centred(key_list[13], (D,), 0.3, 4.0, ((0, 32),))
    grad_out = centred(key_list[14], (SEQ_ALL, LEN, D), 1.0, 6.0, ((0, 4), (1, 8)))
    return {"hidden_in": hidden_in, "lengths": lengths, "attn_weight": attn_weight, "attn_bias": attn_bias, "proj_weight": proj_weight, "proj_bias": proj_bias, "first_gain": first_gain, "first_shift": first_shift, "up_weight": up_weight, "up_bias": up_bias, "down_weight": down_weight, "down_bias": down_bias, "second_gain": second_gain, "second_shift": second_shift, "grad_out": grad_out}


HIGHEST = lax.Precision.HIGHEST
EPSILON = 1e-12
NEG_BIG = -1e+30

@jax.custom_vjp
def low(v):
    return lax.optimization_barrier(v.astype(jnp.bfloat16)).astype(jnp.float32)

@jax.custom_vjp
def low_back(v):
    return v

def low_keep(v):
    return (low(v), None)

def low_pass(kept, grad):
    return (grad,)

def back_keep(v):
    return (v, None)

def back_low(kept, grad):
    return (low(grad),)
low.defvjp(low_keep, low_pass)
low_back.defvjp(back_keep, back_low)

def matmul_high(left, right):
    return jnp.dot(left, right, precision=HIGHEST)

def rotate(vectors, positions):
    half_dim = vectors.shape[-1] // 2
    frequency = 10000.0 ** (-2.0 * jnp.arange(half_dim, dtype=jnp.float32) / vectors.shape[-1])
    angles = positions[:, None] * frequency[None, :]
    cosine = jnp.cos(angles)[:, None, :]
    sine_part = jnp.sin(angles)[:, None, :]
    split_pairs = vectors.reshape(vectors.shape[:-1] + (half_dim, 2))
    even_part = split_pairs[..., 0]
    odd_part = split_pairs[..., 1]
    turned = jnp.stack([even_part * cosine - odd_part * sine_part, odd_part * cosine + even_part * sine_part], axis=-1)
    return turned.reshape(vectors.shape)

def layer_norm(residual, scale_gain, shift_bias):
    row_mean = lax.optimization_barrier(jnp.mean(residual, axis=-1, keepdims=True))
    centered = residual - row_mean
    variance = lax.optimization_barrier(jnp.mean(centered * centered, axis=-1, keepdims=True))
    return centered * lax.rsqrt(variance + EPSILON) * scale_gain + shift_bias

def attention(queries, keys, values, lengths):
    span_rows = queries.shape[1]
    block_rows = math.gcd(span_rows, 512)
    score_scale = HEAD_DIM ** (-0.5)

    def one_sequence(packed):
        seq_queries, seq_keys, seq_values, seq_length = packed
        key_valid = (jnp.arange(span_rows, dtype=jnp.int32) < seq_length)[None, None, :]

        def one_block(block_queries):
            scores = low_back(score_scale * jnp.einsum('qhd,khd->hqk', block_queries, seq_keys, precision=HIGHEST))
            scores = jnp.where(key_valid, scores, NEG_BIG)
            row_max = lax.optimization_barrier(jnp.max(scores, axis=-1, keepdims=True))
            weights = jnp.where(key_valid, jnp.exp(scores - row_max), 0.0)
            row_sum = lax.optimization_barrier(jnp.sum(weights, axis=-1))
            unnormed = low_back(jnp.einsum('hqk,khd->qhd', low(weights), seq_values, precision=HIGHEST))
            return unnormed / jnp.transpose(row_sum)[:, :, None]
        blocks = seq_queries.reshape(span_rows // block_rows, block_rows, HEADS, HEAD_DIM)
        return lax.map(jax.checkpoint(one_block), blocks).reshape(span_rows, HEADS, HEAD_DIM)
    return lax.map(one_sequence, (queries, keys, values, lengths))

def layer(hidden, attn_weight, attn_bias, proj_weight, proj_bias, first_gain, first_shift, up_weight, up_bias, down_weight, down_bias, second_gain, second_shift, lengths):
    seq_count, span_rows, model_width = hidden.shape
    tokens_flat = hidden.reshape(seq_count * span_rows, model_width)
    projected = low_back(matmul_high(tokens_flat, attn_weight) + attn_bias)
    projected = projected.reshape(seq_count, span_rows, 3, HEADS, HEAD_DIM)
    positions = jnp.arange(span_rows, dtype=jnp.float32)
    queries = low(rotate(projected[:, :, 0], positions))
    keys = low(rotate(projected[:, :, 1], positions))
    values = low(projected[:, :, 2])
    attended = attention(queries, keys, values, lengths)
    attn_rows = low_back(low(attended.reshape(seq_count * span_rows, model_width)))
    mixed = low_back(matmul_high(attn_rows, proj_weight) + proj_bias)
    normed = layer_norm(tokens_flat + mixed, first_gain, first_shift)
    upward = low_back(matmul_high(low(normed), up_weight) + up_bias)
    active = jax.nn.gelu(upward, approximate=False)
    downward = low_back(matmul_high(low(active), down_weight) + down_bias)
    return layer_norm(normed + downward, second_gain, second_shift).reshape(seq_count, span_rows, model_width)

def reference(hidden_in, lengths, attn_weight, attn_bias, proj_weight, proj_bias, first_gain, first_shift, up_weight, up_bias, down_weight, down_bias, second_gain, second_shift, grad_out):
    weight_list = tuple((weight_item.astype(jnp.float32) for weight_item in (attn_weight, attn_bias, proj_weight, proj_bias, first_gain, first_shift, up_weight, up_bias, down_weight, down_bias, second_gain, second_shift)))

    def forward(hidden, *weights_now):
        return layer(hidden, *weights_now, lengths)
    layer_out, pull_back = jax.vjp(forward, hidden_in.astype(jnp.float32), *weight_list)
    span_rows = hidden_in.shape[1]
    model_width = hidden_in.shape[2]
    row_valid = (jnp.arange(span_rows, dtype=jnp.int32)[None, :] < lengths[:, None]).astype(jnp.float32)
    cotangent = grad_out.astype(jnp.float32) * row_valid[:, :, None]
    gradients = pull_back(cotangent)
    bias_grad = gradients[2]
    return (layer_out.astype(jnp.bfloat16), gradients[0], gradients[1], bias_grad[:2 * model_width], bias_grad[2 * model_width:], gradients[3], gradients[4], gradients[5], gradients[6], gradients[7], gradients[8], gradients[9], gradients[10], gradients[11], gradients[12])
```

```python
import jax
import jax.numpy as jnp
from jax import lax
from jax.sharding import PartitionSpec as P

HEADS = 12
HEAD_DIM = 64


EPSILON = 1e-12
NEG_BIG = -1e30


def passed_along(value, axis, steps):
    count = lax.axis_size(axis)
    pairs = [(source, (source + steps) % count) for source in range(count)]
    return lax.ppermute(value, axis, pairs)


def rotate(vectors, positions):
    half_dim = vectors.shape[-1] // 2
    frequency = 10000.0 ** (-2.0 * jnp.arange(half_dim, dtype=jnp.float32) / vectors.shape[-1])
    angles = positions[:, None] * frequency[None, :]
    cosine = jnp.cos(angles)[:, None, :]
    sine_part = jnp.sin(angles)[:, None, :]
    split_pairs = vectors.reshape(vectors.shape[:-1] + (half_dim, 2))
    even_part = split_pairs[..., 0]
    odd_part = split_pairs[..., 1]
    turned = jnp.stack(
        [even_part * cosine - odd_part * sine_part, odd_part * cosine + even_part * sine_part],
        axis=-1,
    )
    return turned.reshape(vectors.shape)


def layer_norm(residual, scale_gain, shift_bias):
    row_mean = jnp.mean(residual, axis=-1, keepdims=True)
    centered = residual - row_mean
    variance = jnp.mean(centered * centered, axis=-1, keepdims=True)
    return centered * lax.rsqrt(variance + EPSILON) * scale_gain + shift_bias


def gelu_exact(upward):
    return jax.nn.gelu(upward, approximate=False)


def run_blocks(step_fn, carry_now, key_piece, first_row, block_keys):
    row_count = key_piece.shape[1]
    width_now = block_keys if row_count % block_keys == 0 else row_count

    def one_turn(index, carry_in):
        begin_at = index * width_now
        sub_piece = lax.dynamic_slice_in_dim(key_piece, begin_at, width_now, 1)
        return step_fn(carry_in, sub_piece, first_row + begin_at)

    return lax.fori_loop(0, row_count // width_now, one_turn, carry_now)


def on_device(
    hidden_in,
    lengths,
    attn_weight,
    attn_bias,
    proj_weight,
    proj_bias,
    first_gain,
    first_shift,
    up_weight,
    up_bias,
    down_weight,
    down_bias,
    second_gain,
    second_shift,
    grad_out,
):
    seq_count, span_rows, model_width = hidden_in.shape
    token_count = seq_count * span_rows
    seq_devices = lax.axis_size("seq")
    my_index = lax.axis_index("seq")
    block_keys = max(span_rows, 512)
    score_scale = HEAD_DIM ** (-0.5)
    offset = my_index * span_rows
    row_index = offset + jnp.arange(span_rows, dtype=jnp.int32)
    positions = row_index.astype(jnp.float32)
    attn_full, attn_bias_full, proj_full, proj_bias_full, gain_one, shift_one = (
        lax.all_gather(attn_weight, ("seq", "batch"), axis=0, tiled=True),
        lax.all_gather(attn_bias, ("seq", "batch"), axis=0, tiled=True),
        lax.all_gather(proj_weight, ("seq", "batch"), axis=0, tiled=True),
        lax.all_gather(proj_bias, ("seq", "batch"), axis=0, tiled=True),
        lax.all_gather(first_gain, ("seq", "batch"), axis=0, tiled=True),
        lax.all_gather(first_shift, ("seq", "batch"), axis=0, tiled=True),
    )
    up_full, up_bias_full, down_full, down_bias_full, gain_two, shift_two = (
        lax.all_gather(up_weight, ("seq", "batch"), axis=0, tiled=True),
        lax.all_gather(up_bias, ("seq", "batch"), axis=0, tiled=True),
        lax.all_gather(down_weight, ("seq", "batch"), axis=0, tiled=True),
        lax.all_gather(down_bias, ("seq", "batch"), axis=0, tiled=True),
        lax.all_gather(second_gain, ("seq", "batch"), axis=0, tiled=True),
        lax.all_gather(second_shift, ("seq", "batch"), axis=0, tiled=True),
    )
    tokens_flat = hidden_in.reshape(token_count, model_width)
    projected = jnp.dot(
        tokens_flat, attn_full, preferred_element_type=jnp.float32
    ) + attn_bias_full.astype(jnp.float32)
    projected = projected.reshape(seq_count, span_rows, 3, HEADS, HEAD_DIM)
    queries = rotate(projected[:, :, 0], positions).astype(jnp.bfloat16)
    keys_low = rotate(projected[:, :, 1], positions).astype(jnp.bfloat16)
    values_low = projected[:, :, 2].astype(jnp.bfloat16)
    key_values = jnp.concatenate(
        [
            keys_low.reshape(seq_count, span_rows, model_width),
            values_low.reshape(seq_count, span_rows, model_width),
        ],
        axis=-1,
    )

    def key_mask(first_row, row_count):
        key_rows = first_row + jnp.arange(row_count, dtype=jnp.int32)
        return (key_rows[None, :] < lengths[:, None])[:, None, None, :]

    def split_pairs(key_piece):
        row_count = key_piece.shape[1]
        keys_part = key_piece[:, :, :model_width].reshape(seq_count, row_count, HEADS, HEAD_DIM)
        values_part = key_piece[:, :, model_width:].reshape(seq_count, row_count, HEADS, HEAD_DIM)
        return (keys_part, values_part)

    def attend_step(carry_in, key_piece, first_row):
        row_max, row_sum, accum = carry_in
        keys_part, values_part = split_pairs(key_piece)
        masked = key_mask(first_row, key_piece.shape[1])
        scores = score_scale * jnp.einsum(
            "sqhd,skhd->shqk", queries, keys_part, preferred_element_type=jnp.float32
        )
        scores = jnp.where(masked, scores, NEG_BIG)
        new_max = jnp.maximum(row_max, jnp.max(scores, axis=-1))
        weights = jnp.where(masked, jnp.exp(scores - new_max[..., None]), 0.0)
        factor = jnp.exp(row_max - new_max)
        row_sum = row_sum * factor + jnp.sum(weights, axis=-1)
        accum = accum * jnp.transpose(factor, (0, 2, 1))[..., None] + jnp.einsum(
            "shqk,skhd->sqhd",
            weights.astype(jnp.bfloat16),
            values_part,
            preferred_element_type=jnp.float32,
        )
        return (new_max, row_sum, accum)

    start_state = (
        jnp.full((seq_count, HEADS, span_rows), NEG_BIG, jnp.float32),
        jnp.zeros((seq_count, HEADS, span_rows), jnp.float32),
        jnp.zeros((seq_count, span_rows, HEADS, HEAD_DIM), jnp.float32),
    )
    row_max, row_sum, accum = run_blocks(
        attend_step,
        start_state,
        lax.all_gather(key_values, "seq", axis=1, tiled=True),
        jnp.int32(0),
        block_keys,
    )
    sum_view = jnp.transpose(row_sum, (0, 2, 1))[..., None]
    attended = accum / sum_view
    attn_rows = attended.reshape(token_count, model_width).astype(jnp.bfloat16)
    mixed = jnp.dot(
        attn_rows, proj_full, preferred_element_type=jnp.float32
    ) + proj_bias_full.astype(jnp.float32)
    normed, norm_back_one = jax.vjp(
        layer_norm,
        tokens_flat.astype(jnp.float32) + mixed,
        gain_one.astype(jnp.float32),
        shift_one.astype(jnp.float32),
    )
    normed_low = normed.astype(jnp.bfloat16)
    upward = jnp.dot(normed_low, up_full, preferred_element_type=jnp.float32) + up_bias_full.astype(
        jnp.float32
    )
    active, gelu_back = jax.vjp(gelu_exact, upward)
    active_low = active.astype(jnp.bfloat16)
    downward = jnp.dot(
        active_low, down_full, preferred_element_type=jnp.float32
    ) + down_bias_full.astype(jnp.float32)
    output_rows, norm_back_two = jax.vjp(
        layer_norm, normed + downward, gain_two.astype(jnp.float32), shift_two.astype(jnp.float32)
    )
    layer_out = output_rows.reshape(seq_count, span_rows, model_width).astype(jnp.bfloat16)
    row_valid = (row_index[None, :] < lengths[:, None]).astype(jnp.float32)
    cotangent = (grad_out.astype(jnp.float32) * row_valid[:, :, None]).reshape(
        token_count, model_width
    )
    d_resid_two, d_gain_two, d_shift_two = norm_back_two(cotangent)
    d_down = d_resid_two.astype(jnp.bfloat16)
    d_down_bias = jnp.sum(d_down.astype(jnp.float32), axis=0)
    d_down_weight = jnp.einsum("tf,td->fd", active_low, d_down, preferred_element_type=jnp.float32)
    d_active = jnp.dot(d_down, down_full.T, preferred_element_type=jnp.float32)
    (d_upward,) = gelu_back(d_active)
    d_up = d_upward.astype(jnp.bfloat16)
    d_up_bias = jnp.sum(d_up.astype(jnp.float32), axis=0)
    d_up_weight = jnp.einsum("td,tf->df", normed_low, d_up, preferred_element_type=jnp.float32)
    d_normed = d_resid_two + jnp.dot(d_up, up_full.T, preferred_element_type=jnp.float32)
    ffn_parts = (
        lax.psum_scatter(d_up_weight, ("seq", "batch"), scatter_dimension=0, tiled=True),
        lax.psum_scatter(d_up_bias, ("seq", "batch"), scatter_dimension=0, tiled=True),
        lax.psum_scatter(d_down_weight, ("seq", "batch"), scatter_dimension=0, tiled=True),
        lax.psum_scatter(d_down_bias, ("seq", "batch"), scatter_dimension=0, tiled=True),
        lax.psum_scatter(d_gain_two, ("seq", "batch"), scatter_dimension=0, tiled=True),
        lax.psum_scatter(d_shift_two, ("seq", "batch"), scatter_dimension=0, tiled=True),
    )
    d_resid_one, d_gain_one, d_shift_one = norm_back_one(d_normed)
    d_mixed = d_resid_one.astype(jnp.bfloat16)
    d_proj_bias = jnp.sum(d_mixed.astype(jnp.float32), axis=0)
    d_proj_weight = jnp.einsum("td,te->de", attn_rows, d_mixed, preferred_element_type=jnp.float32)
    d_attended = jnp.dot(d_mixed, proj_full.T, preferred_element_type=jnp.float32).astype(
        jnp.bfloat16
    )
    d_attended = d_attended.astype(jnp.float32).reshape(seq_count, span_rows, HEADS, HEAD_DIM)
    delta = jnp.transpose(jnp.sum(d_attended * attended, axis=-1), (0, 2, 1))
    delta_scaled = delta / row_sum
    guide = (d_attended / sum_view).astype(jnp.bfloat16)

    def back_step(carry_in, key_piece, first_row):
        d_queries, buffer = carry_in
        keys_part, values_part = split_pairs(key_piece)
        row_count = key_piece.shape[1]
        masked = key_mask(first_row, row_count)
        scores = score_scale * jnp.einsum(
            "sqhd,skhd->shqk", queries, keys_part, preferred_element_type=jnp.float32
        )
        scores = jnp.where(masked, scores, NEG_BIG)
        weights = jnp.where(masked, jnp.exp(scores - row_max[..., None]), 0.0)
        d_weights = jnp.einsum(
            "sqhd,skhd->shqk", guide, values_part, preferred_element_type=jnp.float32
        )
        d_scores = (weights * (d_weights - delta_scaled[..., None])).astype(jnp.bfloat16)
        d_queries = d_queries + score_scale * jnp.einsum(
            "shqk,skhd->sqhd", d_scores, keys_part, preferred_element_type=jnp.float32
        )
        d_keys = score_scale * jnp.einsum(
            "shqk,sqhd->skhd", d_scores, queries, preferred_element_type=jnp.float32
        )
        d_values = jnp.einsum(
            "shqk,sqhd->skhd",
            weights.astype(jnp.bfloat16),
            guide,
            preferred_element_type=jnp.float32,
        )
        new_terms = jnp.concatenate(
            [
                d_keys.reshape(seq_count, row_count, model_width),
                d_values.reshape(seq_count, row_count, model_width),
            ],
            axis=-1,
        )
        current = buffer
        buffer = current + new_terms
        return (d_queries, buffer)

    zero_queries = jnp.zeros((seq_count, span_rows, HEADS, HEAD_DIM), jnp.float32)

    def cycle_turn(turn, carry_in):
        d_queries, pair_piece, grad_piece = carry_in
        owner = (my_index - turn) % seq_devices
        base_row = owner * span_rows

        def owner_step(inner, key_piece, first_row):
            return back_step(inner, key_piece, first_row)

        d_queries, grad_piece = run_blocks(
            owner_step, (d_queries, grad_piece), pair_piece, base_row, block_keys
        )
        grad_piece = passed_along(grad_piece.astype(jnp.bfloat16), "seq", 1).astype(
            grad_piece.dtype
        )
        pair_piece = passed_along(pair_piece, "seq", 1)
        return (d_queries, pair_piece, grad_piece)

    start_cycle = (
        zero_queries,
        key_values,
        jnp.zeros((seq_count, span_rows, 2 * model_width), jnp.float32),
    )
    d_queries, pair_spent, d_pairs = lax.fori_loop(0, seq_devices, cycle_turn, start_cycle)
    d_keys_own = d_pairs[:, :, :model_width].reshape(seq_count, span_rows, HEADS, HEAD_DIM)
    d_values_own = d_pairs[:, :, model_width:].reshape(seq_count, span_rows, HEADS, HEAD_DIM)
    d_projected = jnp.stack(
        [rotate(d_queries, -positions), rotate(d_keys_own, -positions), d_values_own], axis=2
    )
    d_projected = d_projected.reshape(token_count, 3 * model_width).astype(jnp.bfloat16)
    d_attn_bias = jnp.sum(d_projected.astype(jnp.float32), axis=0)
    d_pair_bias = d_attn_bias[: 2 * model_width]
    d_value_bias = d_attn_bias[2 * model_width :]
    d_attn_weight = jnp.einsum(
        "td,tf->df", tokens_flat, d_projected, preferred_element_type=jnp.float32
    )
    grad_hidden = d_resid_one + jnp.dot(
        d_projected, attn_full.T, preferred_element_type=jnp.float32
    )
    attn_parts = (
        lax.psum_scatter(d_attn_weight, ("seq", "batch"), scatter_dimension=0, tiled=True),
        lax.psum_scatter(d_pair_bias, ("seq", "batch"), scatter_dimension=0, tiled=True),
        lax.psum_scatter(d_value_bias, ("seq", "batch"), scatter_dimension=0, tiled=True),
        lax.psum_scatter(d_proj_weight, ("seq", "batch"), scatter_dimension=0, tiled=True),
        lax.psum_scatter(d_proj_bias, ("seq", "batch"), scatter_dimension=0, tiled=True),
        lax.psum_scatter(d_gain_one, ("seq", "batch"), scatter_dimension=0, tiled=True),
        lax.psum_scatter(d_shift_one, ("seq", "batch"), scatter_dimension=0, tiled=True),
    )
    return (
        layer_out,
        grad_hidden.reshape(seq_count, span_rows, model_width),
        attn_parts[0],
        attn_parts[1],
        attn_parts[2],
        attn_parts[3],
        attn_parts[4],
        attn_parts[5],
        attn_parts[6],
        ffn_parts[0],
        ffn_parts[1],
        ffn_parts[2],
        ffn_parts[3],
        ffn_parts[4],
        ffn_parts[5],
    )


SEQ_SIDE = 8
BATCH_SIDE = 4
GROUP = 192
EVEN = (0, 2, 4, 6)
ODD = (1, 3, 5, 7)


def swap_seq(value, mask):
    return lax.ppermute(value, "seq", [(i, i ^ mask) for i in range(SEQ_SIDE)])


def swap_batch(value, mask):
    return lax.ppermute(value, "batch", [(i, i ^ mask) for i in range(BATCH_SIDE)])


def in_order(bit, mine, other, axis):
    low = jnp.where(bit == 0, mine, other)
    high = jnp.where(bit == 0, other, mine)
    return jnp.stack([low, high], axis=axis)


def pick(value, index, axis=0):
    return lax.dynamic_index_in_dim(value, index, axis, keepdims=False)


def turn(vectors, cosine, sine):
    left = jnp.roll(vectors, -1, axis=-1)
    right = jnp.roll(vectors, 1, axis=-1)
    even = (jnp.arange(vectors.shape[-1]) % 2) == 0
    return vectors * cosine + jnp.where(even, left, right) * sine


def gather_up(piece, x, y, z):
    far = [swap_batch(piece, k) for k in (1, 2, 3)]
    stacked = jnp.stack([piece] + far, axis=0)
    column = jnp.stack([pick(stacked, k ^ z) for k in range(4)], axis=1)
    n = piece.shape[-1]
    column = column.reshape(2, 96, n)
    first, second = column[0], column[1]
    first = in_order(x, first, swap_seq(first, 2), 0)
    second = in_order(y, second, swap_seq(second, 4), 0)
    first = in_order(y, first, swap_seq(first, 4), 0)
    second = in_order(x, second, swap_seq(second, 2), 1)
    return jnp.stack([first, second], axis=2).reshape(768, n)


def gather_down(piece, x, y, z):
    far = [swap_batch(piece, k) for k in (1, 2, 3)]
    stacked = jnp.stack([piece] + far, axis=0)
    column = jnp.stack([pick(stacked, k ^ z) for k in range(4)], axis=0)
    n = piece.shape[-1]
    first, second = column[:2], column[2:]
    first = in_order(x, first, swap_seq(first, 2), 0)
    second = in_order(y, second, swap_seq(second, 4), 0)
    first = in_order(y, first, swap_seq(first, 4), 0)
    second = in_order(x, second, swap_seq(second, 2), 1)
    return jnp.concatenate([first, second], axis=2).reshape(1536, n)


def add_low(left, right):
    return (left.astype(jnp.float32) + right.astype(jnp.float32)).astype(jnp.bfloat16)


def halve(value, bit, mask, axis):
    return add_low(pick(value, bit, axis), swap_seq(pick(value, 1 - bit, axis), mask))


def scatter_last(value, z):
    total = pick(value, z).astype(jnp.float32)
    for k in (1, 2, 3):
        total = total + swap_batch(pick(value, z ^ k), k).astype(jnp.float32)
    return total


def scatter_up(value, x, y, z):
    n = value.shape[-1]
    value = value.reshape(2, 2, 2, 96, n)
    first, second = value[:, :, 0], value[:, :, 1]
    first = halve(halve(first, y, 4, 0), x, 2, 0)
    second = halve(halve(second, x, 2, 1), y, 4, 0)
    both = jnp.stack([first, second], axis=0).reshape(2, 4, 24, n)
    return scatter_last(jnp.transpose(both, (1, 0, 2, 3)), z)


def scatter_down(value, x, y, z):
    n = value.shape[-1]
    value = value.reshape(2, 2, 4, 96, n)
    first, second = value[:, :, :2], value[:, :, 2:]
    first = halve(halve(first, y, 4, 0), x, 2, 0)
    second = halve(halve(second, x, 2, 1), y, 4, 0)
    return scatter_last(jnp.concatenate([first, second], axis=0), z)


def split_layer(
    hidden_in,
    lengths,
    attn_weight,
    attn_bias,
    proj_weight,
    proj_bias,
    first_gain,
    first_shift,
    up_weight,
    up_bias,
    down_weight,
    down_bias,
    second_gain,
    second_shift,
    grad_out,
):
    both_axes = ("seq", "batch")
    f32, bf16 = jnp.float32, jnp.bfloat16
    _, span_rows, width = hidden_in.shape
    hidden_units = up_weight.shape[1]
    rows_all = SEQ_SIDE * span_rows
    s = lax.axis_index("seq")
    z = lax.axis_index("batch")
    core, x, y = s & 1, (s >> 1) & 1, s >> 2
    group = s & 3
    scale = HEAD_DIM ** (-0.5)
    heads_here = GROUP // HEAD_DIM

    small = jnp.concatenate(
        [attn_bias, proj_bias, first_gain, first_shift, down_bias, second_gain, second_shift, up_bias]
    )
    small_all = lax.all_gather(small[None], both_axes, axis=0, tiled=True).astype(f32)
    attn_bias_all = small_all[:, :72].reshape(3, 4, GROUP)
    vectors = [small_all[:, 72 + 24 * i : 96 + 24 * i].reshape(width) for i in range(6)]
    proj_bias_all, gain_one, shift_one, down_bias_all, gain_two, shift_two = vectors
    up_bias_all = small_all[:, 216:].reshape(4, 2, 384)
    up_bias_here = pick(up_bias_all, core, 1).reshape(1536)
    bias_here = pick(attn_bias_all, group, 1).reshape(3 * GROUP)

    by_group = attn_weight.reshape(24, 3, 4, GROUP).transpose(2, 0, 1, 3).reshape(4, 24, 3 * GROUP)
    sent = jnp.broadcast_to(by_group[None, :, None], (2, 4, 4, 24, 3 * GROUP)).reshape(
        32, 24, 3 * GROUP
    )
    weight_here = lax.all_to_all(sent, both_axes, 0, 0, tiled=True).reshape(width, 3 * GROUP)

    mine = pick(hidden_in, y)
    other = pick(hidden_in, 1 - y)
    even_rows = jnp.concatenate([mine, swap_seq(mine, 2), swap_seq(other, 4), swap_seq(other, 6)])
    rows_here = jnp.concatenate([even_rows, swap_seq(even_rows, 1)])
    block_owner = jnp.array([s ^ j for j in EVEN + ODD])
    positions = (block_owner[:, None] * span_rows + jnp.arange(span_rows)[None, :]).reshape(-1)
    length = pick(lengths, y)

    up_view = up_weight.reshape(24, 4, 2, 384)
    proj_view = proj_weight.reshape(24, 2, 384)

    def half_rows(which):
        return jnp.concatenate(
            [pick(up_view, which, 2).reshape(24, 1536), pick(proj_view, which, 1)], axis=-1
        )

    chip_rows = in_order(core, half_rows(core), swap_seq(half_rows(1 - core), 1), 0)
    up_proj = gather_up(chip_rows, x, y, z)
    up_here = up_proj[:, :1536]
    proj_half = up_proj[:, 1536:]
    proj_all = in_order(core, proj_half, swap_seq(proj_half, 1), 1).reshape(width, width)
    down_here = gather_down(down_weight, x, y, z)

    projected = jnp.dot(rows_here, weight_here, preferred_element_type=f32) + bias_here
    frequency = 10000.0 ** (-2.0 * (jnp.arange(HEAD_DIM) // 2).astype(f32) / HEAD_DIM)
    angles = positions.astype(f32)[:, None] * frequency[None, :]
    cosine = jnp.tile(jnp.cos(angles), (1, heads_here))
    sine = jnp.tile(
        jnp.sin(angles) * jnp.where(jnp.arange(HEAD_DIM) % 2 == 0, -1.0, 1.0), (1, heads_here)
    )

    def by_head(value):
        return value.reshape(rows_all, heads_here, HEAD_DIM).transpose(1, 0, 2)

    def merged(value):
        return value.transpose(1, 0, 2).reshape(rows_all, GROUP)

    queries = by_head(turn(projected[:, :GROUP], cosine, sine).astype(bf16))
    keys = by_head(turn(projected[:, GROUP : 2 * GROUP], cosine, sine).astype(bf16))
    values = by_head(projected[:, 2 * GROUP :].astype(bf16))
    valid = (positions < length)[None, None, :]
    scores = scale * jnp.einsum("hqd,hkd->hqk", queries, keys, preferred_element_type=f32)
    scores = jnp.where(valid, scores, NEG_BIG)
    row_max = jnp.max(scores, axis=-1, keepdims=True)
    weights = jnp.where(valid, jnp.exp(scores - row_max), 0.0)
    row_sum = jnp.sum(weights, axis=-1, keepdims=True)
    weights_low = weights.astype(bf16)
    attended = (
        jnp.einsum("hqk,hkd->hqd", weights_low, values, preferred_element_type=f32) / row_sum
    )

    sent = merged(attended).astype(bf16).reshape(8, span_rows, GROUP)
    came = swap_seq(sent[4:], 1)
    pair = jnp.concatenate(
        [jnp.where(core == 0, sent[:4], came), jnp.where(core == 0, came, sent[:4])], axis=-1
    )

    def columns(mine_part, other_part):
        return jnp.concatenate(
            [
                jnp.where(x == 0, mine_part, other_part),
                jnp.where(x == 0, other_part, mine_part),
            ],
            axis=-1,
        )

    attn_rows = jnp.concatenate(
        [
            columns(pair[0], swap_seq(pair[1], 2)),
            columns(swap_seq(pair[2], 4), swap_seq(pair[3], 6)),
        ],
        axis=0,
    )
    tokens = jnp.concatenate([mine, other], axis=0)

    mixed = jnp.dot(attn_rows, proj_all, preferred_element_type=f32) + proj_bias_all
    normed, norm_back_one = jax.vjp(layer_norm, tokens.astype(f32) + mixed, gain_one, shift_one)
    normed_mine = normed.astype(bf16)
    normed_low = jnp.concatenate([normed_mine, swap_seq(normed_mine, 1)], axis=0)
    upward = jnp.dot(normed_low, up_here, preferred_element_type=f32) + up_bias_here
    active, gelu_back = jax.vjp(gelu_exact, upward)
    active_low = active.astype(bf16)
    part = jnp.dot(active_low, down_here, preferred_element_type=f32)
    downward = part[:256] + swap_seq(part[256:].astype(bf16), 1).astype(f32) + down_bias_all
    output_rows, norm_back_two = jax.vjp(layer_norm, normed + downward, gain_two, shift_two)

    row_index = s * span_rows + jnp.arange(span_rows, dtype=jnp.int32)

    def by_sequence(value, dtype):
        value = value.reshape(2, span_rows, width)
        return jnp.where(y == 0, value, value[::-1]).astype(dtype)

    layer_out = by_sequence(output_rows, bf16)
    lengths_here = jnp.stack([length, pick(lengths, 1 - y)])
    row_valid = (row_index[None, :] < lengths_here[:, None]).astype(f32).reshape(-1, 1)
    cotangent = (
        jnp.concatenate([pick(grad_out, y), pick(grad_out, 1 - y)], axis=0).astype(f32) * row_valid
    )
    d_resid_two, d_gain_two, d_shift_two = norm_back_two(cotangent)
    d_down_mine = d_resid_two.astype(bf16)
    d_down_bias = jnp.sum(d_down_mine.astype(f32), axis=0)
    d_down = jnp.concatenate([d_down_mine, swap_seq(d_down_mine, 1)], axis=0)
    d_down_weight = jnp.einsum("tf,td->fd", active_low, d_down, preferred_element_type=f32)
    grad_down_weight = scatter_down(d_down_weight.astype(bf16), x, y, z)
    d_active = jnp.dot(d_down, down_here.T, preferred_element_type=f32)
    (d_upward,) = gelu_back(d_active)
    d_up = d_upward.astype(bf16)
    d_up_bias = jnp.sum(d_up.astype(f32), axis=0)
    d_up_weight = jnp.einsum("td,tf->df", normed_low, d_up, preferred_element_type=f32)
    part = jnp.dot(d_up, up_here.T, preferred_element_type=f32)
    d_normed = d_resid_two + part[:256] + swap_seq(part[256:].astype(bf16), 1).astype(f32)
    d_resid_one, d_gain_one, d_shift_one = norm_back_one(d_normed)
    d_mixed = d_resid_one.astype(bf16)
    d_proj_bias = jnp.sum(d_mixed.astype(f32), axis=0)
    d_proj_weight = jnp.einsum("td,te->de", attn_rows, d_mixed, preferred_element_type=f32)
    d_attended = jnp.dot(d_mixed, proj_all.T, preferred_element_type=f32).astype(bf16)

    d_proj_view = d_proj_weight.astype(bf16).reshape(width, 2, 384)
    d_proj_half = halve(d_proj_view, core, 1, 1)
    d_up_proj = jnp.concatenate([d_up_weight.astype(bf16), d_proj_half], axis=-1)
    d_chip_rows = scatter_up(d_up_proj, x, y, z)
    d_sent = pick(d_chip_rows, 1 - core).astype(bf16)
    d_came = swap_seq(d_sent, 1).astype(f32)
    d_own = pick(d_chip_rows, core)
    low_half = jnp.where(core == 0, d_own, d_came)
    high_half = jnp.where(core == 0, d_came, d_own)
    grad_up_weight = jnp.stack(
        [low_half[:, :1536].reshape(24, 4, 384), high_half[:, :1536].reshape(24, 4, 384)], axis=2
    ).reshape(24, hidden_units)
    grad_proj_weight = jnp.concatenate([low_half[:, 1536:], high_half[:, 1536:]], axis=-1)

    d_view = d_attended.reshape(2, span_rows, 2, 384)
    d_here, d_there = pick(d_view, x, 2), pick(d_view, 1 - x, 2)
    d_even = jnp.stack(
        [d_here[0], swap_seq(d_there[0], 2), swap_seq(d_here[1], 4), swap_seq(d_there[1], 6)]
    ).reshape(4, span_rows, 2, GROUP)
    d_even_mine = pick(d_even, core, 2)
    d_odd = swap_seq(pick(d_even, 1 - core, 2), 1)
    d_att = by_head(jnp.concatenate([d_even_mine, d_odd]).reshape(rows_all, GROUP)).astype(f32)
    delta = jnp.sum(d_att * attended, axis=-1, keepdims=True) / row_sum
    guide = (d_att / row_sum).astype(bf16)
    d_weights = jnp.einsum("hqd,hkd->hqk", guide, values, preferred_element_type=f32)
    d_scores = (weights * (d_weights - delta)).astype(bf16)
    d_queries = scale * jnp.einsum("hqk,hkd->hqd", d_scores, keys, preferred_element_type=f32)
    d_keys = scale * jnp.einsum("hqk,hqd->hkd", d_scores, queries, preferred_element_type=f32)
    d_values = jnp.einsum("hqk,hqd->hkd", weights_low, guide, preferred_element_type=f32)
    d_projected = jnp.concatenate(
        [
            turn(merged(d_queries), cosine, -sine),
            turn(merged(d_keys), cosine, -sine),
            merged(d_values),
        ],
        axis=-1,
    ).astype(bf16)
    d_bias_here = jnp.sum(d_projected.astype(f32), axis=0).reshape(3, 1, GROUP)
    d_attn_bias = jnp.where(jnp.arange(4)[None, :, None] == group, d_bias_here, 0.0).reshape(-1)
    d_weight_here = jnp.einsum("td,tf->df", rows_here, d_projected, preferred_element_type=f32)
    d_parts = lax.all_to_all(
        d_weight_here.astype(bf16).reshape(32, 24, 3 * GROUP), both_axes, 0, 0, tiled=True
    )
    d_parts = d_parts.reshape(2, 4, 4, 24, 3, GROUP).astype(f32)
    grad_attn_weight = (
        jnp.sum(d_parts, axis=(0, 2)).transpose(1, 2, 0, 3).reshape(24, 3 * width)
    )

    d_part = jnp.dot(d_projected, weight_here.T, preferred_element_type=f32)
    d_part = d_part.reshape(8, span_rows, width)
    d_blocks = d_part[:4] + swap_seq(d_part[4:].astype(bf16), 1).astype(f32)
    d_sends = d_blocks.astype(bf16)
    d_first = d_blocks[0] + swap_seq(d_sends[1], 2).astype(f32)
    d_second = swap_seq(d_sends[2], 4).astype(f32) + swap_seq(d_sends[3], 6).astype(f32)
    grad_hidden = by_sequence(d_resid_one + jnp.concatenate([d_first, d_second], axis=0), f32)

    d_up_bias_all = jnp.where(
        jnp.arange(2)[None, :, None] == core, d_up_bias.reshape(4, 1, 384), 0.0
    ).reshape(-1)
    d_small = jnp.concatenate(
        [
            d_attn_bias[: 2 * width].reshape(32, 48),
            d_attn_bias[2 * width :].reshape(32, 24),
            d_proj_bias.reshape(32, 24),
            d_gain_one.reshape(32, 24),
            d_shift_one.reshape(32, 24),
            d_down_bias.reshape(32, 24),
            d_gain_two.reshape(32, 24),
            d_shift_two.reshape(32, 24),
            d_up_bias_all.reshape(32, 96),
        ],
        axis=-1,
    )
    d_small = jnp.sum(lax.all_to_all(d_small, both_axes, 0, 0, tiled=True), axis=0)
    d_vectors = [d_small[72 + 24 * i : 96 + 24 * i] for i in range(6)]
    return (
        layer_out,
        grad_hidden,
        grad_attn_weight,
        d_small[:48],
        d_small[48:72],
        grad_proj_weight,
        d_vectors[0],
        d_vectors[1],
        d_vectors[2],
        grad_up_weight,
        d_small[216:],
        grad_down_weight,
        d_vectors[3],
        d_vectors[4],
        d_vectors[5],
    )


def solution(mesh):
    in_specs = (
        P("batch", "seq", None),
        P("batch"),
        P(("seq", "batch"), None),
        P(("seq", "batch")),
        P(("seq", "batch"), None),
        P(("seq", "batch")),
        P(("seq", "batch")),
        P(("seq", "batch")),
        P(("seq", "batch"), None),
        P(("seq", "batch")),
        P(("seq", "batch"), None),
        P(("seq", "batch")),
        P(("seq", "batch")),
        P(("seq", "batch")),
        P("batch", "seq", None),
    )
    out_specs = (
        P("batch", "seq", None),
        P("batch", "seq", None),
        P(("seq", "batch"), None),
        P(("seq", "batch")),
        P(("seq", "batch")),
        P(("seq", "batch"), None),
        P(("seq", "batch")),
        P(("seq", "batch")),
        P(("seq", "batch")),
        P(("seq", "batch"), None),
        P(("seq", "batch")),
        P(("seq", "batch"), None),
        P(("seq", "batch")),
        P(("seq", "batch")),
        P(("seq", "batch")),
    )
    fits = mesh.shape["seq"] == SEQ_SIDE and mesh.shape["batch"] == BATCH_SIDE
    return jax.shard_map(
        split_layer if fits else on_device, mesh=mesh, in_specs=in_specs, out_specs=out_specs, check_vma=False
    )
```

```python
import math

import jax
import jax.numpy as jnp
from jax import lax
from jax.experimental import pallas as pl
from jax.experimental.pallas import tpu as pltpu
from jax.sharding import PartitionSpec as P

HEADS = 12
HEAD_DIM = 64


EPSILON = 1e-12
NEG_BIG = -1e30


def passed_along(value, axis, steps):
    count = lax.axis_size(axis)
    pairs = [(source, (source + steps) % count) for source in range(count)]
    return lax.ppermute(value, axis, pairs)


def rotate(vectors, positions):
    half_dim = vectors.shape[-1] // 2
    frequency = 10000.0 ** (-2.0 * jnp.arange(half_dim, dtype=jnp.float32) / vectors.shape[-1])
    angles = positions[:, None] * frequency[None, :]
    cosine = jnp.cos(angles)[:, None, :]
    sine_part = jnp.sin(angles)[:, None, :]
    split_pairs = vectors.reshape(vectors.shape[:-1] + (half_dim, 2))
    even_part = split_pairs[..., 0]
    odd_part = split_pairs[..., 1]
    turned = jnp.stack(
        [even_part * cosine - odd_part * sine_part, odd_part * cosine + even_part * sine_part],
        axis=-1,
    )
    return turned.reshape(vectors.shape)


def layer_norm(residual, scale_gain, shift_bias):
    row_mean = jnp.mean(residual, axis=-1, keepdims=True)
    centered = residual - row_mean
    variance = jnp.mean(centered * centered, axis=-1, keepdims=True)
    return centered * lax.rsqrt(variance + EPSILON) * scale_gain + shift_bias


def gelu_exact(upward):
    return jax.nn.gelu(upward, approximate=False)


def run_blocks(step_fn, carry_now, key_piece, first_row, block_keys):
    row_count = key_piece.shape[1]
    width_now = block_keys if row_count % block_keys == 0 else row_count

    def one_turn(index, carry_in):
        begin_at = index * width_now
        sub_piece = lax.dynamic_slice_in_dim(key_piece, begin_at, width_now, 1)
        return step_fn(carry_in, sub_piece, first_row + begin_at)

    return lax.fori_loop(0, row_count // width_now, one_turn, carry_now)


def on_device(
    hidden_in,
    lengths,
    attn_weight,
    attn_bias,
    proj_weight,
    proj_bias,
    first_gain,
    first_shift,
    up_weight,
    up_bias,
    down_weight,
    down_bias,
    second_gain,
    second_shift,
    grad_out,
):
    seq_count, span_rows, model_width = hidden_in.shape
    token_count = seq_count * span_rows
    seq_devices = lax.axis_size("seq")
    my_index = lax.axis_index("seq")
    block_keys = max(span_rows, 512)
    score_scale = HEAD_DIM ** (-0.5)
    offset = my_index * span_rows
    row_index = offset + jnp.arange(span_rows, dtype=jnp.int32)
    positions = row_index.astype(jnp.float32)
    attn_full, attn_bias_full, proj_full, proj_bias_full, gain_one, shift_one = (
        lax.all_gather(attn_weight, ("seq", "batch"), axis=0, tiled=True),
        lax.all_gather(attn_bias, ("seq", "batch"), axis=0, tiled=True),
        lax.all_gather(proj_weight, ("seq", "batch"), axis=0, tiled=True),
        lax.all_gather(proj_bias, ("seq", "batch"), axis=0, tiled=True),
        lax.all_gather(first_gain, ("seq", "batch"), axis=0, tiled=True),
        lax.all_gather(first_shift, ("seq", "batch"), axis=0, tiled=True),
    )
    up_full, up_bias_full, down_full, down_bias_full, gain_two, shift_two = (
        lax.all_gather(up_weight, ("seq", "batch"), axis=0, tiled=True),
        lax.all_gather(up_bias, ("seq", "batch"), axis=0, tiled=True),
        lax.all_gather(down_weight, ("seq", "batch"), axis=0, tiled=True),
        lax.all_gather(down_bias, ("seq", "batch"), axis=0, tiled=True),
        lax.all_gather(second_gain, ("seq", "batch"), axis=0, tiled=True),
        lax.all_gather(second_shift, ("seq", "batch"), axis=0, tiled=True),
    )
    tokens_flat = hidden_in.reshape(token_count, model_width)
    projected = jnp.dot(
        tokens_flat, attn_full, preferred_element_type=jnp.float32
    ) + attn_bias_full.astype(jnp.float32)
    projected = projected.reshape(seq_count, span_rows, 3, HEADS, HEAD_DIM)
    queries = rotate(projected[:, :, 0], positions).astype(jnp.bfloat16)
    keys_low = rotate(projected[:, :, 1], positions).astype(jnp.bfloat16)
    values_low = projected[:, :, 2].astype(jnp.bfloat16)
    key_values = jnp.concatenate(
        [
            keys_low.reshape(seq_count, span_rows, model_width),
            values_low.reshape(seq_count, span_rows, model_width),
        ],
        axis=-1,
    )

    def key_mask(first_row, row_count):
        key_rows = first_row + jnp.arange(row_count, dtype=jnp.int32)
        return (key_rows[None, :] < lengths[:, None])[:, None, None, :]

    def split_pairs(key_piece):
        row_count = key_piece.shape[1]
        keys_part = key_piece[:, :, :model_width].reshape(seq_count, row_count, HEADS, HEAD_DIM)
        values_part = key_piece[:, :, model_width:].reshape(seq_count, row_count, HEADS, HEAD_DIM)
        return (keys_part, values_part)

    def attend_step(carry_in, key_piece, first_row):
        row_max, row_sum, accum = carry_in
        keys_part, values_part = split_pairs(key_piece)
        masked = key_mask(first_row, key_piece.shape[1])
        scores = score_scale * jnp.einsum(
            "sqhd,skhd->shqk", queries, keys_part, preferred_element_type=jnp.float32
        )
        scores = jnp.where(masked, scores, NEG_BIG)
        new_max = jnp.maximum(row_max, jnp.max(scores, axis=-1))
        weights = jnp.where(masked, jnp.exp(scores - new_max[..., None]), 0.0)
        factor = jnp.exp(row_max - new_max)
        row_sum = row_sum * factor + jnp.sum(weights, axis=-1)
        accum = accum * jnp.transpose(factor, (0, 2, 1))[..., None] + jnp.einsum(
            "shqk,skhd->sqhd",
            weights.astype(jnp.bfloat16),
            values_part,
            preferred_element_type=jnp.float32,
        )
        return (new_max, row_sum, accum)

    start_state = (
        jnp.full((seq_count, HEADS, span_rows), NEG_BIG, jnp.float32),
        jnp.zeros((seq_count, HEADS, span_rows), jnp.float32),
        jnp.zeros((seq_count, span_rows, HEADS, HEAD_DIM), jnp.float32),
    )
    row_max, row_sum, accum = run_blocks(
        attend_step,
        start_state,
        lax.all_gather(key_values, "seq", axis=1, tiled=True),
        jnp.int32(0),
        block_keys,
    )
    sum_view = jnp.transpose(row_sum, (0, 2, 1))[..., None]
    attended = accum / sum_view
    attn_rows = attended.reshape(token_count, model_width).astype(jnp.bfloat16)
    mixed = jnp.dot(
        attn_rows, proj_full, preferred_element_type=jnp.float32
    ) + proj_bias_full.astype(jnp.float32)
    normed, norm_back_one = jax.vjp(
        layer_norm,
        tokens_flat.astype(jnp.float32) + mixed,
        gain_one.astype(jnp.float32),
        shift_one.astype(jnp.float32),
    )
    normed_low = normed.astype(jnp.bfloat16)
    upward = jnp.dot(normed_low, up_full, preferred_element_type=jnp.float32) + up_bias_full.astype(
        jnp.float32
    )
    active, gelu_back = jax.vjp(gelu_exact, upward)
    active_low = active.astype(jnp.bfloat16)
    downward = jnp.dot(
        active_low, down_full, preferred_element_type=jnp.float32
    ) + down_bias_full.astype(jnp.float32)
    output_rows, norm_back_two = jax.vjp(
        layer_norm, normed + downward, gain_two.astype(jnp.float32), shift_two.astype(jnp.float32)
    )
    layer_out = output_rows.reshape(seq_count, span_rows, model_width).astype(jnp.bfloat16)
    row_valid = (row_index[None, :] < lengths[:, None]).astype(jnp.float32)
    cotangent = (grad_out.astype(jnp.float32) * row_valid[:, :, None]).reshape(
        token_count, model_width
    )
    d_resid_two, d_gain_two, d_shift_two = norm_back_two(cotangent)
    d_down = d_resid_two.astype(jnp.bfloat16)
    d_down_bias = jnp.sum(d_down.astype(jnp.float32), axis=0)
    d_down_weight = jnp.einsum("tf,td->fd", active_low, d_down, preferred_element_type=jnp.float32)
    d_active = jnp.dot(d_down, down_full.T, preferred_element_type=jnp.float32)
    (d_upward,) = gelu_back(d_active)
    d_up = d_upward.astype(jnp.bfloat16)
    d_up_bias = jnp.sum(d_up.astype(jnp.float32), axis=0)
    d_up_weight = jnp.einsum("td,tf->df", normed_low, d_up, preferred_element_type=jnp.float32)
    d_normed = d_resid_two + jnp.dot(d_up, up_full.T, preferred_element_type=jnp.float32)
    ffn_parts = (
        lax.psum_scatter(d_up_weight, ("seq", "batch"), scatter_dimension=0, tiled=True),
        lax.psum_scatter(d_up_bias, ("seq", "batch"), scatter_dimension=0, tiled=True),
        lax.psum_scatter(d_down_weight, ("seq", "batch"), scatter_dimension=0, tiled=True),
        lax.psum_scatter(d_down_bias, ("seq", "batch"), scatter_dimension=0, tiled=True),
        lax.psum_scatter(d_gain_two, ("seq", "batch"), scatter_dimension=0, tiled=True),
        lax.psum_scatter(d_shift_two, ("seq", "batch"), scatter_dimension=0, tiled=True),
    )
    d_resid_one, d_gain_one, d_shift_one = norm_back_one(d_normed)
    d_mixed = d_resid_one.astype(jnp.bfloat16)
    d_proj_bias = jnp.sum(d_mixed.astype(jnp.float32), axis=0)
    d_proj_weight = jnp.einsum("td,te->de", attn_rows, d_mixed, preferred_element_type=jnp.float32)
    d_attended = jnp.dot(d_mixed, proj_full.T, preferred_element_type=jnp.float32).astype(
        jnp.bfloat16
    )
    d_attended = d_attended.astype(jnp.float32).reshape(seq_count, span_rows, HEADS, HEAD_DIM)
    delta = jnp.transpose(jnp.sum(d_attended * attended, axis=-1), (0, 2, 1))
    delta_scaled = delta / row_sum
    guide = (d_attended / sum_view).astype(jnp.bfloat16)

    def back_step(carry_in, key_piece, first_row):
        d_queries, buffer = carry_in
        keys_part, values_part = split_pairs(key_piece)
        row_count = key_piece.shape[1]
        masked = key_mask(first_row, row_count)
        scores = score_scale * jnp.einsum(
            "sqhd,skhd->shqk", queries, keys_part, preferred_element_type=jnp.float32
        )
        scores = jnp.where(masked, scores, NEG_BIG)
        weights = jnp.where(masked, jnp.exp(scores - row_max[..., None]), 0.0)
        d_weights = jnp.einsum(
            "sqhd,skhd->shqk", guide, values_part, preferred_element_type=jnp.float32
        )
        d_scores = (weights * (d_weights - delta_scaled[..., None])).astype(jnp.bfloat16)
        d_queries = d_queries + score_scale * jnp.einsum(
            "shqk,skhd->sqhd", d_scores, keys_part, preferred_element_type=jnp.float32
        )
        d_keys = score_scale * jnp.einsum(
            "shqk,sqhd->skhd", d_scores, queries, preferred_element_type=jnp.float32
        )
        d_values = jnp.einsum(
            "shqk,sqhd->skhd",
            weights.astype(jnp.bfloat16),
            guide,
            preferred_element_type=jnp.float32,
        )
        new_terms = jnp.concatenate(
            [
                d_keys.reshape(seq_count, row_count, model_width),
                d_values.reshape(seq_count, row_count, model_width),
            ],
            axis=-1,
        )
        current = buffer
        buffer = current + new_terms
        return (d_queries, buffer)

    zero_queries = jnp.zeros((seq_count, span_rows, HEADS, HEAD_DIM), jnp.float32)

    def cycle_turn(turn, carry_in):
        d_queries, pair_piece, grad_piece = carry_in
        owner = (my_index - turn) % seq_devices
        base_row = owner * span_rows

        def owner_step(inner, key_piece, first_row):
            return back_step(inner, key_piece, first_row)

        d_queries, grad_piece = run_blocks(
            owner_step, (d_queries, grad_piece), pair_piece, base_row, block_keys
        )
        grad_piece = passed_along(grad_piece.astype(jnp.bfloat16), "seq", 1).astype(
            grad_piece.dtype
        )
        pair_piece = passed_along(pair_piece, "seq", 1)
        return (d_queries, pair_piece, grad_piece)

    start_cycle = (
        zero_queries,
        key_values,
        jnp.zeros((seq_count, span_rows, 2 * model_width), jnp.float32),
    )
    d_queries, pair_spent, d_pairs = lax.fori_loop(0, seq_devices, cycle_turn, start_cycle)
    d_keys_own = d_pairs[:, :, :model_width].reshape(seq_count, span_rows, HEADS, HEAD_DIM)
    d_values_own = d_pairs[:, :, model_width:].reshape(seq_count, span_rows, HEADS, HEAD_DIM)
    d_projected = jnp.stack(
        [rotate(d_queries, -positions), rotate(d_keys_own, -positions), d_values_own], axis=2
    )
    d_projected = d_projected.reshape(token_count, 3 * model_width).astype(jnp.bfloat16)
    d_attn_bias = jnp.sum(d_projected.astype(jnp.float32), axis=0)
    d_pair_bias = d_attn_bias[: 2 * model_width]
    d_value_bias = d_attn_bias[2 * model_width :]
    d_attn_weight = jnp.einsum(
        "td,tf->df", tokens_flat, d_projected, preferred_element_type=jnp.float32
    )
    grad_hidden = d_resid_one + jnp.dot(
        d_projected, attn_full.T, preferred_element_type=jnp.float32
    )
    attn_parts = (
        lax.psum_scatter(d_attn_weight, ("seq", "batch"), scatter_dimension=0, tiled=True),
        lax.psum_scatter(d_pair_bias, ("seq", "batch"), scatter_dimension=0, tiled=True),
        lax.psum_scatter(d_value_bias, ("seq", "batch"), scatter_dimension=0, tiled=True),
        lax.psum_scatter(d_proj_weight, ("seq", "batch"), scatter_dimension=0, tiled=True),
        lax.psum_scatter(d_proj_bias, ("seq", "batch"), scatter_dimension=0, tiled=True),
        lax.psum_scatter(d_gain_one, ("seq", "batch"), scatter_dimension=0, tiled=True),
        lax.psum_scatter(d_shift_one, ("seq", "batch"), scatter_dimension=0, tiled=True),
    )
    return (
        layer_out,
        grad_hidden.reshape(seq_count, span_rows, model_width),
        attn_parts[0],
        attn_parts[1],
        attn_parts[2],
        attn_parts[3],
        attn_parts[4],
        attn_parts[5],
        attn_parts[6],
        ffn_parts[0],
        ffn_parts[1],
        ffn_parts[2],
        ffn_parts[3],
        ffn_parts[4],
        ffn_parts[5],
    )


SEQ_SIDE = 8
BATCH_SIDE = 4
GROUP = 192
WIDE = 256
HERE = 3
EVEN = (0, 2, 4, 6)
ODD = (1, 3, 5, 7)
CORE, X, Y, Z, PLACE, LEN_MINE, LEN_OTHER, UNIT = range(8)
F32, BF16 = jnp.float32, jnp.bfloat16
NN = (((1,), (0,)), ((), ()))
NT = (((1,), (1,)), ((), ()))
TN = (((0,), (0,)), ((), ()))


def swap_seq(value, mask):
    return lax.ppermute(value, "seq", [(i, i ^ mask) for i in range(SEQ_SIDE)])


def swap_batch(value, mask):
    return lax.ppermute(value, "batch", [(i, i ^ mask) for i in range(BATCH_SIDE)])


def after(value, *done):
    return lax.optimization_barrier((value,) + done)[0]


def fence(*values):
    return lax.optimization_barrier(values)


def shape(dims, dtype=BF16):
    return jax.ShapeDtypeStruct(dims, dtype)


def call(body, outs, info, *args, scratch=(), flops=0, name=None, alone=False):
    moved = sum(a.size * a.dtype.itemsize for a in args)
    moved += sum(math.prod(o.shape) * o.dtype.itemsize for o in outs)
    held = sum(math.prod(m.shape) * m.dtype.itemsize for m in scratch)
    return pl.pallas_call(
        body,
        out_shape=outs,
        in_specs=[pl.BlockSpec(memory_space=pltpu.SMEM)]
        + [pl.BlockSpec(memory_space=pltpu.VMEM)] * len(args),
        out_specs=[pl.BlockSpec(memory_space=pltpu.VMEM)] * len(outs),
        scratch_shapes=[pltpu.VMEM(m.shape, m.dtype) for m in scratch],
        compiler_params=pltpu.CompilerParams(
            vmem_limit_bytes=60 << 20 if alone else min(56 << 20, moved + held + (16 << 20))
        ),
        cost_estimate=pl.CostEstimate(flops=flops, bytes_accessed=moved, transcendentals=0),
        name=name,
    )(info, *args)


def dot(left, right, dims=NN):
    return lax.dot_general(left, right, dims, preferred_element_type=F32)


def chips(info):
    x, y = info[X], info[Y]
    return ((y, x), (y, 1 - x), (1 - y, x), (1 - y, 1 - x))


def lanes(start, size):
    return pl.ds(pl.multiple_of(start, 128), size)


def rows(start, size, unit=16):
    return pl.ds(pl.multiple_of(start, unit), size)


def select_body(
    info, hidden, up, proj, v0, v1, v2, v3, v4, v5, v6, v7, mine, other, joined, small
):
    y = info[Y]
    mine[...] = hidden[y]
    other[...] = hidden[1 - y]
    joined[:, :3072] = up[...]
    joined[:, 3072:] = proj[...]
    parts = [v[...].astype(F32) for v in (v0, v1, v2, v3, v4, v5, v6, v7)]
    row = jnp.concatenate(parts + [jnp.zeros((1, 72), F32)], axis=1)
    small[...] = jnp.broadcast_to(row, (32, 384))


def by_batch(info, pieces):
    z = info[Z]
    values = [p[...].astype(F32) for p in pieces]
    ordered = []
    for zz in range(4):
        k = zz ^ z
        low = jnp.where(k == 0, values[0], values[1])
        high = jnp.where(k == 2, values[2], values[3])
        ordered.append(jnp.where(k < 2, low, high))
    return ordered


def attn_column_body(info, p0, p1, p2, p3, out):
    column = jnp.concatenate(by_batch(info, (p0, p1, p2, p3)), axis=0)
    for g in range(4):
        part = jnp.concatenate(
            [column[:, 768 * i + GROUP * g : 768 * i + GROUP * (g + 1)] for i in range(3)], axis=1
        ).astype(BF16)
        out[g] = part
        out[4 + g] = part


def up_column_body(info, p0, p1, p2, p3, keep, sent, proj, held):
    core = info[CORE]
    column = jnp.concatenate(by_batch(info, (p0, p1, p2, p3)), axis=0).astype(BF16)
    held[...] = column
    proj[...] = column[:, 3072:]
    for which, out in ((core, keep), (1 - core, sent)):
        for q in range(4):
            out[96 * (q // 2) : 96 * (q // 2 + 1), 384 * (q % 2) : 384 * (q % 2 + 1)] = held[
                :, lanes(768 * q + 384 * which, 384)
            ]


def up_join_body(info, keep, came, proj, out):
    out[0:96] = keep[:96]
    out[96:192] = came[:96]
    out[192:288] = keep[96:]
    out[288:384] = came[96:]
    out[384:480] = proj[...]


def down_column_body(info, p0, p1, p2, p3, out):
    z = info[Z]
    for k, p in enumerate((p0, p1, p2, p3)):
        out[rows((z ^ k) * 96, 96), :] = p[...]


def attend_body(
    info, mine, r2, r4, r6, odd, given, bias, cosine, sine, padding,
    x_out, weight, qt_out, k_out, v_out, att_out, stats, even_low, odd_low,
):
    weight[:, :, GROUP:] = jnp.zeros((3, 768, WIDE - GROUP), BF16)
    for i in range(3):
        weight[i, :, :GROUP] = given[:, GROUP * i : GROUP * (i + 1)]
    x_out[0:128] = mine[...]
    x_out[128:256] = r2[...]
    x_out[256:384] = r4[...]
    x_out[384:512] = r6[...]
    x_out[512:1024] = odd[...]
    tokens = x_out[...]
    lane = lax.broadcasted_iota(jnp.int32, (1024, WIDE), 1)
    is_even = lane % 2 == 0

    def part(i):
        return dot(tokens, weight[i]) + bias[i : i + 1, :]

    def turned(value):
        left = pltpu.roll(value, WIDE - 1, 1)
        right = pltpu.roll(value, 1, 1)
        return value * cosine[...] + jnp.where(is_even, left, right) * sine[...]

    query = turned(part(0)).astype(BF16).astype(F32) * (HEAD_DIM**-0.5)
    query = jnp.where(lane == GROUP, 1.0, query).T.astype(BF16)
    qt_out[...] = query
    key = jnp.where(lane == GROUP, padding[...], turned(part(1))).astype(BF16)
    k_out[...] = key
    value = part(2).astype(BF16)
    v_out[...] = value
    value_t = value.astype(F32).T
    ones = jnp.ones((16, 1024), BF16)
    row = lax.broadcasted_iota(jnp.int32, (WIDE, WIDE), 0)
    for h in range(HERE):
        here = (row // HEAD_DIM == h) | (row == GROUP)
        value_h = jnp.concatenate(
            [value_t[HEAD_DIM * h : HEAD_DIM * (h + 1)].astype(BF16), ones], axis=0
        )
        for b in range(4):
            block = qt_out[:, WIDE * b : WIDE * (b + 1)].astype(F32)
            scores = dot(key, jnp.where(here, block, 0.0).astype(BF16))
            top = jnp.max(scores, axis=0, keepdims=True)
            weights = jnp.exp(scores - top).astype(BF16)
            summed = dot(value_h, weights)
            total = summed[HEAD_DIM : HEAD_DIM + 1]
            att_out[HEAD_DIM * h : HEAD_DIM * (h + 1), WIDE * b : WIDE * (b + 1)] = (
                summed[:HEAD_DIM] / total
            )
            stats[h : h + 1, WIDE * b : WIDE * (b + 1)] = top
            stats[4 + h : 5 + h, WIDE * b : WIDE * (b + 1)] = total
    low = att_out[...].T.astype(BF16)
    for i in range(4):
        even_low[i] = low[128 * i : 128 * (i + 1)]
        odd_low[i] = low[512 + 128 * i : 640 + 128 * i]


def pair_body(info, own, came, p0, p1, p2, p3):
    for i, out in enumerate((p0, p1, p2, p3)):
        out[...] = jnp.concatenate(
            [own[i].astype(F32), came[i].astype(F32)], axis=1
        ).astype(BF16)


def proj_rows_body(info, d0, dx, dy, dd, out):
    for i, d in enumerate((d0, dx, dy, dd)):
        out[i] = d[384:480]


def attn_order(info):
    x, core = info[X], info[CORE]
    return ((x, core), (x, 1 - core), (1 - x, core), (1 - x, 1 - core))


def mix_body(
    info, p0, r2, r4, r6, d0, dx, dy, dd, proj_came, mine, other, vectors,
    normed_out, low_out, hat_out, rstd_out, rows_out, proj, held,
):
    core = info[CORE]
    for j, (yy, xx) in enumerate(chips(info)):
        held[rows((yy * 4 + xx * 2 + core) * 96, 96), :] = (d0, dx, dy, dd)[j][384:480]
        held[rows((yy * 4 + xx * 2 + 1 - core) * 96, 96), :] = proj_came[j]
    for i, (xx, cc) in enumerate(attn_order(info)):
        proj[GROUP * i : GROUP * (i + 1)] = held[rows((xx * 2 + cc) * GROUP, GROUP), :]
    rows_out[0:128, 0:384] = p0[...]
    rows_out[0:128, 384:768] = r2[...]
    rows_out[128:256, 0:384] = r4[...]
    rows_out[128:256, 384:768] = r6[...]
    tokens = jnp.concatenate([mine[...], other[...]], axis=0).astype(F32)
    resid = tokens + dot(rows_out[...], proj[...]) + vectors[0:1, :]
    centred = resid - jnp.mean(resid, axis=1, keepdims=True)
    rstd = lax.rsqrt(jnp.mean(centred * centred, axis=1, keepdims=True) + EPSILON)
    hat = centred * rstd
    normed = hat * vectors[1:2, :] + vectors[2:3, :]
    hat_out[...] = hat
    rstd_out[...] = jnp.broadcast_to(rstd, (256, 128))
    normed_out[...] = normed
    low_out[...] = normed.astype(BF16)


def whole_up(info, blocks, held):
    core = info[CORE]
    for block, (yy, xx) in zip(blocks, chips(info)):
        for half in range(2):
            span = slice(768 * half, 768 * (half + 1))
            for i, cc in enumerate((core, 1 - core)):
                held[rows((yy * 4 + xx * 2 + cc) * 96, 96), span] = block[
                    192 * half + 96 * i : 192 * half + 96 * (i + 1)
                ]


def whole_down(info, blocks, held):
    for block, (yy, xx) in zip(blocks, chips(info)):
        held[rows((yy * 2 + xx) * 384, 384), :] = block[...]


def gelu_parts(upward):
    gauss = jnp.exp(-0.5 * upward * upward)
    t = 1.0 / (1.0 + (0.3275911 * 2.0**-0.5) * jnp.abs(upward))
    poly = t * (
        0.127414796
        + t * (-0.142248368 + t * (0.7107068705 + t * (-0.7265760135 + t * 0.5307027145)))
    )
    tail = poly * gauss
    below = jnp.where(upward < 0, tail, 1.0 - tail)
    return upward * below, below + upward * gauss * 0.3989422804014327


def up_body(
    info, low_mine, low_other, u0, ux, uy, ud, d0, dx, dy, dd, bias,
    part_mine, part_other, active_out, slope_out, up_held, down_held,
):
    whole_up(info, (u0, ux, uy, ud), up_held)
    whole_down(info, (d0, dx, dy, dd), down_held)
    for i, low in enumerate((low_mine, low_other)):
        upward = dot(low[...], up_held[...]) + bias[...]
        active, slope = gelu_parts(upward)
        active = active.astype(BF16)
        active_out[256 * i : 256 * (i + 1)] = active
        slope_out[256 * i : 256 * (i + 1)] = slope.astype(BF16)
        part = dot(active, down_held[...])
        if i == 0:
            part_mine[...] = part
        else:
            part_other[...] = part.astype(BF16)


def back_norm(d_hat, hat, rstd):
    return rstd * (
        d_hat
        - jnp.mean(d_hat, axis=1, keepdims=True)
        - hat * jnp.mean(d_hat * hat, axis=1, keepdims=True)
    )


def column_sum(value):
    return jnp.sum(value, axis=0, keepdims=True)


def norm_two_body(
    info, part_mine, came, normed, vectors, grad, out, d_resid_out, d_low, sums,
):
    y = info[Y]
    resid = normed[...] + (part_mine[...] + came[...].astype(F32) + vectors[3:4, :])
    centred = resid - jnp.mean(resid, axis=1, keepdims=True)
    rstd = lax.rsqrt(jnp.mean(centred * centred, axis=1, keepdims=True) + EPSILON)
    hat = centred * rstd
    result = (hat * vectors[4:5, :] + vectors[5:6, :]).astype(BF16)
    out[y] = result[:128]
    out[1 - y] = result[128:]
    position = info[PLACE] * 128 + lax.broadcasted_iota(jnp.int32, (128, 768), 0)
    first = jnp.where(position < info[LEN_MINE], grad[y].astype(F32), 0.0)
    second = jnp.where(position < info[LEN_OTHER], grad[1 - y].astype(F32), 0.0)
    cotangent = jnp.concatenate([first, second], axis=0)
    d_resid = back_norm(cotangent * vectors[4:5, :], hat, rstd)
    d_resid_out[...] = d_resid
    low = d_resid.astype(BF16)
    d_low[...] = low
    sums[0:1] = column_sum(low.astype(F32))
    sums[1:2] = column_sum(cotangent * hat)
    sums[2:3] = column_sum(cotangent)


def down_grad_body(info, active, d_mine, d_other, g0, xa, xb, ya, yb, da, db, held):
    d_low = jnp.concatenate([d_mine[...], d_other[...]], axis=0)
    for i in range(4):
        held[384 * i : 384 * (i + 1)] = dot(
            active[:, 384 * i : 384 * (i + 1)], d_low, TN
        ).astype(BF16)
    outs = ((g0,), (xa, xb), (ya, yb), (da, db))
    for out, (yy, xx) in zip(outs, chips(info)):
        base = (yy * 2 + xx) * 384
        if len(out) == 1:
            out[0][...] = held[rows(base, 384), :]
        else:
            out[0][...] = held[rows(base, 192), :]
            out[1][...] = held[rows(base + 192, 192), :]


def add_two_body(info, a, a_came, b, b_came, a_out, b_out):
    a_out[...] = (a[...].astype(F32) + a_came[...].astype(F32)).astype(BF16)
    b_out[...] = (b[...].astype(F32) + b_came[...].astype(F32)).astype(BF16)


def add_half_body(info, x, x_came, y, y_came, x_out, y_out):
    half = x.shape[0] // 2
    x_out[:half] = x[:half]
    x_out[half:] = (x[half:].astype(F32) + x_came[...].astype(F32)).astype(BF16)
    y_out[:half] = (y[:half].astype(F32) + y_came[...].astype(F32)).astype(BF16)
    y_out[half:] = y[half:]


def up_grad_body(
    info, d_mine, d_other, slope, low_mine, low_other, u0, ux, uy, ud, d0, dx, dy, dd,
    part_mine, part_other, g0, gx, gy, gd, sums, up_held, down_held, held,
):
    core = info[CORE]
    whole_up(info, (u0, ux, uy, ud), up_held)
    whole_down(info, (d0, dx, dy, dd), down_held)
    d_ups = []
    total = jnp.zeros((1, 1536), F32)
    for i, d_low in enumerate((d_mine, d_other)):
        d_active = dot(d_low[...], down_held[...], NT)
        d_up = (slope[256 * i : 256 * (i + 1)].astype(F32) * d_active).astype(BF16)
        total = total + column_sum(d_up.astype(F32))
        d_ups.append(d_up)
        part = dot(d_up, up_held[...], NT)
        if i == 0:
            part_mine[...] = part
        else:
            part_other[...] = part.astype(BF16)
    sums[...] = total
    d_up = jnp.concatenate(d_ups, axis=0)
    low = jnp.concatenate([low_mine[...], low_other[...]], axis=0)
    held[...] = dot(low, d_up, TN).astype(BF16)
    for out, (yy, xx) in zip((g0, gx, gy, gd), chips(info)):
        for i, cc in enumerate((core, 1 - core)):
            block = held[rows((yy * 4 + xx * 2 + cc) * 96, 96), :]
            out[96 * i : 96 * (i + 1)] = block[:, :768]
            out[192 + 96 * i : 288 + 96 * i] = block[:, 768:]


def norm_one_body(
    info, d_resid_two, part_mine, came, hat, rstd, vectors, rows_here, proj,
    d_resid_out, e0, e2, e4, e6, proj_own, proj_sent, sums, held,
):
    core = info[CORE]
    d_normed = d_resid_two[...] + part_mine[...] + came[...].astype(F32)
    sums[0:1] = column_sum(d_normed * hat[...])
    sums[1:2] = column_sum(d_normed)
    d_resid = back_norm(d_normed * vectors[1:2, :], hat[...], rstd[:, 0:1])
    d_resid_out[...] = d_resid
    low = d_resid.astype(BF16)
    sums[2:3] = column_sum(low.astype(F32))
    d_att = dot(low, proj[...], NT).astype(BF16)
    e0[...] = d_att[:128, :384]
    e2[...] = d_att[:128, 384:]
    e4[...] = d_att[128:, :384]
    e6[...] = d_att[128:, 384:]
    d_weight = dot(rows_here[...], low, TN).astype(BF16)
    for i, (xx, cc) in enumerate(attn_order(info)):
        held[rows((xx * 2 + cc) * GROUP, GROUP), :] = d_weight[GROUP * i : GROUP * (i + 1)]
    for j, (yy, xx) in enumerate(chips(info)):
        proj_own[j] = held[rows((yy * 4 + xx * 2 + core) * 96, 96), :]
        proj_sent[j] = held[rows((yy * 4 + xx * 2 + 1 - core) * 96, 96), :]


def split_core_body(info, e0, e2, e4, e6, out):
    for i, e in enumerate((e0, e2, e4, e6)):
        out[128 * i : 128 * (i + 1)] = e[...].astype(F32)[:, GROUP:].astype(BF16)


def attend_back_body(
    info, e0, e2, e4, e6, came, qt, key, value, att, stats, cosine, sine,
    d_proj, sums, guide, weights_held, d_scores_held, dq_held, dk_held, dv_held,
):
    d_att = jnp.concatenate(
        [e[...].astype(F32)[:, :GROUP] for e in (e0, e2, e4, e6)] + [came[...].astype(F32)], axis=0
    )
    d_att_t = d_att.T
    product = d_att_t * att[...]
    pieces = []
    deltas = []
    for h in range(HERE):
        here = slice(HEAD_DIM * h, HEAD_DIM * (h + 1))
        total = stats[4 + h : 5 + h, :]
        pieces.append(d_att_t[here] / total)
        deltas.append(column_sum(product[here]) / total)
    pieces.append(jnp.zeros((WIDE - GROUP, 1024), F32))
    guide[...] = jnp.concatenate(pieces, axis=0).astype(BF16)
    key_t = key[...].astype(F32).T
    row = lax.broadcasted_iota(jnp.int32, (WIDE, WIDE), 0)
    dk_held[...] = jnp.zeros((1024, WIDE), F32)
    dv_held[...] = jnp.zeros((1024, WIDE), F32)
    dq_held[GROUP:] = jnp.zeros((WIDE - GROUP, 1024), F32)
    wide_row = lax.broadcasted_iota(jnp.int32, (WIDE, 1024), 0)
    for h in range(HERE):
        mine = row // HEAD_DIM == h
        with_pad = mine | (row == GROUP)
        key_h = key_t[HEAD_DIM * h : HEAD_DIM * (h + 1)].astype(BF16)
        for b in range(4):
            span = slice(WIDE * b, WIDE * (b + 1))
            q_block = jnp.where(with_pad, qt[:, span].astype(F32), 0.0).astype(BF16)
            g_block = jnp.where(mine, guide[:, span].astype(F32), 0.0).astype(BF16)
            scores = dot(key[...], q_block)
            weights = jnp.exp(scores - stats[h : h + 1, span])
            d_weights = dot(value[...], g_block)
            d_scores = (weights * (d_weights - deltas[h][:, span])).astype(BF16)
            weights_held[:, span] = weights.astype(BF16)
            d_scores_held[:, span] = d_scores
            dq_held[HEAD_DIM * h : HEAD_DIM * (h + 1), span] = dot(key_h, d_scores)
        here = wide_row // HEAD_DIM == h
        q_all = jnp.where(here, qt[...].astype(F32), 0.0).astype(BF16)
        g_all = jnp.where(here, guide[...].astype(F32), 0.0).astype(BF16)
        dk_held[...] += dot(d_scores_held[...], q_all, NT)
        dv_held[...] += dot(weights_held[...], g_all, NT)
    lane = lax.broadcasted_iota(jnp.int32, (1024, WIDE), 1)
    is_even = lane % 2 == 0

    def turned_back(value):
        left = pltpu.roll(value, WIDE - 1, 1)
        right = pltpu.roll(value, 1, 1)
        return value * cosine[...] - jnp.where(is_even, left, right) * sine[...]

    d_query = turned_back(dq_held[...].T * (HEAD_DIM**-0.5)).astype(BF16)
    d_key = turned_back(dk_held[...]).astype(BF16)
    d_value = dv_held[...].astype(BF16)
    for i, part in enumerate((d_query, d_key, d_value)):
        d_proj[i] = part
        sums[i : i + 1] = column_sum(part.astype(F32))


def attn_grad_body(info, tokens, d_proj, own, sent, held):
    core = info[CORE]
    parts = [dot(tokens[...], d_proj[i], TN)[:, :GROUP] for i in range(3)]
    held[...] = jnp.concatenate(parts, axis=1).astype(BF16)
    for j, (yy, xx) in enumerate(chips(info)):
        own[j] = held[rows((yy * 4 + xx * 2 + core) * 96, 96), :]
        sent[j] = held[rows((yy * 4 + xx * 2 + 1 - core) * 96, 96), :]


def attn_pair_body(info, own, came, s0, s2, s4, s6):
    for j, out in enumerate((s0, s2, s4, s6)):
        out[0] = own[j]
        out[1] = came[j]


def attn_blocks_body(info, own, r2, r4, r6, first, s1, s2, s3, held):
    core, x, z = info[CORE], info[X], info[Z]
    mine = own[...].astype(F32) + r4[...].astype(F32)
    other = r2[...].astype(F32) + r6[...].astype(F32)
    for i, cc in enumerate((core, 1 - core)):
        held[2 * x + cc] = mine[i]
        held[2 * (1 - x) + cc] = other[i]
    for k, out in enumerate((first, s1, s2, s3)):
        here = rows((z ^ k) * 24, 24, 8)
        blocks = [held[g, here, :] for g in range(4)]
        for i in range(3):
            part = jnp.concatenate([b[:, GROUP * i : GROUP * (i + 1)] for b in blocks], axis=1)
            out[:, 768 * i : 768 * (i + 1)] = part.astype(out.dtype)


def sum_four_body(info, first, r1, r2, r3, out):
    out[...] = (
        first[...] + r1[...].astype(F32) + r2[...].astype(F32) + r3[...].astype(F32)
    )


def hidden_grad_body(info, d_proj, weight, even_out, odd_out):
    total = jnp.zeros((1024, 768), F32)
    for i in range(3):
        total = total + dot(d_proj[i], weight[i], NT)
    even_out[...] = total[:512]
    odd_out[...] = total[512:].astype(BF16)


def hidden_pair_body(info, even, came, own, s2, s4, s6):
    total = even[...] + came[...].astype(F32)
    own[...] = total[:128]
    s2[...] = total[128:256].astype(BF16)
    s4[...] = total[256:384].astype(BF16)
    s6[...] = total[384:].astype(BF16)


def hidden_end_body(info, d_resid, own, r2, r4, r6, out):
    y = info[Y]
    out[y] = d_resid[:128] + own[...] + r2[...].astype(F32)
    out[1 - y] = d_resid[128:] + r4[...].astype(F32) + r6[...].astype(F32)


def down_blocks_body(info, own, xa, xb, ya, yb, first, s1, s2, s3, held):
    z = info[Z]
    held[:192] = own[:192].astype(F32) + xa[...].astype(F32) + ya[...].astype(F32)
    held[192:] = own[192:].astype(F32) + xb[...].astype(F32) + yb[...].astype(F32)
    first[...] = held[rows(z * 96, 96), :]
    for k, out in ((1, s1), (2, s2), (3, s3)):
        out[...] = held[rows((z ^ k) * 96, 96), :].astype(BF16)


def up_blocks_body(info, own, a, b, first, s1, s2, s3, held):
    z = info[Z]
    held[...] = own[...].astype(F32) + a[...].astype(F32) + b[...].astype(F32)
    for k, out in enumerate((first, s1, s2, s3)):
        block = [held[rows(96 * i + (z ^ k) * 24, 24, 8), :] for i in range(5)]
        out[...] = jnp.concatenate(block, axis=0).astype(out.dtype)


def up_sum_body(info, first, r1, r2, r3, own, sent, proj_out):
    total = first[...] + r1[...].astype(F32) + r2[...].astype(F32) + r3[...].astype(F32)
    own[...] = jnp.concatenate([total[:24], total[48:72]], axis=1)
    sent[...] = jnp.concatenate([total[24:48], total[72:96]], axis=1).astype(BF16)
    proj_out[...] = total[96:]


def up_end_body(info, own, came, up_out):
    core = info[CORE]
    for which, source in ((core, own), (1 - core, came)):
        for q in range(4):
            up_out[:, lanes(768 * q + 384 * which, 384)] = source[
                :, 384 * q : 384 * (q + 1)
            ].astype(F32)


def join_body(info, g0, gx, gy, gd, p_own, p_came, o0, ox, oy, da, db):
    proj = [(p_own[j].astype(F32) + p_came[j].astype(F32)).astype(BF16) for j in range(4)]
    for j, (g, out) in enumerate(((g0, o0), (gx, ox), (gy, oy))):
        out[:384] = g[...]
        out[384:] = proj[j]
    da[...] = gd[:240]
    db[:144] = gd[240:]
    db[144:] = proj[3]


def split_layer(
    hidden_in,
    lengths,
    attn_weight,
    attn_bias,
    proj_weight,
    proj_bias,
    first_gain,
    first_shift,
    up_weight,
    up_bias,
    down_weight,
    down_bias,
    second_gain,
    second_shift,
    grad_out,
):
    both_axes = ("seq", "batch")
    place = lax.axis_index("seq")
    z = lax.axis_index("batch")
    core, x, y = place & 1, (place >> 1) & 1, place >> 2
    group = place & 3
    len_mine = jnp.where(y == 0, lengths[0], lengths[1])
    len_other = jnp.where(y == 0, lengths[1], lengths[0])
    info = jnp.stack([core, x, y, z, place, len_mine, len_other, group]).astype(jnp.int32)

    attn_far = [swap_batch(attn_weight, k) for k in (1, 2, 3)]
    small_vectors = (
        attn_bias, proj_bias, first_gain, first_shift, down_bias, second_gain, second_shift, up_bias
    )
    mine, other, up_proj, small_sent = call(
        select_body,
        [shape((128, 768)), shape((128, 768)), shape((24, 3840)), shape((32, 384), F32)],
        info, hidden_in, up_weight, proj_weight, *[v[None] for v in small_vectors], name="select",
        alone=True,
    )
    r2, r4, r6 = swap_seq(mine, 2), swap_seq(other, 4), swap_seq(other, 6)
    up_far = [swap_batch(up_proj, k) for k in (1, 2, 3)]
    small_all = lax.all_to_all(small_sent[:, None], both_axes, 0, 0, tiled=True)[:, 0]
    attn_far, r2, r4, r6, small_all, mine = fence(attn_far, r2, r4, r6, small_all, mine)

    (w_sent,) = call(
        attn_column_body, [shape((8, 96, 576))], info, attn_weight, *attn_far, name="attn_column"
    )
    weight_given = lax.all_to_all(w_sent, "seq", 0, 0, tiled=True).reshape(768, 576)
    odd = swap_seq(jnp.concatenate([mine, r2, r4, r6], axis=0), 1)
    owners = place ^ jnp.array(EVEN + ODD, jnp.int32)
    positions = (owners[:, None] * 128 + jnp.arange(128, dtype=jnp.int32)[None, :]).reshape(-1)
    entry = jnp.arange(WIDE)
    frequency = 10000.0 ** (-2.0 * ((entry % HEAD_DIM) // 2).astype(F32) / HEAD_DIM)
    angles = positions.astype(F32)[:, None] * frequency[None, :]
    used = (entry < GROUP).astype(F32)
    cosine = jnp.cos(angles) * used
    sine = jnp.sin(angles) * (used * jnp.where(entry % 2 == 0, -1.0, 1.0))
    padding = jnp.broadcast_to(
        jnp.where(positions < len_mine, 0.0, NEG_BIG)[:, None], (1024, WIDE)
    )
    up_far, odd, cosine, sine, padding, small_all = fence(
        up_far, odd, cosine, sine, padding, small_all
    )

    up_keep, up_sent, proj_column = call(
        up_column_body, [shape((192, 768)), shape((192, 768)), shape((96, 768))],
        info, up_proj, *up_far, scratch=[shape((96, 3840))], name="up_column",
    )
    (up_column,) = call(
        up_join_body, [shape((480, 768))], info, up_keep, swap_seq(up_sent, 1), proj_column,
        name="up_join",
    )
    attn_bias_all = small_all[:, :72].reshape(3, 4, GROUP)
    bias_here = lax.dynamic_index_in_dim(attn_bias_all, group, 1, keepdims=False)
    bias_here = jnp.pad(bias_here, ((0, 0), (0, WIDE - GROUP)))
    vectors = small_all[:, 72:216].reshape(32, 6, 24).transpose(1, 0, 2).reshape(6, 768)
    up_bias_all = small_all[:, 216:312].reshape(4, 2, 384)
    up_bias_here = lax.dynamic_index_in_dim(up_bias_all, core, 1, keepdims=False).reshape(1, 1536)
    weight_given, up_column, bias_here, vectors, up_bias_here, mine, down_weight = fence(
        weight_given, up_column, bias_here, vectors, up_bias_here, mine, down_weight
    )

    up_x, up_y = swap_seq(up_column, 2), swap_seq(up_column, 4)
    down_far = [swap_batch(down_weight, k) for k in (1, 2, 3)]
    tokens_here, weight_here, query_t, key, value, attended, stats, even_low, odd_low = call(
        attend_body,
        [
            shape((1024, 768)), shape((3, 768, WIDE)),
            shape((WIDE, 1024)), shape((1024, WIDE)), shape((1024, WIDE)),
            shape((GROUP, 1024), F32), shape((8, 1024), F32),
            shape((4, 128, GROUP)), shape((4, 128, GROUP)),
        ],
        info, mine, r2, r4, r6, odd, weight_given, bias_here, cosine, sine, padding,
        flops=8_000_000_000, name="attend", alone=True,
    )
    down_far, even_low, odd_low = fence(down_far, even_low, odd_low)

    (down_column,) = call(
        down_column_body, [shape((384, 768))], info, down_weight, *down_far, name="down_column"
    )
    p0, p1, p2, p3 = call(
        pair_body, [shape((128, 384))] * 4, info, even_low, swap_seq(odd_low, 1), name="pair"
    )
    p0, p1, p2, p3, down_column, up_x, up_y = fence(p0, p1, p2, p3, down_column, up_x, up_y)

    a2, a4, a6 = swap_seq(p1, 2), swap_seq(p2, 4), swap_seq(p3, 6)
    up_da, up_db = swap_seq(up_y[:240], 2), swap_seq(up_x[240:], 4)
    a2, a4, a6, up_da, up_db, down_column = fence(a2, a4, a6, up_da, up_db, down_column)

    down_x, down_y = swap_seq(down_column, 2), swap_seq(down_column, 4)
    up_blocks = (up_column, up_x, up_y, jnp.concatenate([up_da, up_db], axis=0))
    (proj_rows,) = call(proj_rows_body, [shape((4, 96, 768))], info, *up_blocks, name="proj_rows")
    proj_came = swap_seq(proj_rows, 1)
    normed, low_mine, hat_one, rstd_one, rows_here, proj_here = call(
        mix_body,
        [
            shape((256, 768), F32), shape((256, 768)), shape((256, 768), F32),
            shape((256, 128), F32), shape((256, 768)), shape((768, 768)),
        ],
        info, p0, a2, a4, a6, *up_blocks, proj_came, mine, other, vectors,
        scratch=[shape((768, 768))], flops=300_000_000, name="mix",
    )
    low_other = swap_seq(low_mine, 1)
    down_x, down_y, low_other = fence(down_x, down_y, low_other)
    down_da, down_db = swap_seq(down_y[:192], 2), swap_seq(down_x[192:], 4)
    down_blocks = (down_column, down_x, down_y, jnp.concatenate([down_da, down_db], axis=0))

    part_mine, part_other, active, slope = call(
        up_body,
        [shape((256, 768), F32), shape((256, 768)), shape((512, 1536)), shape((512, 1536))],
        info, low_mine, low_other, *up_blocks, *down_blocks, up_bias_here,
        scratch=[shape((768, 1536)), shape((1536, 768))], flops=2_400_000_000, name="up",
    )
    layer_out, d_resid_two, d_low, sums_two = call(
        norm_two_body,
        [shape((2, 128, 768)), shape((256, 768), F32), shape((256, 768)), shape((8, 768), F32)],
        info, part_mine, swap_seq(part_other, 1), normed, vectors, grad_out, name="norm_two",
    )
    d_came = swap_seq(d_low, 1)
    g_down, gxa, gxb, gya, gyb, gda, gdb = call(
        down_grad_body, [shape((384, 768))] + [shape((192, 768))] * 6, info, active, d_low, d_came,
        scratch=[shape((1536, 768))], flops=1_200_000_000, name="down_grad",
    )
    gxa, gxb, gya, gyb, gda, gdb, d_low, d_came = fence(gxa, gxb, gya, gyb, gda, gdb, d_low, d_came)

    gda, gdb = swap_seq(gda, 2), swap_seq(gdb, 4)
    part_mine, part_other, g0, gx, gy, gd, up_sums = call(
        up_grad_body,
        [shape((256, 768), F32), shape((256, 768))] + [shape((384, 768))] * 4
        + [shape((1, 1536), F32)],
        info, d_low, d_came, slope, low_mine, low_other, *up_blocks, *down_blocks,
        scratch=[shape((768, 1536)), shape((1536, 768)), shape((768, 1536))],
        flops=3_600_000_000, name="up_grad",
    )
    gda, gdb, part_mine, part_other, gxa, gyb = fence(gda, gdb, part_mine, part_other, gxa, gyb)
    gxa, gyb = swap_seq(gxa, 2), swap_seq(gyb, 4)
    d_resid_one, e0, e2, e4, e6, proj_own, proj_sent, sums_one = call(
        norm_one_body,
        [shape((256, 768), F32)] + [shape((128, 384))] * 4 + [shape((4, 96, 768))] * 2
        + [shape((8, 768), F32)],
        info, d_resid_two, part_mine, swap_seq(part_other, 1), hat_one, rstd_one, vectors,
        rows_here, proj_here,
        scratch=[shape((768, 768))], flops=600_000_000, name="norm_one",
    )
    gxa, gyb, e0, e2, e4, e6, proj_sent = fence(gxa, gyb, e0, e2, e4, e6, proj_sent)

    e2, e4, e6 = swap_seq(e2, 2), swap_seq(e4, 4), swap_seq(e6, 6)
    proj_came = swap_seq(proj_sent, 1)
    gxb, gya = call(
        add_two_body, [shape((192, 768))] * 2, info, gxb, gdb, gya, gda, name="down_add"
    )
    j0, jx, jy, jda, jdb = call(
        join_body, [shape((480, 768))] * 3 + [shape((240, 768))] * 2,
        info, g0, gx, gy, gd, proj_own, proj_came, name="join",
    )
    (split,) = call(split_core_body, [shape((512, GROUP))], info, e0, e2, e4, e6, name="split")
    e_came = swap_seq(split, 1)
    e2, e4, e6, e_came, gxb, gya, jda, jdb = fence(e2, e4, e6, e_came, gxb, gya, jda, jdb)

    jda, jdb = swap_seq(jda, 2), swap_seq(jdb, 4)
    gxb, gya = swap_seq(gxb, 2), swap_seq(gya, 4)
    d_proj, sums_attn = call(
        attend_back_body,
        [shape((3, 1024, WIDE)), shape((8, WIDE), F32)],
        info, e0, e2, e4, e6, e_came, query_t, key, value, attended, stats, cosine, sine,
        scratch=[
            shape((WIDE, 1024)), shape((1024, 1024)), shape((1024, 1024)),
            shape((WIDE, 1024), F32), shape((1024, WIDE), F32), shape((1024, WIDE), F32),
        ],
        flops=8_000_000_000, name="attend_back",
    )
    wg_own, wg_sent = call(
        attn_grad_body, [shape((4, 96, 576))] * 2, info, tokens_here, d_proj,
        scratch=[shape((768, 576))], flops=1_200_000_000, name="attn_grad",
    )
    even, odd_sent = call(
        hidden_grad_body, [shape((512, 768), F32), shape((512, 768))], info, d_proj, weight_here,
        flops=1_200_000_000, name="hidden_grad",
    )
    jda, jdb, gxb, gya, wg_sent, odd_sent = fence(jda, jdb, gxb, gya, wg_sent, odd_sent)

    wg_came, odd_came = swap_seq(wg_sent, 1), swap_seq(odd_sent, 1)
    jx, jy = call(add_half_body, [shape((480, 768))] * 2, info, jx, jdb, jy, jda, name="up_add")
    first, b1, b2, b3 = call(
        down_blocks_body, [shape((96, 768), F32)] + [shape((96, 768))] * 3,
        info, g_down, gxa, gxb, gya, gyb, scratch=[shape((384, 768), F32)], name="down_blocks",
    )
    wg_came, odd_came, jx, jy, b1, b2, b3 = fence(wg_came, odd_came, jx, jy, b1, b2, b3)

    jx, jy = swap_seq(jx, 2), swap_seq(jy, 4)
    b1, b2, b3 = [swap_batch(b, k) for k, b in ((1, b1), (2, b2), (3, b3))]
    h0, h2, h4, h6 = call(
        attn_pair_body, [shape((2, 96, 576))] * 4, info, wg_own, wg_came, name="attn_pair",
    )
    own, s2, s4, s6 = call(
        hidden_pair_body, [shape((128, 768), F32)] + [shape((128, 768))] * 3,
        info, even, odd_came, name="hidden_pair",
    )
    is_group = (jnp.arange(4) == group)[None, :, None]
    d_attn_bias = jnp.where(is_group, sums_attn[:3, None, :GROUP], 0.0).reshape(-1)
    is_core = (jnp.arange(2) == core)[None, :, None]
    d_up_bias = jnp.where(is_core, up_sums.reshape(4, 1, 384), 0.0).reshape(32, 96)
    d_six = jnp.stack(
        [sums_one[2], sums_one[0], sums_one[1], sums_two[0], sums_two[1], sums_two[2]]
    )
    d_small = jnp.concatenate(
        [
            d_attn_bias[:1536].reshape(32, 48),
            d_attn_bias[1536:].reshape(32, 24),
            d_six.reshape(6, 32, 24).transpose(1, 0, 2).reshape(32, 144),
            d_up_bias,
        ],
        axis=-1,
    )
    d_small = lax.all_to_all(d_small[:, None], both_axes, 0, 0, tiled=True)
    jx, jy, h2, h4, h6, s2, s4, s6, b1, b2, b3, d_small = fence(
        jx, jy, h2, h4, h6, s2, s4, s6, b1, b2, b3, d_small
    )

    up_first, c1, c2, c3 = call(
        up_blocks_body, [shape((120, 768), F32)] + [shape((120, 768))] * 3,
        info, j0, jx, jy, scratch=[shape((480, 768), F32)], name="up_blocks",
    )
    c1, c2, c3 = [swap_batch(c, k) for k, c in ((1, c1), (2, c2), (3, c3))]
    h2, h4, h6 = swap_seq(h2, 2), swap_seq(h4, 4), swap_seq(h6, 6)
    h2, h4, h6, c1, s2, s4, s6 = fence(h2, h4, h6, c1, s2, s4, s6)

    s2, s4 = swap_seq(s2, 2), swap_seq(s4, 4)
    attn_first, *attn_sends = call(
        attn_blocks_body, [shape((24, 2304), F32)] + [shape((24, 2304))] * 3,
        info, h0, h2, h4, h6, scratch=[shape((4, 96, 576), F32)], name="attn_blocks",
    )
    c2, c3, s2, s4, s6, attn_sends = fence(c2, c3, s2, s4, s6, attn_sends)

    attn_came = [swap_batch(part, k) for k, part in zip((1, 2, 3), attn_sends)]
    s6 = swap_seq(s6, 6)
    up_own, up_sent, grad_proj_weight = call(
        up_sum_body, [shape((24, 1536), F32), shape((24, 1536)), shape((24, 768), F32)],
        info, up_first, c1, c2, c3, name="up_sum",
    )
    (grad_up_weight,) = call(
        up_end_body, [shape((24, 3072), F32)], info, up_own, swap_seq(up_sent, 1), name="up_end"
    )
    (grad_down_weight,) = call(
        sum_four_body, [shape((96, 768), F32)], info, first, b1, b2, b3, name="down_end"
    )
    (grad_attn_weight,) = call(
        sum_four_body, [shape((24, 2304), F32)], info, attn_first, *attn_came, name="attn_end"
    )
    (grad_hidden,) = call(
        hidden_end_body, [shape((2, 128, 768), F32)], info, d_resid_one, own, s2, s4, s6,
        name="hidden_end",
    )

    d_small = jnp.sum(d_small[:, 0], axis=0)
    d_vectors = [d_small[72 + 24 * i : 96 + 24 * i] for i in range(6)]
    return (
        layer_out,
        grad_hidden,
        grad_attn_weight,
        d_small[:48],
        d_small[48:72],
        grad_proj_weight,
        d_vectors[0],
        d_vectors[1],
        d_vectors[2],
        grad_up_weight,
        d_small[216:],
        grad_down_weight,
        d_vectors[3],
        d_vectors[4],
        d_vectors[5],
    )


def solution(mesh):
    in_specs = (
        P("batch", "seq", None),
        P("batch"),
        P(("seq", "batch"), None),
        P(("seq", "batch")),
        P(("seq", "batch"), None),
        P(("seq", "batch")),
        P(("seq", "batch")),
        P(("seq", "batch")),
        P(("seq", "batch"), None),
        P(("seq", "batch")),
        P(("seq", "batch"), None),
        P(("seq", "batch")),
        P(("seq", "batch")),
        P(("seq", "batch")),
        P("batch", "seq", None),
    )
    out_specs = (
        P("batch", "seq", None),
        P("batch", "seq", None),
        P(("seq", "batch"), None),
        P(("seq", "batch")),
        P(("seq", "batch")),
        P(("seq", "batch"), None),
        P(("seq", "batch")),
        P(("seq", "batch")),
        P(("seq", "batch")),
        P(("seq", "batch"), None),
        P(("seq", "batch")),
        P(("seq", "batch"), None),
        P(("seq", "batch")),
        P(("seq", "batch")),
        P(("seq", "batch")),
    )
    fits = mesh.shape["seq"] == SEQ_SIDE and mesh.shape["batch"] == BATCH_SIDE
    return jax.shard_map(
        split_layer if fits else on_device, mesh=mesh, in_specs=in_specs, out_specs=out_specs, check_vma=False
    )
```

```python
import math

import jax
import jax.numpy as jnp
from jax import lax
from jax.experimental import pallas as pl
from jax.experimental.pallas import tpu as pltpu
from jax.sharding import PartitionSpec as P

HEADS = 12
HEAD_DIM = 64


EPSILON = 1e-12
NEG_BIG = -1e30


def passed_along(value, axis, steps):
    count = lax.axis_size(axis)
    pairs = [(source, (source + steps) % count) for source in range(count)]
    return lax.ppermute(value, axis, pairs)


def rotate(vectors, positions):
    half_dim = vectors.shape[-1] // 2
    frequency = 10000.0 ** (-2.0 * jnp.arange(half_dim, dtype=jnp.float32) / vectors.shape[-1])
    angles = positions[:, None] * frequency[None, :]
    cosine = jnp.cos(angles)[:, None, :]
    sine_part = jnp.sin(angles)[:, None, :]
    split_pairs = vectors.reshape(vectors.shape[:-1] + (half_dim, 2))
    even_part = split_pairs[..., 0]
    odd_part = split_pairs[..., 1]
    turned = jnp.stack(
        [even_part * cosine - odd_part * sine_part, odd_part * cosine + even_part * sine_part],
        axis=-1,
    )
    return turned.reshape(vectors.shape)


def layer_norm(residual, scale_gain, shift_bias):
    row_mean = jnp.mean(residual, axis=-1, keepdims=True)
    centered = residual - row_mean
    variance = jnp.mean(centered * centered, axis=-1, keepdims=True)
    return centered * lax.rsqrt(variance + EPSILON) * scale_gain + shift_bias


def gelu_exact(upward):
    return jax.nn.gelu(upward, approximate=False)


def run_blocks(step_fn, carry_now, key_piece, first_row, block_keys):
    row_count = key_piece.shape[1]
    width_now = block_keys if row_count % block_keys == 0 else row_count

    def one_turn(index, carry_in):
        begin_at = index * width_now
        sub_piece = lax.dynamic_slice_in_dim(key_piece, begin_at, width_now, 1)
        return step_fn(carry_in, sub_piece, first_row + begin_at)

    return lax.fori_loop(0, row_count // width_now, one_turn, carry_now)


def on_device(
    hidden_in,
    lengths,
    attn_weight,
    attn_bias,
    proj_weight,
    proj_bias,
    first_gain,
    first_shift,
    up_weight,
    up_bias,
    down_weight,
    down_bias,
    second_gain,
    second_shift,
    grad_out,
):
    seq_count, span_rows, model_width = hidden_in.shape
    token_count = seq_count * span_rows
    seq_devices = lax.axis_size("seq")
    my_index = lax.axis_index("seq")
    block_keys = max(span_rows, 512)
    score_scale = HEAD_DIM ** (-0.5)
    offset = my_index * span_rows
    row_index = offset + jnp.arange(span_rows, dtype=jnp.int32)
    positions = row_index.astype(jnp.float32)
    attn_full, attn_bias_full, proj_full, proj_bias_full, gain_one, shift_one = (
        lax.all_gather(attn_weight, ("seq", "batch"), axis=0, tiled=True),
        lax.all_gather(attn_bias, ("seq", "batch"), axis=0, tiled=True),
        lax.all_gather(proj_weight, ("seq", "batch"), axis=0, tiled=True),
        lax.all_gather(proj_bias, ("seq", "batch"), axis=0, tiled=True),
        lax.all_gather(first_gain, ("seq", "batch"), axis=0, tiled=True),
        lax.all_gather(first_shift, ("seq", "batch"), axis=0, tiled=True),
    )
    up_full, up_bias_full, down_full, down_bias_full, gain_two, shift_two = (
        lax.all_gather(up_weight, ("seq", "batch"), axis=0, tiled=True),
        lax.all_gather(up_bias, ("seq", "batch"), axis=0, tiled=True),
        lax.all_gather(down_weight, ("seq", "batch"), axis=0, tiled=True),
        lax.all_gather(down_bias, ("seq", "batch"), axis=0, tiled=True),
        lax.all_gather(second_gain, ("seq", "batch"), axis=0, tiled=True),
        lax.all_gather(second_shift, ("seq", "batch"), axis=0, tiled=True),
    )
    tokens_flat = hidden_in.reshape(token_count, model_width)
    projected = jnp.dot(
        tokens_flat, attn_full, preferred_element_type=jnp.float32
    ) + attn_bias_full.astype(jnp.float32)
    projected = projected.reshape(seq_count, span_rows, 3, HEADS, HEAD_DIM)
    queries = rotate(projected[:, :, 0], positions).astype(jnp.bfloat16)
    keys_low = rotate(projected[:, :, 1], positions).astype(jnp.bfloat16)
    values_low = projected[:, :, 2].astype(jnp.bfloat16)
    key_values = jnp.concatenate(
        [
            keys_low.reshape(seq_count, span_rows, model_width),
            values_low.reshape(seq_count, span_rows, model_width),
        ],
        axis=-1,
    )

    def key_mask(first_row, row_count):
        key_rows = first_row + jnp.arange(row_count, dtype=jnp.int32)
        return (key_rows[None, :] < lengths[:, None])[:, None, None, :]

    def split_pairs(key_piece):
        row_count = key_piece.shape[1]
        keys_part = key_piece[:, :, :model_width].reshape(seq_count, row_count, HEADS, HEAD_DIM)
        values_part = key_piece[:, :, model_width:].reshape(seq_count, row_count, HEADS, HEAD_DIM)
        return (keys_part, values_part)

    def attend_step(carry_in, key_piece, first_row):
        row_max, row_sum, accum = carry_in
        keys_part, values_part = split_pairs(key_piece)
        masked = key_mask(first_row, key_piece.shape[1])
        scores = score_scale * jnp.einsum(
            "sqhd,skhd->shqk", queries, keys_part, preferred_element_type=jnp.float32
        )
        scores = jnp.where(masked, scores, NEG_BIG)
        new_max = jnp.maximum(row_max, jnp.max(scores, axis=-1))
        weights = jnp.where(masked, jnp.exp(scores - new_max[..., None]), 0.0)
        factor = jnp.exp(row_max - new_max)
        row_sum = row_sum * factor + jnp.sum(weights, axis=-1)
        accum = accum * jnp.transpose(factor, (0, 2, 1))[..., None] + jnp.einsum(
            "shqk,skhd->sqhd",
            weights.astype(jnp.bfloat16),
            values_part,
            preferred_element_type=jnp.float32,
        )
        return (new_max, row_sum, accum)

    start_state = (
        jnp.full((seq_count, HEADS, span_rows), NEG_BIG, jnp.float32),
        jnp.zeros((seq_count, HEADS, span_rows), jnp.float32),
        jnp.zeros((seq_count, span_rows, HEADS, HEAD_DIM), jnp.float32),
    )
    row_max, row_sum, accum = run_blocks(
        attend_step,
        start_state,
        lax.all_gather(key_values, "seq", axis=1, tiled=True),
        jnp.int32(0),
        block_keys,
    )
    sum_view = jnp.transpose(row_sum, (0, 2, 1))[..., None]
    attended = accum / sum_view
    attn_rows = attended.reshape(token_count, model_width).astype(jnp.bfloat16)
    mixed = jnp.dot(
        attn_rows, proj_full, preferred_element_type=jnp.float32
    ) + proj_bias_full.astype(jnp.float32)
    normed, norm_back_one = jax.vjp(
        layer_norm,
        tokens_flat.astype(jnp.float32) + mixed,
        gain_one.astype(jnp.float32),
        shift_one.astype(jnp.float32),
    )
    normed_low = normed.astype(jnp.bfloat16)
    upward = jnp.dot(normed_low, up_full, preferred_element_type=jnp.float32) + up_bias_full.astype(
        jnp.float32
    )
    active, gelu_back = jax.vjp(gelu_exact, upward)
    active_low = active.astype(jnp.bfloat16)
    downward = jnp.dot(
        active_low, down_full, preferred_element_type=jnp.float32
    ) + down_bias_full.astype(jnp.float32)
    output_rows, norm_back_two = jax.vjp(
        layer_norm, normed + downward, gain_two.astype(jnp.float32), shift_two.astype(jnp.float32)
    )
    layer_out = output_rows.reshape(seq_count, span_rows, model_width).astype(jnp.bfloat16)
    row_valid = (row_index[None, :] < lengths[:, None]).astype(jnp.float32)
    cotangent = (grad_out.astype(jnp.float32) * row_valid[:, :, None]).reshape(
        token_count, model_width
    )
    d_resid_two, d_gain_two, d_shift_two = norm_back_two(cotangent)
    d_down = d_resid_two.astype(jnp.bfloat16)
    d_down_bias = jnp.sum(d_down.astype(jnp.float32), axis=0)
    d_down_weight = jnp.einsum("tf,td->fd", active_low, d_down, preferred_element_type=jnp.float32)
    d_active = jnp.dot(d_down, down_full.T, preferred_element_type=jnp.float32)
    (d_upward,) = gelu_back(d_active)
    d_up = d_upward.astype(jnp.bfloat16)
    d_up_bias = jnp.sum(d_up.astype(jnp.float32), axis=0)
    d_up_weight = jnp.einsum("td,tf->df", normed_low, d_up, preferred_element_type=jnp.float32)
    d_normed = d_resid_two + jnp.dot(d_up, up_full.T, preferred_element_type=jnp.float32)
    ffn_parts = (
        lax.psum_scatter(d_up_weight, ("seq", "batch"), scatter_dimension=0, tiled=True),
        lax.psum_scatter(d_up_bias, ("seq", "batch"), scatter_dimension=0, tiled=True),
        lax.psum_scatter(d_down_weight, ("seq", "batch"), scatter_dimension=0, tiled=True),
        lax.psum_scatter(d_down_bias, ("seq", "batch"), scatter_dimension=0, tiled=True),
        lax.psum_scatter(d_gain_two, ("seq", "batch"), scatter_dimension=0, tiled=True),
        lax.psum_scatter(d_shift_two, ("seq", "batch"), scatter_dimension=0, tiled=True),
    )
    d_resid_one, d_gain_one, d_shift_one = norm_back_one(d_normed)
    d_mixed = d_resid_one.astype(jnp.bfloat16)
    d_proj_bias = jnp.sum(d_mixed.astype(jnp.float32), axis=0)
    d_proj_weight = jnp.einsum("td,te->de", attn_rows, d_mixed, preferred_element_type=jnp.float32)
    d_attended = jnp.dot(d_mixed, proj_full.T, preferred_element_type=jnp.float32).astype(
        jnp.bfloat16
    )
    d_attended = d_attended.astype(jnp.float32).reshape(seq_count, span_rows, HEADS, HEAD_DIM)
    delta = jnp.transpose(jnp.sum(d_attended * attended, axis=-1), (0, 2, 1))
    delta_scaled = delta / row_sum
    guide = (d_attended / sum_view).astype(jnp.bfloat16)

    def back_step(carry_in, key_piece, first_row):
        d_queries, buffer = carry_in
        keys_part, values_part = split_pairs(key_piece)
        row_count = key_piece.shape[1]
        masked = key_mask(first_row, row_count)
        scores = score_scale * jnp.einsum(
            "sqhd,skhd->shqk", queries, keys_part, preferred_element_type=jnp.float32
        )
        scores = jnp.where(masked, scores, NEG_BIG)
        weights = jnp.where(masked, jnp.exp(scores - row_max[..., None]), 0.0)
        d_weights = jnp.einsum(
            "sqhd,skhd->shqk", guide, values_part, preferred_element_type=jnp.float32
        )
        d_scores = (weights * (d_weights - delta_scaled[..., None])).astype(jnp.bfloat16)
        d_queries = d_queries + score_scale * jnp.einsum(
            "shqk,skhd->sqhd", d_scores, keys_part, preferred_element_type=jnp.float32
        )
        d_keys = score_scale * jnp.einsum(
            "shqk,sqhd->skhd", d_scores, queries, preferred_element_type=jnp.float32
        )
        d_values = jnp.einsum(
            "shqk,sqhd->skhd",
            weights.astype(jnp.bfloat16),
            guide,
            preferred_element_type=jnp.float32,
        )
        new_terms = jnp.concatenate(
            [
                d_keys.reshape(seq_count, row_count, model_width),
                d_values.reshape(seq_count, row_count, model_width),
            ],
            axis=-1,
        )
        current = buffer
        buffer = current + new_terms
        return (d_queries, buffer)

    zero_queries = jnp.zeros((seq_count, span_rows, HEADS, HEAD_DIM), jnp.float32)

    def cycle_turn(turn, carry_in):
        d_queries, pair_piece, grad_piece = carry_in
        owner = (my_index - turn) % seq_devices
        base_row = owner * span_rows

        def owner_step(inner, key_piece, first_row):
            return back_step(inner, key_piece, first_row)

        d_queries, grad_piece = run_blocks(
            owner_step, (d_queries, grad_piece), pair_piece, base_row, block_keys
        )
        grad_piece = passed_along(grad_piece.astype(jnp.bfloat16), "seq", 1).astype(
            grad_piece.dtype
        )
        pair_piece = passed_along(pair_piece, "seq", 1)
        return (d_queries, pair_piece, grad_piece)

    start_cycle = (
        zero_queries,
        key_values,
        jnp.zeros((seq_count, span_rows, 2 * model_width), jnp.float32),
    )
    d_queries, pair_spent, d_pairs = lax.fori_loop(0, seq_devices, cycle_turn, start_cycle)
    d_keys_own = d_pairs[:, :, :model_width].reshape(seq_count, span_rows, HEADS, HEAD_DIM)
    d_values_own = d_pairs[:, :, model_width:].reshape(seq_count, span_rows, HEADS, HEAD_DIM)
    d_projected = jnp.stack(
        [rotate(d_queries, -positions), rotate(d_keys_own, -positions), d_values_own], axis=2
    )
    d_projected = d_projected.reshape(token_count, 3 * model_width).astype(jnp.bfloat16)
    d_attn_bias = jnp.sum(d_projected.astype(jnp.float32), axis=0)
    d_pair_bias = d_attn_bias[: 2 * model_width]
    d_value_bias = d_attn_bias[2 * model_width :]
    d_attn_weight = jnp.einsum(
        "td,tf->df", tokens_flat, d_projected, preferred_element_type=jnp.float32
    )
    grad_hidden = d_resid_one + jnp.dot(
        d_projected, attn_full.T, preferred_element_type=jnp.float32
    )
    attn_parts = (
        lax.psum_scatter(d_attn_weight, ("seq", "batch"), scatter_dimension=0, tiled=True),
        lax.psum_scatter(d_pair_bias, ("seq", "batch"), scatter_dimension=0, tiled=True),
        lax.psum_scatter(d_value_bias, ("seq", "batch"), scatter_dimension=0, tiled=True),
        lax.psum_scatter(d_proj_weight, ("seq", "batch"), scatter_dimension=0, tiled=True),
        lax.psum_scatter(d_proj_bias, ("seq", "batch"), scatter_dimension=0, tiled=True),
        lax.psum_scatter(d_gain_one, ("seq", "batch"), scatter_dimension=0, tiled=True),
        lax.psum_scatter(d_shift_one, ("seq", "batch"), scatter_dimension=0, tiled=True),
    )
    return (
        layer_out,
        grad_hidden.reshape(seq_count, span_rows, model_width),
        attn_parts[0],
        attn_parts[1],
        attn_parts[2],
        attn_parts[3],
        attn_parts[4],
        attn_parts[5],
        attn_parts[6],
        ffn_parts[0],
        ffn_parts[1],
        ffn_parts[2],
        ffn_parts[3],
        ffn_parts[4],
        ffn_parts[5],
    )


SEQ_SIDE = 8
BATCH_SIDE = 4
GROUP = 192
WIDE = 256
HERE = 3
EVEN = (0, 2, 4, 6)
ODD = (1, 3, 5, 7)
CORE, X, Y, Z, PLACE, LEN_MINE, LEN_OTHER = range(7)
F32, BF16 = jnp.float32, jnp.bfloat16
NN = (((1,), (0,)), ((), ()))
NT = (((1,), (1,)), ((), ()))
TN = (((0,), (0,)), ((), ()))


def swap_seq(value, mask):
    return lax.ppermute(value, "seq", [(i, i ^ mask) for i in range(SEQ_SIDE)])


def swap_batch(value, mask):
    return lax.ppermute(value, "batch", [(i, i ^ mask) for i in range(BATCH_SIDE)])


def after(value, *done):
    return lax.optimization_barrier((value,) + done)[0]


def fence(*values):
    return lax.optimization_barrier(values)


def shape(dims, dtype=BF16):
    return jax.ShapeDtypeStruct(dims, dtype)


def call(body, outs, info, *args, scratch=(), flops=0, name=None, alone=False):
    moved = sum(a.size * a.dtype.itemsize for a in args)
    moved += sum(math.prod(o.shape) * o.dtype.itemsize for o in outs)
    held = sum(math.prod(m.shape) * m.dtype.itemsize for m in scratch)
    return pl.pallas_call(
        lambda lengths, *refs: body(Spot(lengths), *refs),
        out_shape=outs,
        in_specs=[pl.BlockSpec(memory_space=pltpu.SMEM)]
        + [pl.BlockSpec(memory_space=pltpu.VMEM)] * len(args),
        out_specs=[pl.BlockSpec(memory_space=pltpu.VMEM)] * len(outs),
        scratch_shapes=[pltpu.VMEM(m.shape, m.dtype) for m in scratch],
        compiler_params=pltpu.CompilerParams(
            vmem_limit_bytes=60 << 20 if alone else min(56 << 20, moved + held + (10 << 20))
        ),
        cost_estimate=pl.CostEstimate(flops=1, bytes_accessed=1, transcendentals=0),
        name=name,
    )(info, *args)


def dot(left, right, dims=NN):
    return lax.dot_general(left, right, dims, preferred_element_type=F32)


class Spot:
    def __init__(self, lengths):
        self.lengths = lengths

    def __getitem__(self, what):
        place = lax.axis_index("seq")
        if what == Z:
            return lax.axis_index("batch")
        if what == LEN_MINE:
            return self.lengths[place >> 2]
        if what == LEN_OTHER:
            return self.lengths[1 - (place >> 2)]
        return {CORE: place & 1, X: (place >> 1) & 1, Y: place >> 2, PLACE: place}[what]


def chips(info):
    x, y = info[X], info[Y]
    return ((y, x), (y, 1 - x), (1 - y, x), (1 - y, 1 - x))


def lanes(start, size):
    return pl.ds(pl.multiple_of(start, 128), size)


def rows(start, size, unit=16):
    return pl.ds(pl.multiple_of(start, unit), size)


def prepare_body(
    info, hidden, attn, up, proj, down, v0, v1, v2, v3, v4, v5, v6, v7,
    mine, other, joined, early,
):
    y = info[Y]
    mine[...] = hidden[y]
    other[...] = hidden[1 - y]
    late = down[48:96].astype(F32)
    early[...] = down[:48]
    parts = [v[...].astype(F32) for v in (v0, v1, v2, v3, v4, v5, v6, v7)]
    row = jnp.concatenate(parts + [jnp.zeros((1, 8), F32)], axis=1)
    small = jnp.concatenate(
        [row[:, 64 * i : 64 * (i + 1)] for i in range(5)] + [jnp.zeros((19, 64), F32)], axis=0
    )
    small = jnp.concatenate([small, jnp.zeros((24, 64), F32)], axis=1).astype(BF16)
    for k in range(4):
        joined[k, :, :3072] = up[...]
        joined[k, :, 3072:3840] = proj[...]
        joined[k, :, 3840:4608] = late[:24].astype(BF16)
        joined[k, :, 4608:5376] = late[24:].astype(BF16)
        joined[k, :, 5376:7680] = attn[...]
        joined[k, :, 7680:] = small


def attn_column_body(info, pieces, out):
    column = jnp.concatenate([pieces[zz, :, 5376:].astype(F32) for zz in range(4)], axis=0)
    small = [column[24 * zz + i : 24 * zz + i + 1, 2304:2368] for i in range(5) for zz in range(4)]
    small = jnp.concatenate(small + [jnp.zeros((76, 64), F32)], axis=0)
    for g in range(4):
        part = jnp.concatenate(
            [column[:, 768 * i + GROUP * g : 768 * i + GROUP * (g + 1)] for i in range(3)] + [small],
            axis=1,
        ).astype(BF16)
        out[g] = part
        out[4 + g] = part


def up_column_body(info, pieces, keep, sent, rest, held):
    core = info[CORE]
    column = jnp.concatenate(
        [pieces[zz, :, :3840].astype(F32) for zz in range(4)], axis=0
    ).astype(BF16)
    held[...] = column[:, :3072]
    rest[:96] = column[:, 3072:]
    for zz in range(4):
        rest[96 + 48 * zz : 144 + 48 * zz] = jnp.concatenate(
            [pieces[zz, :, 3840:4608].astype(F32), pieces[zz, :, 4608:5376].astype(F32)], axis=0
        ).astype(BF16)
    for which, out in ((core, keep), (1 - core, sent)):
        for q in range(4):
            out[96 * (q // 2) : 96 * (q // 2 + 1), 384 * (q % 2) : 384 * (q % 2 + 1)] = held[
                :, lanes(768 * q + 384 * which, 384)
            ]


def up_join_body(info, keep, came, rest, out):
    out[0:96] = keep[:96]
    out[96:192] = came[:96]
    out[192:288] = keep[96:]
    out[288:384] = came[96:]
    out[384:672] = rest[...]


def early_body(info, p0, px, py, pd, out):
    for j, p in enumerate((p0, px, py, pd)):
        out[48 * j : 48 * (j + 1)] = p[...]


def attend_body(
    info, mine, r2, r4, r6, odd, given, cosine, sine,
    x_out, weight, qt_out, k_out, v_out, att_out, stats, even_low, odd_low,
):
    weight[:, :, GROUP:] = jnp.zeros((3, 768, WIDE - GROUP), BF16)
    for i in range(3):
        for s in range(8):
            weight[i, 96 * s : 96 * (s + 1), :GROUP] = given[s, :, GROUP * i : GROUP * (i + 1)]
    small = jnp.concatenate(
        [
            jnp.concatenate([given[s, 0:16, 576:640][4 * i : 4 * (i + 1)] for s in range(8)], axis=0)
            for i in range(2)
        ],
        axis=1,
    ).astype(F32)
    group = info[PLACE] & 3

    def bias_row(i):
        entry = 768 * i + GROUP * group + lax.broadcasted_iota(jnp.int32, (128, WIDE), 1)
        source = lax.broadcasted_iota(jnp.int32, (128, WIDE), 0)
        picked = dot(small.astype(BF16), jnp.where(source == entry % 72, 1.0, 0.0).astype(BF16))
        picked = jnp.where(source[:32] == entry[:32] // 72, picked, 0.0)
        used = lax.broadcasted_iota(jnp.int32, (1, WIDE), 1) < GROUP
        return jnp.where(used, column_sum(picked), 0.0)

    x_out[0:128] = mine[...]
    x_out[128:256] = r2[...]
    x_out[256:384] = r4[...]
    x_out[384:512] = r6[...]
    x_out[512:1024] = odd[...]
    tokens = x_out[...]
    lane = lax.broadcasted_iota(jnp.int32, (1024, WIDE), 1)
    is_even = lane % 2 == 0

    def part(i):
        return dot(tokens, weight[i]) + bias_row(i)

    def turned(value):
        left = pltpu.roll(value, WIDE - 1, 1)
        right = pltpu.roll(value, 1, 1)
        return value * cosine[...] + jnp.where(is_even, left, right) * sine[...]

    query = turned(part(0)).astype(BF16).astype(F32) * (HEAD_DIM**-0.5)
    query = jnp.where(lane == GROUP, 1.0, query).T.astype(BF16)
    qt_out[...] = query
    index = lax.broadcasted_iota(jnp.int32, (1024, WIDE), 0)
    block = index >> 7
    owner = info[PLACE] ^ (((block & 3) << 1) | (block >> 2))
    valid = owner * 128 + (index & 127) < info[LEN_MINE]
    padding = jnp.where(valid, 0.0, NEG_BIG)
    key = jnp.where(lane == GROUP, padding, turned(part(1))).astype(BF16)
    k_out[...] = key
    value = part(2).astype(BF16)
    v_out[...] = value
    value_t = value.astype(F32).T
    ones = jnp.ones((16, 1024), BF16)
    row = lax.broadcasted_iota(jnp.int32, (WIDE, WIDE), 0)
    for h in range(HERE):
        here = (row // HEAD_DIM == h) | (row == GROUP)
        value_h = jnp.concatenate(
            [value_t[HEAD_DIM * h : HEAD_DIM * (h + 1)].astype(BF16), ones], axis=0
        )
        for b in range(4):
            block = qt_out[:, WIDE * b : WIDE * (b + 1)].astype(F32)
            scores = dot(key, jnp.where(here, block, 0.0).astype(BF16))
            top = jnp.max(scores, axis=0, keepdims=True)
            weights = jnp.exp(scores - top).astype(BF16)
            summed = dot(value_h, weights)
            total = summed[HEAD_DIM : HEAD_DIM + 1]
            att_out[HEAD_DIM * h : HEAD_DIM * (h + 1), WIDE * b : WIDE * (b + 1)] = (
                summed[:HEAD_DIM] / total
            )
            stats[h : h + 1, WIDE * b : WIDE * (b + 1)] = top
            stats[4 + h : 5 + h, WIDE * b : WIDE * (b + 1)] = total
    low = att_out[...].T.astype(BF16)
    for i in range(4):
        even_low[i] = low[128 * i : 128 * (i + 1)]
        odd_low[i] = low[512 + 128 * i : 640 + 128 * i]


def small_body(info, given, vectors, up_bias):
    core = info[CORE]
    values = jnp.concatenate(
        [
            jnp.concatenate([given[s, 0:32, 576:640][4 * i : 4 * (i + 1)] for s in range(8)], axis=0)
            for i in range(5)
        ],
        axis=1,
    ).astype(F32)
    entry = lax.broadcasted_iota(jnp.int32, (32, 768), 1)
    source = lax.broadcasted_iota(jnp.int32, (32, 768), 0)
    spread = jnp.where(source == entry % 24, 1.0, 0.0).astype(BF16)
    here = source == entry // 24
    padding = jnp.zeros((32, 8), F32)
    for i in range(6):
        part = jnp.concatenate([values[:, 72 + 24 * i : 96 + 24 * i], padding], axis=1)
        vectors[i : i + 1] = column_sum(jnp.where(here, dot(part.astype(BF16), spread), 0.0))
    entry = lax.broadcasted_iota(jnp.int32, (128, 1536), 1)
    entry = entry // 384 * 768 + core * 384 + entry % 384
    source = lax.broadcasted_iota(jnp.int32, (128, 1536), 0)
    spread = jnp.where(source == entry % 96, 1.0, 0.0).astype(BF16)
    part = jnp.concatenate([values[:, 216:312], jnp.zeros((32, 32), F32)], axis=1)
    part = dot(part.astype(BF16), spread)
    up_bias[...] = column_sum(jnp.where(source[:32] == entry[:32] // 96, part, 0.0))


def pair_body(info, own, came, p0, p1, p2, p3):
    for i, out in enumerate((p0, p1, p2, p3)):
        out[...] = jnp.concatenate(
            [own[i].astype(F32), came[i].astype(F32)], axis=1
        ).astype(BF16)


def proj_rows_body(info, d0, dx, dy, dd, out):
    for i, d in enumerate((d0, dx, dy, dd)):
        out[i] = d[384:480]


def attn_order(info):
    x, core = info[X], info[CORE]
    return ((x, core), (x, 1 - core), (1 - x, core), (1 - x, 1 - core))


def mix_body(
    info, p0, r2, r4, r6, d0, dx, dy, dd, proj_came, mine, other, vectors,
    normed_out, low_out, hat_out, rstd_out, rows_out, proj, held,
):
    core = info[CORE]
    for j, (yy, xx) in enumerate(chips(info)):
        held[rows((yy * 4 + xx * 2 + core) * 96, 96), :] = (d0, dx, dy, dd)[j][384:480]
        held[rows((yy * 4 + xx * 2 + 1 - core) * 96, 96), :] = proj_came[j]
    for i, (xx, cc) in enumerate(attn_order(info)):
        proj[GROUP * i : GROUP * (i + 1)] = held[rows((xx * 2 + cc) * GROUP, GROUP), :]
    rows_out[0:128, 0:384] = p0[...]
    rows_out[0:128, 384:768] = r2[...]
    rows_out[128:256, 0:384] = r4[...]
    rows_out[128:256, 384:768] = r6[...]
    tokens = jnp.concatenate([mine[...], other[...]], axis=0).astype(F32)
    resid = tokens + dot(rows_out[...], proj[...]) + vectors[0:1, :]
    centred = resid - jnp.mean(resid, axis=1, keepdims=True)
    rstd = lax.rsqrt(jnp.mean(centred * centred, axis=1, keepdims=True) + EPSILON)
    hat = centred * rstd
    normed = hat * vectors[1:2, :] + vectors[2:3, :]
    hat_out[...] = hat
    rstd_out[...] = jnp.broadcast_to(rstd, (256, 128))
    normed_out[...] = normed
    low_out[...] = normed.astype(BF16)


def whole_up(info, blocks, held):
    core = info[CORE]
    for block, (yy, xx) in zip(blocks, chips(info)):
        for half in range(2):
            span = slice(768 * half, 768 * (half + 1))
            for i, cc in enumerate((core, 1 - core)):
                held[rows((yy * 4 + xx * 2 + cc) * 96, 96), span] = block[
                    192 * half + 96 * i : 192 * half + 96 * (i + 1)
                ]


def whole_down(info, blocks, early, held):
    z = info[Z]
    for j, (yy, xx) in enumerate(chips(info)):
        base = (yy * 2 + xx) * 384
        for zz in range(4):
            held[rows(base + 96 * zz + 48, 48), :] = blocks[j][480 + 48 * zz : 528 + 48 * zz]
        for k, piece in enumerate(early):
            held[rows(base + 96 * (z ^ k), 48), :] = piece[48 * j : 48 * (j + 1)]


def gelu_parts(upward):
    gauss = jnp.exp(-0.5 * upward * upward)
    t = 1.0 / (1.0 + (0.3275911 * 2.0**-0.5) * jnp.abs(upward))
    poly = t * (
        0.127414796
        + t * (-0.142248368 + t * (0.7107068705 + t * (-0.7265760135 + t * 0.5307027145)))
    )
    tail = poly * gauss
    below = jnp.where(upward < 0, tail, 1.0 - tail)
    return upward * below, below + upward * gauss * 0.3989422804014327


def up_body(
    info, low_mine, low_other, u0, ux, uy, ud, d0, d1, d2, d3, bias,
    part_mine, part_other, active_out, slope_out, up_held, down_held,
):
    whole_up(info, (u0, ux, uy, ud), up_held)
    whole_down(info, (u0, ux, uy, ud), (d0, d1, d2, d3), down_held)
    for i, low in enumerate((low_mine, low_other)):
        upward = dot(low[...], up_held[...]) + bias[...]
        active, slope = gelu_parts(upward)
        active = active.astype(BF16)
        active_out[256 * i : 256 * (i + 1)] = active
        slope_out[256 * i : 256 * (i + 1)] = slope.astype(BF16)
        part = dot(active, down_held[...])
        if i == 0:
            part_mine[...] = part
        else:
            part_other[...] = part.astype(BF16)


def back_norm(d_hat, hat, rstd):
    return rstd * (
        d_hat
        - jnp.mean(d_hat, axis=1, keepdims=True)
        - hat * jnp.mean(d_hat * hat, axis=1, keepdims=True)
    )


def column_sum(value):
    return jnp.sum(value, axis=0, keepdims=True)


def norm_two_body(
    info, part_mine, came, normed, vectors, grad, out, d_resid_out, d_low, sums,
):
    y = info[Y]
    resid = normed[...] + (part_mine[...] + came[...].astype(F32) + vectors[3:4, :])
    centred = resid - jnp.mean(resid, axis=1, keepdims=True)
    rstd = lax.rsqrt(jnp.mean(centred * centred, axis=1, keepdims=True) + EPSILON)
    hat = centred * rstd
    result = (hat * vectors[4:5, :] + vectors[5:6, :]).astype(BF16)
    out[y] = result[:128]
    out[1 - y] = result[128:]
    position = info[PLACE] * 128 + lax.broadcasted_iota(jnp.int32, (128, 768), 0)
    first = jnp.where(position < info[LEN_MINE], grad[y].astype(F32), 0.0)
    second = jnp.where(position < info[LEN_OTHER], grad[1 - y].astype(F32), 0.0)
    cotangent = jnp.concatenate([first, second], axis=0)
    d_resid = back_norm(cotangent * vectors[4:5, :], hat, rstd)
    d_resid_out[...] = d_resid
    low = d_resid.astype(BF16)
    d_low[...] = low
    sums[0:1] = column_sum(low.astype(F32))
    sums[1:2] = column_sum(cotangent * hat)
    sums[2:3] = column_sum(cotangent)


def down_grad_body(info, active, d_mine, d_other, g0, gx, gy, da, db, held):
    d_low = jnp.concatenate([d_mine[...], d_other[...]], axis=0)
    for i in range(4):
        held[384 * i : 384 * (i + 1)] = dot(
            active[:, 384 * i : 384 * (i + 1)], d_low, TN
        ).astype(BF16)
    outs = ((g0,), (gx,), (gy,), (da, db))
    for out, (yy, xx) in zip(outs, chips(info)):
        base = (yy * 2 + xx) * 384
        if len(out) == 1:
            out[0][...] = held[rows(base, 384), :]
        else:
            out[0][...] = held[rows(base, 192), :]
            out[1][...] = held[rows(base + 192, 192), :]


def up_grad_body(
    info, d_mine, d_other, slope, low_mine, low_other, u0, ux, uy, ud, d0, d1, d2, d3,
    part_mine, part_other, g0, gx, gy, gd, z0, z1, z2, z3, sums, up_held, down_held, held,
):
    core = info[CORE]
    whole_up(info, (u0, ux, uy, ud), up_held)
    whole_down(info, (u0, ux, uy, ud), (d0, d1, d2, d3), down_held)
    d_ups = []
    total = jnp.zeros((1, 1536), F32)
    for i, d_low in enumerate((d_mine, d_other)):
        d_active = dot(d_low[...], down_held[...], NT)
        d_up = (slope[256 * i : 256 * (i + 1)].astype(F32) * d_active).astype(BF16)
        total = total + column_sum(d_up.astype(F32))
        d_ups.append(d_up)
        part = dot(d_up, up_held[...], NT)
        if i == 0:
            part_mine[...] = part
        else:
            part_other[...] = part.astype(BF16)
    sums[...] = total
    d_up = jnp.concatenate(d_ups, axis=0)
    low = jnp.concatenate([low_mine[...], low_other[...]], axis=0)
    held[...] = dot(low, d_up, TN)
    z = info[Z]
    for j, (yy, xx) in enumerate(chips(info)):
        for i, cc in enumerate((core, 1 - core)):
            base = (yy * 4 + xx * 2 + cc) * 96
            (g0, gx, gy, gd)[j][96 * i : 96 * (i + 1)] = held[rows(base, 96), :768].astype(BF16)
    for k, out in enumerate((z0, z1, z2, z3)):
        for j, (yy, xx) in enumerate(chips(info)):
            block = [
                held[rows((yy * 4 + xx * 2 + cc) * 96 + (z ^ k) * 24, 24, 8), 768:]
                for cc in (core, 1 - core)
            ]
            out[48 * j : 48 * (j + 1)] = jnp.concatenate(block, axis=0).astype(BF16)


def norm_one_body(
    info, d_resid_two, part_mine, came, hat, rstd, vectors, rows_here, proj,
    d_resid_out, e0, e2, e4, e6, proj_own, proj_sent, sums, held,
):
    core = info[CORE]
    d_normed = d_resid_two[...] + part_mine[...] + came[...].astype(F32)
    sums[0:1] = column_sum(d_normed * hat[...])
    sums[1:2] = column_sum(d_normed)
    d_resid = back_norm(d_normed * vectors[1:2, :], hat[...], rstd[:, 0:1])
    d_resid_out[...] = d_resid
    low = d_resid.astype(BF16)
    sums[2:3] = column_sum(low.astype(F32))
    d_att = dot(low, proj[...], NT).astype(BF16)
    e0[...] = d_att[:128, :384]
    e2[...] = d_att[:128, 384:]
    e4[...] = d_att[128:, :384]
    e6[...] = d_att[128:, 384:]
    d_weight = dot(rows_here[...], low, TN).astype(BF16)
    for i, (xx, cc) in enumerate(attn_order(info)):
        held[rows((xx * 2 + cc) * GROUP, GROUP), :] = d_weight[GROUP * i : GROUP * (i + 1)]
    for j, (yy, xx) in enumerate(chips(info)):
        proj_own[j] = held[rows((yy * 4 + xx * 2 + core) * 96, 96), :]
        proj_sent[j] = held[rows((yy * 4 + xx * 2 + 1 - core) * 96, 96), :]


def split_core_body(info, e0, e2, e4, e6, out):
    for i, e in enumerate((e0, e2, e4, e6)):
        out[128 * i : 128 * (i + 1)] = e[...].astype(F32)[:, GROUP:].astype(BF16)


def attend_back_body(
    info, e0, e2, e4, e6, came, qt, key, value, att, stats, cosine, sine,
    d_proj, sums, guide, weights_held, d_scores_held, dq_held, dk_held, dv_held,
):
    d_att = jnp.concatenate(
        [e[...].astype(F32)[:, :GROUP] for e in (e0, e2, e4, e6)] + [came[...].astype(F32)], axis=0
    )
    d_att_t = d_att.T
    product = d_att_t * att[...]
    pieces = []
    deltas = []
    for h in range(HERE):
        here = slice(HEAD_DIM * h, HEAD_DIM * (h + 1))
        total = stats[4 + h : 5 + h, :]
        pieces.append(d_att_t[here] / total)
        deltas.append(column_sum(product[here]) / total)
    pieces.append(jnp.zeros((WIDE - GROUP, 1024), F32))
    guide[...] = jnp.concatenate(pieces, axis=0).astype(BF16)
    key_t = key[...].astype(F32).T
    row = lax.broadcasted_iota(jnp.int32, (WIDE, WIDE), 0)
    dk_held[...] = jnp.zeros((1024, WIDE), F32)
    dv_held[...] = jnp.zeros((1024, WIDE), F32)
    dq_held[GROUP:] = jnp.zeros((WIDE - GROUP, 1024), F32)
    wide_row = lax.broadcasted_iota(jnp.int32, (WIDE, 1024), 0)
    for h in range(HERE):
        mine = row // HEAD_DIM == h
        with_pad = mine | (row == GROUP)
        key_h = key_t[HEAD_DIM * h : HEAD_DIM * (h + 1)].astype(BF16)
        for b in range(4):
            span = slice(WIDE * b, WIDE * (b + 1))
            q_block = jnp.where(with_pad, qt[:, span].astype(F32), 0.0).astype(BF16)
            g_block = jnp.where(mine, guide[:, span].astype(F32), 0.0).astype(BF16)
            scores = dot(key[...], q_block)
            weights = jnp.exp(scores - stats[h : h + 1, span])
            d_weights = dot(value[...], g_block)
            d_scores = (weights * (d_weights - deltas[h][:, span])).astype(BF16)
            weights_held[:, span] = weights.astype(BF16)
            d_scores_held[:, span] = d_scores
            dq_held[HEAD_DIM * h : HEAD_DIM * (h + 1), span] = dot(key_h, d_scores)
        here = wide_row // HEAD_DIM == h
        q_all = jnp.where(here, qt[...].astype(F32), 0.0).astype(BF16)
        g_all = jnp.where(here, guide[...].astype(F32), 0.0).astype(BF16)
        dk_held[...] += dot(d_scores_held[...], q_all, NT)
        dv_held[...] += dot(weights_held[...], g_all, NT)
    lane = lax.broadcasted_iota(jnp.int32, (1024, WIDE), 1)
    is_even = lane % 2 == 0

    def turned_back(value):
        left = pltpu.roll(value, WIDE - 1, 1)
        right = pltpu.roll(value, 1, 1)
        return value * cosine[...] - jnp.where(is_even, left, right) * sine[...]

    d_query = turned_back(dq_held[...].T * (HEAD_DIM**-0.5)).astype(BF16)
    d_key = turned_back(dk_held[...]).astype(BF16)
    d_value = dv_held[...].astype(BF16)
    for i, part in enumerate((d_query, d_key, d_value)):
        d_proj[i] = part
        sums[i : i + 1] = column_sum(part.astype(F32))


def attn_grad_body(info, tokens, d_proj, small, out):
    parts = [dot(tokens[...], d_proj[i], TN)[:, :GROUP] for i in range(3)]
    whole = jnp.concatenate(parts, axis=1)
    for s in range(8):
        beside = jnp.concatenate([small[s], jnp.zeros((56, 64), F32)], axis=0)
        out[s] = jnp.concatenate([whole[96 * s : 96 * (s + 1)], beside], axis=1).astype(BF16)


def sum_four_body(info, first, r1, r2, r3, out):
    out[...] = (
        first[...] + r1[...].astype(F32) + r2[...].astype(F32) + r3[...].astype(F32)
    )


def hidden_grad_body(info, d_proj, weight, even_out, odd_out):
    total = jnp.zeros((1024, 768), F32)
    for i in range(3):
        total = total + dot(d_proj[i], weight[i], NT)
    even_out[...] = total[:512]
    odd_out[...] = total[512:].astype(BF16)


def first_sums_body(info, jx, cy, jy, cx, down, x_out, y_out, first, s1, s2, s3, held):
    x_out[:144] = jx[:144]
    x_out[144:] = (jx[144:].astype(F32) + cy[384:].astype(F32)).astype(BF16)
    y_out[:144] = (jy[:144].astype(F32) + cx[384:].astype(F32)).astype(BF16)
    y_out[144:] = jy[144:]
    z = info[Z]
    held[...] = down[...].astype(F32) + cx[:384].astype(F32) + cy[:384].astype(F32)
    for k, out in enumerate((first, s1, s2, s3)):
        out[...] = held[rows((z ^ k) * 96, 96), :].astype(out.dtype)


def second_sums_body(info, even, came, u0, u1, u2, u3, own, half_first, x_out, y_out, across):
    hidden = even[...] + came[...].astype(F32)
    up = u0[...].astype(F32) + u1[...].astype(F32) + u2[...].astype(F32) + u3[...].astype(F32)
    own[...] = hidden[:128]
    half_first[...] = up[:48]
    for i, out in enumerate((x_out, y_out, across)):
        out[:48] = up[48 * (i + 1) : 48 * (i + 2)].astype(BF16)
        out[48:] = hidden[128 * (i + 1) : 128 * (i + 2)].astype(BF16)


def small_grads_body(info, attn, one, two, up, out):
    core = info[CORE]
    group = info[PLACE] & 3

    def split(value, place):
        n = value.shape[1]
        entry = lax.broadcasted_iota(jnp.int32, (1, n), 1)
        return jnp.where(
            lax.broadcasted_iota(jnp.int32, (32, n), 0) == place(entry), value, 0.0
        )

    def gather(value, width):
        n = value.shape[1]
        entry = lax.broadcasted_iota(jnp.int32, (n, 1), 0) % width
        chosen = jnp.where(lax.broadcasted_iota(jnp.int32, (n, 128), 1) == entry, 1.0, 0.0)
        return lax.dot_general(
            value, chosen, NN, precision=lax.Precision.HIGHEST, preferred_element_type=F32
        )

    inside = lax.broadcasted_iota(jnp.int32, (1, WIDE), 1) < GROUP
    own = [jnp.where(inside, attn[i : i + 1], 0.0) for i in range(3)]
    pairs = gather(
        split(own[0], lambda n: 4 * group + n // 48)
        + split(own[1], lambda n: 16 + 4 * group + n // 48),
        48,
    )
    values = gather(split(own[2], lambda n: 8 * group + n // 24), 24)
    six = (one[2:3], one[0:1], one[1:2], two[0:1], two[1:2], two[2:3])
    six = gather(jnp.concatenate([split(v, lambda n: n // 24) for v in six], axis=0), 24)
    ups = gather(split(up[...], lambda n: n // 96 + 4 * (n // 384) + 4 * core), 96)
    parts = [pairs[:, :48], values[:, :24]]
    parts += [six[32 * i : 32 * (i + 1), :24] for i in range(6)]
    parts += [ups[:, :96], jnp.zeros((32, 8), F32)]
    row = jnp.concatenate(parts, axis=1)
    high = row.astype(BF16).astype(F32)
    for s in range(8):
        here = slice(4 * s, 4 * (s + 1))
        out[s] = jnp.concatenate(
            [v[here, 64 * i : 64 * (i + 1)] for v in (high, row - high) for i in range(5)], axis=0
        )


def last_blocks_body(info, own, a, b, came, first, s1, s2, s3, up_held, attn_held, small_held):
    z = info[Z]
    up_held[...] = own[...].astype(F32) + a[...].astype(F32) + b[...].astype(F32)
    for g in range(4):
        attn_held[g] = came[g].astype(F32) + came[4 + g].astype(F32)
    small = sum(attn_held[g, :40, 576:] for g in range(4))
    small = small[:20] + small[20:]
    pad = jnp.zeros((1, 64), F32)
    for zz in range(4):
        small_held[zz] = jnp.concatenate(
            [small[4 * i + zz : 4 * i + zz + 1] for i in range(5)] + [pad], axis=1
        )
    for k, out in enumerate((first, s1, s2, s3)):
        parts = [up_held[rows(96 * i + (z ^ k) * 24, 24, 8), :] for i in range(3)]
        blocks = [attn_held[g, rows((z ^ k) * 24, 24, 8), :] for g in range(4)]
        for i in range(3):
            parts.append(
                jnp.concatenate([b[:, GROUP * i : GROUP * (i + 1)] for b in blocks], axis=1)
            )
        row = small_held[z ^ k]
        high = row.astype(BF16).astype(F32)
        parts.append(jnp.concatenate([high, row - high], axis=1))
        parts.append(jnp.zeros((7, 768), F32))
        out[...] = jnp.concatenate(parts, axis=0).astype(out.dtype)


def last_sum_body(info, first, r1, r2, r3, half, proj_out, attn_out, small):
    total = first[...] + r1[...].astype(F32) + r2[...].astype(F32) + r3[...].astype(F32)
    half[...] = total[:48]
    proj_out[...] = total[48:72]
    for i in range(3):
        attn_out[:, 768 * i : 768 * (i + 1)] = total[72 + 24 * i : 96 + 24 * i]
    small[...] = total[144:145, :384] + total[144:145, 384:]


def end_sum_body(info, half, other_half, d_resid, hidden, r2, r4, r6, own, sent, out):
    y = info[Y]
    other = other_half[...] + r2[:48].astype(F32) + r4[:48].astype(F32) + r6[:48].astype(F32)
    own[...] = jnp.concatenate([half[:24], other[:24]], axis=1)
    sent[...] = jnp.concatenate([half[24:], other[24:]], axis=1).astype(BF16)
    out[y] = d_resid[:128] + hidden[...] + r2[48:].astype(F32)
    out[1 - y] = d_resid[128:] + r4[48:].astype(F32) + r6[48:].astype(F32)


def up_end_body(info, own, came, up_out):
    core = info[CORE]
    for which, source in ((core, own), (1 - core, came)):
        for q in range(4):
            up_out[:, lanes(768 * q + 384 * which, 384)] = source[
                :, 384 * q : 384 * (q + 1)
            ].astype(F32)


def join_body(
    info, g0, gx, gy, gd, p_own, p_came, dx, d_from_y, dy, d_from_x, j0, jx, jy, mx, my
):
    proj = [(p_own[j].astype(F32) + p_came[j].astype(F32)).astype(BF16) for j in range(4)]
    for j, (g, out) in enumerate(((g0, j0), (gx, jx), (gy, jy))):
        out[:192] = g[...]
        out[192:] = proj[j]
    mx[:192] = dx[:192]
    mx[192:384] = (dx[192:].astype(F32) + d_from_y[...].astype(F32)).astype(BF16)
    my[:192] = (dy[:192].astype(F32) + d_from_x[...].astype(F32)).astype(BF16)
    my[192:384] = dy[192:]
    mx[384:] = gd[:144]
    my[384:432] = gd[144:]
    my[432:] = proj[3]
def split_layer(
    hidden_in,
    lengths,
    attn_weight,
    attn_bias,
    proj_weight,
    proj_bias,
    first_gain,
    first_shift,
    up_weight,
    up_bias,
    down_weight,
    down_bias,
    second_gain,
    second_shift,
    grad_out,
):
    both_axes = ("seq", "batch")
    place = lax.axis_index("seq")
    info = lengths

    small_vectors = (
        attn_bias, proj_bias, first_gain, first_shift, down_bias, second_gain, second_shift, up_bias
    )
    mine, other, joined, early = call(
        prepare_body,
        [
            shape((128, 768)), shape((128, 768)), shape((4, 24, 7808)), shape((48, 768)),
        ],
        info, hidden_in, attn_weight, up_weight, proj_weight, down_weight,
        *[v[None] for v in small_vectors], name="prepare", alone=True,
    )
    owners = place ^ jnp.array(EVEN + ODD, jnp.int32)
    positions = (owners[:, None] * 128 + jnp.arange(128, dtype=jnp.int32)[None, :]).reshape(-1)
    entry = jnp.arange(WIDE)
    frequency = 10000.0 ** (-2.0 * ((entry % HEAD_DIM) // 2).astype(F32) / HEAD_DIM)
    angles = positions.astype(F32)[:, None] * frequency[None, :]
    used = (entry < GROUP).astype(F32)
    cosine = jnp.cos(angles) * used
    sine = jnp.sin(angles) * (used * jnp.where(entry % 2 == 0, -1.0, 1.0))
    joined = lax.all_to_all(joined, "batch", 0, 0, tiled=True)
    r2, r4, r6 = swap_seq(mine, 2), swap_seq(other, 4), swap_seq(other, 6)
    odd = swap_seq(jnp.concatenate([mine, r2, r4, r6], axis=0), 1)
    early_far = [swap_seq(early, k) for k in (2, 4, 6)]
    (early_plane,) = call(early_body, [shape((192, 768))], info, early, *early_far, name="early")
    joined, odd, cosine, sine, early_plane = fence(joined, odd, cosine, sine, early_plane)

    (weight_sent,) = call(
        attn_column_body, [shape((8, 96, 640))], info, joined, name="attn_column"
    )
    weight_given = lax.all_to_all(weight_sent, "seq", 0, 0, tiled=True)
    up_keep, up_sent, rest = call(
        up_column_body, [shape((192, 768)), shape((192, 768)), shape((288, 768))],
        info, joined, scratch=[shape((96, 3072))], name="up_column",
    )
    (up_column,) = call(
        up_join_body, [shape((672, 768))], info, up_keep, swap_seq(up_sent, 1), rest,
        name="up_join",
    )
    up_column, early_plane = fence(up_column, early_plane)

    up_x, up_y = swap_seq(up_column, 2), swap_seq(up_column, 4)
    early_far = [swap_batch(early_plane, k) for k in (1, 2, 3)]
    weight_given = fence(weight_given)[0]

    tokens_here, weight_here, query_t, key, value, attended, stats, even_low, odd_low = call(
        attend_body,
        [
            shape((1024, 768)), shape((3, 768, WIDE)),
            shape((WIDE, 1024)), shape((1024, WIDE)), shape((1024, WIDE)),
            shape((GROUP, 1024), F32), shape((8, 1024), F32),
            shape((4, 128, GROUP)), shape((4, 128, GROUP)),
        ],
        info, mine, r2, r4, r6, odd, weight_given, cosine, sine,
        flops=8_000_000_000, name="attend", alone=True,
    )
    even_low, odd_low, early_far, weight_given = fence(even_low, odd_low, early_far, weight_given)

    p0, p1, p2, p3 = call(
        pair_body, [shape((128, 384))] * 4, info, even_low, swap_seq(odd_low, 1), name="pair"
    )
    p0, p1, p2, p3, up_x, up_y, early_far = fence(p0, p1, p2, p3, up_x, up_y, early_far)

    a2, a4, a6 = swap_seq(p1, 2), swap_seq(p2, 4), swap_seq(p3, 6)
    up_da, up_db = swap_seq(up_y[:336], 2), swap_seq(up_x[336:], 4)
    vectors, up_bias_here = call(
        small_body, [shape((8, 768), F32), shape((1, 1536), F32)], info, after(weight_given, p0), name="small"
    )
    a2, a4, a6, up_da, up_db, vectors, up_bias_here = fence(
        a2, a4, a6, up_da, up_db, vectors, up_bias_here
    )
    up_blocks = (up_column, up_x, up_y, jnp.concatenate([up_da, up_db], axis=0))
    down_blocks = (early_plane, *early_far)
    (proj_rows,) = call(proj_rows_body, [shape((4, 96, 768))], info, *up_blocks, name="proj_rows")
    proj_came = swap_seq(proj_rows, 1)
    normed, low_mine, hat_one, rstd_one, rows_here, proj_here = call(
        mix_body,
        [
            shape((256, 768), F32), shape((256, 768)), shape((256, 768), F32),
            shape((256, 128), F32), shape((256, 768)), shape((768, 768)),
        ],
        info, p0, a2, a4, a6, *up_blocks, proj_came, mine, other, vectors,
        scratch=[shape((768, 768))], flops=300_000_000, name="mix",
    )
    low_other = swap_seq(low_mine, 1)
    part_mine, part_other, active, slope = call(
        up_body,
        [shape((256, 768), F32), shape((256, 768)), shape((512, 1536)), shape((512, 1536))],
        info, low_mine, low_other, *up_blocks, *down_blocks, up_bias_here,
        scratch=[shape((768, 1536)), shape((1536, 768))], flops=2_400_000_000, name="up",
    )
    layer_out, d_resid_two, d_low, sums_two = call(
        norm_two_body,
        [shape((2, 128, 768)), shape((256, 768), F32), shape((256, 768)), shape((8, 768), F32)],
        info, part_mine, swap_seq(part_other, 1), normed, vectors, grad_out, name="norm_two",
    )
    d_came = swap_seq(d_low, 1)
    g_down, gx_down, gy_down, gda, gdb = call(
        down_grad_body, [shape((384, 768))] * 3 + [shape((192, 768))] * 2,
        info, active, d_low, d_came,
        scratch=[shape((1536, 768))], flops=1_200_000_000, name="down_grad",
    )
    gx_down, gy_down, gda, gdb, d_low, d_came = fence(gx_down, gy_down, gda, gdb, d_low, d_came)

    gda, gdb = swap_seq(gda, 2), swap_seq(gdb, 4)
    part_mine, part_other, g0, gx, gy, gd, z0, z1, z2, z3, up_sums = call(
        up_grad_body,
        [shape((256, 768), F32), shape((256, 768))] + [shape((192, 768))] * 8
        + [shape((1, 1536), F32)],
        info, d_low, d_came, slope, low_mine, low_other, *up_blocks, *down_blocks,
        scratch=[shape((768, 1536)), shape((1536, 768)), shape((768, 1536), F32)],
        flops=3_600_000_000, name="up_grad",
    )
    gda, gdb, part_mine, part_other = fence(gda, gdb, part_mine, part_other)
    d_resid_one, e0, e2, e4, e6, proj_own, proj_sent, sums_one = call(
        norm_one_body,
        [shape((256, 768), F32)] + [shape((128, 384))] * 4 + [shape((4, 96, 768))] * 2
        + [shape((8, 768), F32)],
        info, d_resid_two, part_mine, swap_seq(part_other, 1), hat_one, rstd_one, vectors,
        rows_here, proj_here,
        scratch=[shape((768, 768))], flops=600_000_000, name="norm_one",
    )
    e0, e2, e4, e6, proj_sent = fence(e0, e2, e4, e6, proj_sent)

    e2, e4, e6 = swap_seq(e2, 2), swap_seq(e4, 4), swap_seq(e6, 6)
    proj_came = swap_seq(proj_sent, 1)
    j0, jx, jy, mx, my = call(
        join_body, [shape((288, 768))] * 3 + [shape((528, 768))] * 2,
        info, g0, gx, gy, gd, proj_own, proj_came, gx_down, gdb, gy_down, gda, name="join",
    )
    e2, e4, e6, j0, jx, jy, mx, my = fence(e2, e4, e6, j0, jx, jy, mx, my)
    (split,) = call(split_core_body, [shape((512, GROUP))], info, e0, e2, e4, e6, name="split")
    e_came = swap_seq(split, 1)
    e_came, mx, my, z1, z2, z3 = fence(e_came, mx, my, z1, z2, z3)

    mx, my = swap_seq(mx, 2), swap_seq(my, 4)
    z_came = [swap_batch(part, k) for k, part in zip((1, 2, 3), (z1, z2, z3))]
    d_proj, sums_attn = call(
        attend_back_body,
        [shape((3, 1024, WIDE)), shape((8, WIDE), F32)],
        info, e0, e2, e4, e6, e_came, query_t, key, value, attended, stats, cosine, sine,
        scratch=[
            shape((WIDE, 1024)), shape((1024, 1024)), shape((1024, 1024)),
            shape((WIDE, 1024), F32), shape((1024, WIDE), F32), shape((1024, WIDE), F32),
        ],
        flops=8_000_000_000, name="attend_back",
    )
    (small_grads,) = call(
        small_grads_body, [shape((8, 40, 64), F32)], info, sums_attn, sums_one, sums_two, up_sums,
        name="small_grads",
    )
    (w_sent,) = call(
        attn_grad_body, [shape((8, 96, 640))], info, tokens_here, d_proj, small_grads,
        flops=1_200_000_000, name="attn_grad",
    )
    even, odd_sent = call(
        hidden_grad_body, [shape((512, 768), F32), shape((512, 768))], info, d_proj, weight_here,
        flops=1_200_000_000, name="hidden_grad",
    )
    w_came = lax.all_to_all(w_sent, "seq", 0, 0, tiled=True)
    mx, my, z_came, odd_sent, _ = fence(mx, my, z_came, odd_sent, w_sent)

    jx, jy, first, b1, b2, b3 = call(
        first_sums_body,
        [shape((288, 768))] * 2 + [shape((96, 768), F32)] + [shape((96, 768))] * 3,
        info, jx, my, jy, mx, g_down, scratch=[shape((384, 768), F32)], name="first_sums",
        alone=True,
    )
    jx, jy = swap_seq(jx, 2), swap_seq(jy, 4)
    b1, b2, b3 = [swap_batch(b, k) for k, b in ((1, b1), (2, b2), (3, b3))]
    own, half_first, s2, s4, s6 = call(
        second_sums_body,
        [shape((128, 768), F32), shape((48, 768), F32)] + [shape((176, 768))] * 3,
        info, even, swap_seq(odd_sent, 1), z0, *z_came, name="second_sums", alone=True,
    )
    jx, jy, s2, s4, s6, w_came, b1, b2, b3 = fence(jx, jy, s2, s4, s6, w_came, b1, b2, b3)

    last_first, *last_sends = call(
        last_blocks_body, [shape((152, 768), F32)] + [shape((152, 768))] * 3,
        info, j0, jx, jy, w_came,
        scratch=[shape((288, 768), F32), shape((4, 96, 640), F32), shape((4, 1, 384), F32)],
        name="last_blocks", alone=True,
    )
    last_came = [swap_batch(part, k) for k, part in zip((1, 2, 3), last_sends)]
    s2, s4, s6 = swap_seq(s2, 2), swap_seq(s4, 4), swap_seq(s6, 6)
    (grad_down_weight,) = call(
        sum_four_body, [shape((96, 768), F32)], info, first, b1, b2, b3, name="down_end"
    )
    up_half, grad_proj_weight, grad_attn_weight, d_small = call(
        last_sum_body,
        [shape((48, 768), F32), shape((24, 768), F32), shape((24, 2304), F32), shape((1, 384), F32)],
        info, last_first, *last_came, name="last_sum",
    )
    up_own, up_sent, grad_hidden = call(
        end_sum_body,
        [shape((24, 1536), F32), shape((24, 1536)), shape((2, 128, 768), F32)],
        info, up_half, half_first, d_resid_one, own, s2, s4, s6, name="end_sum",
    )
    (grad_up_weight,) = call(
        up_end_body, [shape((24, 3072), F32)], info, up_own, swap_seq(up_sent, 1), name="up_end"
    )

    d_small = d_small[0]
    d_vectors = [d_small[72 + 24 * i : 96 + 24 * i] for i in range(6)]
    return (
        layer_out,
        grad_hidden,
        grad_attn_weight,
        d_small[:48],
        d_small[48:72],
        grad_proj_weight,
        d_vectors[0],
        d_vectors[1],
        d_vectors[2],
        grad_up_weight,
        d_small[216:312],
        grad_down_weight,
        d_vectors[3],
        d_vectors[4],
        d_vectors[5],
    )


def solution(mesh):
    in_specs = (
        P("batch", "seq", None),
        P("batch"),
        P(("seq", "batch"), None),
        P(("seq", "batch")),
        P(("seq", "batch"), None),
        P(("seq", "batch")),
        P(("seq", "batch")),
        P(("seq", "batch")),
        P(("seq", "batch"), None),
        P(("seq", "batch")),
        P(("seq", "batch"), None),
        P(("seq", "batch")),
        P(("seq", "batch")),
        P(("seq", "batch")),
        P("batch", "seq", None),
    )
    out_specs = (
        P("batch", "seq", None),
        P("batch", "seq", None),
        P(("seq", "batch"), None),
        P(("seq", "batch")),
        P(("seq", "batch")),
        P(("seq", "batch"), None),
        P(("seq", "batch")),
        P(("seq", "batch")),
        P(("seq", "batch")),
        P(("seq", "batch"), None),
        P(("seq", "batch")),
        P(("seq", "batch"), None),
        P(("seq", "batch")),
        P(("seq", "batch")),
        P(("seq", "batch")),
    )
    fits = mesh.shape["seq"] == SEQ_SIDE and mesh.shape["batch"] == BATCH_SIDE
    return jax.shard_map(
        split_layer if fits else on_device, mesh=mesh, in_specs=in_specs, out_specs=out_specs, check_vma=False
    )
```

```python
import math

import jax
import jax.numpy as jnp
import numpy as np
from jax import lax
from jax.experimental import pallas as pl
from jax.experimental.pallas import tpu as pltpu
from jax.sharding import PartitionSpec as P

HEADS = 12
HEAD_DIM = 64


EPSILON = 1e-12
NEG_BIG = -1e30


def passed_along(value, axis, steps):
    count = lax.axis_size(axis)
    pairs = [(source, (source + steps) % count) for source in range(count)]
    return lax.ppermute(value, axis, pairs)


def rotate(vectors, positions):
    half_dim = vectors.shape[-1] // 2
    frequency = 10000.0 ** (-2.0 * jnp.arange(half_dim, dtype=jnp.float32) / vectors.shape[-1])
    angles = positions[:, None] * frequency[None, :]
    cosine = jnp.cos(angles)[:, None, :]
    sine_part = jnp.sin(angles)[:, None, :]
    split_pairs = vectors.reshape(vectors.shape[:-1] + (half_dim, 2))
    even_part = split_pairs[..., 0]
    odd_part = split_pairs[..., 1]
    turned = jnp.stack(
        [even_part * cosine - odd_part * sine_part, odd_part * cosine + even_part * sine_part],
        axis=-1,
    )
    return turned.reshape(vectors.shape)


def layer_norm(residual, scale_gain, shift_bias):
    row_mean = jnp.mean(residual, axis=-1, keepdims=True)
    centered = residual - row_mean
    variance = jnp.mean(centered * centered, axis=-1, keepdims=True)
    return centered * lax.rsqrt(variance + EPSILON) * scale_gain + shift_bias


def gelu_exact(upward):
    return jax.nn.gelu(upward, approximate=False)


def run_blocks(step_fn, carry_now, key_piece, first_row, block_keys):
    row_count = key_piece.shape[1]
    width_now = block_keys if row_count % block_keys == 0 else row_count

    def one_turn(index, carry_in):
        begin_at = index * width_now
        sub_piece = lax.dynamic_slice_in_dim(key_piece, begin_at, width_now, 1)
        return step_fn(carry_in, sub_piece, first_row + begin_at)

    return lax.fori_loop(0, row_count // width_now, one_turn, carry_now)


def on_device(
    hidden_in,
    lengths,
    attn_weight,
    attn_bias,
    proj_weight,
    proj_bias,
    first_gain,
    first_shift,
    up_weight,
    up_bias,
    down_weight,
    down_bias,
    second_gain,
    second_shift,
    grad_out,
):
    seq_count, span_rows, model_width = hidden_in.shape
    token_count = seq_count * span_rows
    seq_devices = lax.axis_size("seq")
    my_index = lax.axis_index("seq")
    block_keys = max(span_rows, 512)
    score_scale = HEAD_DIM ** (-0.5)
    offset = my_index * span_rows
    row_index = offset + jnp.arange(span_rows, dtype=jnp.int32)
    positions = row_index.astype(jnp.float32)
    attn_full, attn_bias_full, proj_full, proj_bias_full, gain_one, shift_one = (
        lax.all_gather(attn_weight, ("seq", "batch"), axis=0, tiled=True),
        lax.all_gather(attn_bias, ("seq", "batch"), axis=0, tiled=True),
        lax.all_gather(proj_weight, ("seq", "batch"), axis=0, tiled=True),
        lax.all_gather(proj_bias, ("seq", "batch"), axis=0, tiled=True),
        lax.all_gather(first_gain, ("seq", "batch"), axis=0, tiled=True),
        lax.all_gather(first_shift, ("seq", "batch"), axis=0, tiled=True),
    )
    up_full, up_bias_full, down_full, down_bias_full, gain_two, shift_two = (
        lax.all_gather(up_weight, ("seq", "batch"), axis=0, tiled=True),
        lax.all_gather(up_bias, ("seq", "batch"), axis=0, tiled=True),
        lax.all_gather(down_weight, ("seq", "batch"), axis=0, tiled=True),
        lax.all_gather(down_bias, ("seq", "batch"), axis=0, tiled=True),
        lax.all_gather(second_gain, ("seq", "batch"), axis=0, tiled=True),
        lax.all_gather(second_shift, ("seq", "batch"), axis=0, tiled=True),
    )
    tokens_flat = hidden_in.reshape(token_count, model_width)
    projected = jnp.dot(
        tokens_flat, attn_full, preferred_element_type=jnp.float32
    ) + attn_bias_full.astype(jnp.float32)
    projected = projected.reshape(seq_count, span_rows, 3, HEADS, HEAD_DIM)
    queries = rotate(projected[:, :, 0], positions).astype(jnp.bfloat16)
    keys_low = rotate(projected[:, :, 1], positions).astype(jnp.bfloat16)
    values_low = projected[:, :, 2].astype(jnp.bfloat16)
    key_values = jnp.concatenate(
        [
            keys_low.reshape(seq_count, span_rows, model_width),
            values_low.reshape(seq_count, span_rows, model_width),
        ],
        axis=-1,
    )

    def key_mask(first_row, row_count):
        key_rows = first_row + jnp.arange(row_count, dtype=jnp.int32)
        return (key_rows[None, :] < lengths[:, None])[:, None, None, :]

    def split_pairs(key_piece):
        row_count = key_piece.shape[1]
        keys_part = key_piece[:, :, :model_width].reshape(seq_count, row_count, HEADS, HEAD_DIM)
        values_part = key_piece[:, :, model_width:].reshape(seq_count, row_count, HEADS, HEAD_DIM)
        return (keys_part, values_part)

    def attend_step(carry_in, key_piece, first_row):
        row_max, row_sum, accum = carry_in
        keys_part, values_part = split_pairs(key_piece)
        masked = key_mask(first_row, key_piece.shape[1])
        scores = score_scale * jnp.einsum(
            "sqhd,skhd->shqk", queries, keys_part, preferred_element_type=jnp.float32
        )
        scores = jnp.where(masked, scores, NEG_BIG)
        new_max = jnp.maximum(row_max, jnp.max(scores, axis=-1))
        weights = jnp.where(masked, jnp.exp(scores - new_max[..., None]), 0.0)
        factor = jnp.exp(row_max - new_max)
        row_sum = row_sum * factor + jnp.sum(weights, axis=-1)
        accum = accum * jnp.transpose(factor, (0, 2, 1))[..., None] + jnp.einsum(
            "shqk,skhd->sqhd",
            weights.astype(jnp.bfloat16),
            values_part,
            preferred_element_type=jnp.float32,
        )
        return (new_max, row_sum, accum)

    start_state = (
        jnp.full((seq_count, HEADS, span_rows), NEG_BIG, jnp.float32),
        jnp.zeros((seq_count, HEADS, span_rows), jnp.float32),
        jnp.zeros((seq_count, span_rows, HEADS, HEAD_DIM), jnp.float32),
    )
    row_max, row_sum, accum = run_blocks(
        attend_step,
        start_state,
        lax.all_gather(key_values, "seq", axis=1, tiled=True),
        jnp.int32(0),
        block_keys,
    )
    sum_view = jnp.transpose(row_sum, (0, 2, 1))[..., None]
    attended = accum / sum_view
    attn_rows = attended.reshape(token_count, model_width).astype(jnp.bfloat16)
    mixed = jnp.dot(
        attn_rows, proj_full, preferred_element_type=jnp.float32
    ) + proj_bias_full.astype(jnp.float32)
    normed, norm_back_one = jax.vjp(
        layer_norm,
        tokens_flat.astype(jnp.float32) + mixed,
        gain_one.astype(jnp.float32),
        shift_one.astype(jnp.float32),
    )
    normed_low = normed.astype(jnp.bfloat16)
    upward = jnp.dot(normed_low, up_full, preferred_element_type=jnp.float32) + up_bias_full.astype(
        jnp.float32
    )
    active, gelu_back = jax.vjp(gelu_exact, upward)
    active_low = active.astype(jnp.bfloat16)
    downward = jnp.dot(
        active_low, down_full, preferred_element_type=jnp.float32
    ) + down_bias_full.astype(jnp.float32)
    output_rows, norm_back_two = jax.vjp(
        layer_norm, normed + downward, gain_two.astype(jnp.float32), shift_two.astype(jnp.float32)
    )
    layer_out = output_rows.reshape(seq_count, span_rows, model_width).astype(jnp.bfloat16)
    row_valid = (row_index[None, :] < lengths[:, None]).astype(jnp.float32)
    cotangent = (grad_out.astype(jnp.float32) * row_valid[:, :, None]).reshape(
        token_count, model_width
    )
    d_resid_two, d_gain_two, d_shift_two = norm_back_two(cotangent)
    d_down = d_resid_two.astype(jnp.bfloat16)
    d_down_bias = jnp.sum(d_down.astype(jnp.float32), axis=0)
    d_down_weight = jnp.einsum("tf,td->fd", active_low, d_down, preferred_element_type=jnp.float32)
    d_active = jnp.dot(d_down, down_full.T, preferred_element_type=jnp.float32)
    (d_upward,) = gelu_back(d_active)
    d_up = d_upward.astype(jnp.bfloat16)
    d_up_bias = jnp.sum(d_up.astype(jnp.float32), axis=0)
    d_up_weight = jnp.einsum("td,tf->df", normed_low, d_up, preferred_element_type=jnp.float32)
    d_normed = d_resid_two + jnp.dot(d_up, up_full.T, preferred_element_type=jnp.float32)
    ffn_parts = (
        lax.psum_scatter(d_up_weight, ("seq", "batch"), scatter_dimension=0, tiled=True),
        lax.psum_scatter(d_up_bias, ("seq", "batch"), scatter_dimension=0, tiled=True),
        lax.psum_scatter(d_down_weight, ("seq", "batch"), scatter_dimension=0, tiled=True),
        lax.psum_scatter(d_down_bias, ("seq", "batch"), scatter_dimension=0, tiled=True),
        lax.psum_scatter(d_gain_two, ("seq", "batch"), scatter_dimension=0, tiled=True),
        lax.psum_scatter(d_shift_two, ("seq", "batch"), scatter_dimension=0, tiled=True),
    )
    d_resid_one, d_gain_one, d_shift_one = norm_back_one(d_normed)
    d_mixed = d_resid_one.astype(jnp.bfloat16)
    d_proj_bias = jnp.sum(d_mixed.astype(jnp.float32), axis=0)
    d_proj_weight = jnp.einsum("td,te->de", attn_rows, d_mixed, preferred_element_type=jnp.float32)
    d_attended = jnp.dot(d_mixed, proj_full.T, preferred_element_type=jnp.float32).astype(
        jnp.bfloat16
    )
    d_attended = d_attended.astype(jnp.float32).reshape(seq_count, span_rows, HEADS, HEAD_DIM)
    delta = jnp.transpose(jnp.sum(d_attended * attended, axis=-1), (0, 2, 1))
    delta_scaled = delta / row_sum
    guide = (d_attended / sum_view).astype(jnp.bfloat16)

    def back_step(carry_in, key_piece, first_row):
        d_queries, buffer = carry_in
        keys_part, values_part = split_pairs(key_piece)
        row_count = key_piece.shape[1]
        masked = key_mask(first_row, row_count)
        scores = score_scale * jnp.einsum(
            "sqhd,skhd->shqk", queries, keys_part, preferred_element_type=jnp.float32
        )
        scores = jnp.where(masked, scores, NEG_BIG)
        weights = jnp.where(masked, jnp.exp(scores - row_max[..., None]), 0.0)
        d_weights = jnp.einsum(
            "sqhd,skhd->shqk", guide, values_part, preferred_element_type=jnp.float32
        )
        d_scores = (weights * (d_weights - delta_scaled[..., None])).astype(jnp.bfloat16)
        d_queries = d_queries + score_scale * jnp.einsum(
            "shqk,skhd->sqhd", d_scores, keys_part, preferred_element_type=jnp.float32
        )
        d_keys = score_scale * jnp.einsum(
            "shqk,sqhd->skhd", d_scores, queries, preferred_element_type=jnp.float32
        )
        d_values = jnp.einsum(
            "shqk,sqhd->skhd",
            weights.astype(jnp.bfloat16),
            guide,
            preferred_element_type=jnp.float32,
        )
        new_terms = jnp.concatenate(
            [
                d_keys.reshape(seq_count, row_count, model_width),
                d_values.reshape(seq_count, row_count, model_width),
            ],
            axis=-1,
        )
        current = buffer
        buffer = current + new_terms
        return (d_queries, buffer)

    zero_queries = jnp.zeros((seq_count, span_rows, HEADS, HEAD_DIM), jnp.float32)

    def cycle_turn(turn, carry_in):
        d_queries, pair_piece, grad_piece = carry_in
        owner = (my_index - turn) % seq_devices
        base_row = owner * span_rows

        def owner_step(inner, key_piece, first_row):
            return back_step(inner, key_piece, first_row)

        d_queries, grad_piece = run_blocks(
            owner_step, (d_queries, grad_piece), pair_piece, base_row, block_keys
        )
        grad_piece = passed_along(grad_piece.astype(jnp.bfloat16), "seq", 1).astype(
            grad_piece.dtype
        )
        pair_piece = passed_along(pair_piece, "seq", 1)
        return (d_queries, pair_piece, grad_piece)

    start_cycle = (
        zero_queries,
        key_values,
        jnp.zeros((seq_count, span_rows, 2 * model_width), jnp.float32),
    )
    d_queries, pair_spent, d_pairs = lax.fori_loop(0, seq_devices, cycle_turn, start_cycle)
    d_keys_own = d_pairs[:, :, :model_width].reshape(seq_count, span_rows, HEADS, HEAD_DIM)
    d_values_own = d_pairs[:, :, model_width:].reshape(seq_count, span_rows, HEADS, HEAD_DIM)
    d_projected = jnp.stack(
        [rotate(d_queries, -positions), rotate(d_keys_own, -positions), d_values_own], axis=2
    )
    d_projected = d_projected.reshape(token_count, 3 * model_width).astype(jnp.bfloat16)
    d_attn_bias = jnp.sum(d_projected.astype(jnp.float32), axis=0)
    d_pair_bias = d_attn_bias[: 2 * model_width]
    d_value_bias = d_attn_bias[2 * model_width :]
    d_attn_weight = jnp.einsum(
        "td,tf->df", tokens_flat, d_projected, preferred_element_type=jnp.float32
    )
    grad_hidden = d_resid_one + jnp.dot(
        d_projected, attn_full.T, preferred_element_type=jnp.float32
    )
    attn_parts = (
        lax.psum_scatter(d_attn_weight, ("seq", "batch"), scatter_dimension=0, tiled=True),
        lax.psum_scatter(d_pair_bias, ("seq", "batch"), scatter_dimension=0, tiled=True),
        lax.psum_scatter(d_value_bias, ("seq", "batch"), scatter_dimension=0, tiled=True),
        lax.psum_scatter(d_proj_weight, ("seq", "batch"), scatter_dimension=0, tiled=True),
        lax.psum_scatter(d_proj_bias, ("seq", "batch"), scatter_dimension=0, tiled=True),
        lax.psum_scatter(d_gain_one, ("seq", "batch"), scatter_dimension=0, tiled=True),
        lax.psum_scatter(d_shift_one, ("seq", "batch"), scatter_dimension=0, tiled=True),
    )
    return (
        layer_out,
        grad_hidden.reshape(seq_count, span_rows, model_width),
        attn_parts[0],
        attn_parts[1],
        attn_parts[2],
        attn_parts[3],
        attn_parts[4],
        attn_parts[5],
        attn_parts[6],
        ffn_parts[0],
        ffn_parts[1],
        ffn_parts[2],
        ffn_parts[3],
        ffn_parts[4],
        ffn_parts[5],
    )


SEQ_SIDE = 8
BATCH_SIDE = 4
GROUP = 192
WIDE = 256
HERE = 3
EVEN = (0, 2, 4, 6)
ODD = (1, 3, 5, 7)
CORE, X, Y, Z, PLACE, LEN_MINE, LEN_OTHER = range(7)
F32, BF16 = jnp.float32, jnp.bfloat16
NN = (((1,), (0,)), ((), ()))
NT = (((1,), (1,)), ((), ()))
TN = (((0,), (0,)), ((), ()))


def swap_seq(value, mask):
    return lax.ppermute(value, "seq", [(i, i ^ mask) for i in range(SEQ_SIDE)])


def swap_batch(value, mask):
    return lax.ppermute(value, "batch", [(i, i ^ mask) for i in range(BATCH_SIDE)])


def after(value, *done):
    return lax.optimization_barrier((value,) + done)[0]


def fence(*values):
    return lax.optimization_barrier(values)


def shape(dims, dtype=BF16):
    return jax.ShapeDtypeStruct(dims, dtype)


def call(body, outs, info, *args, scratch=(), flops=0, name=None, alone=False):
    moved = sum(a.size * a.dtype.itemsize for a in args)
    moved += sum(math.prod(o.shape) * o.dtype.itemsize for o in outs)
    held = sum(math.prod(m.shape) * m.dtype.itemsize for m in scratch)
    return pl.pallas_call(
        lambda lengths, *refs: body(Spot(lengths), *refs),
        out_shape=outs,
        in_specs=[pl.BlockSpec(memory_space=pltpu.SMEM)]
        + [pl.BlockSpec(memory_space=pltpu.VMEM)] * len(args),
        out_specs=[pl.BlockSpec(memory_space=pltpu.VMEM)] * len(outs),
        scratch_shapes=[pltpu.VMEM(m.shape, m.dtype) for m in scratch],
        compiler_params=pltpu.CompilerParams(
            vmem_limit_bytes=60 << 20 if alone else min(56 << 20, moved + held + (10 << 20))
        ),
        cost_estimate=pl.CostEstimate(flops=1, bytes_accessed=1, transcendentals=0),
        name=name,
    )(info, *args)


def dot(left, right, dims=NN):
    return lax.dot_general(left, right, dims, preferred_element_type=F32)


class Spot:
    def __init__(self, lengths):
        self.lengths = lengths

    def __getitem__(self, what):
        place = lax.axis_index("seq")
        if what == Z:
            return lax.axis_index("batch")
        if what == LEN_MINE:
            return self.lengths[place >> 2]
        if what == LEN_OTHER:
            return self.lengths[1 - (place >> 2)]
        return {CORE: place & 1, X: (place >> 1) & 1, Y: place >> 2, PLACE: place}[what]


def chips(info):
    x, y = info[X], info[Y]
    return ((y, x), (y, 1 - x), (1 - y, x), (1 - y, 1 - x))


def lanes(start, size):
    return pl.ds(pl.multiple_of(start, 128), size)


def rows(start, size, unit=16):
    return pl.ds(pl.multiple_of(start, unit), size)


def rotary_tables(length):
    entry = np.arange(WIDE)
    frequency = (10000.0 ** (-2.0 * ((entry % HEAD_DIM) // 2) / HEAD_DIM)).astype(np.float32)
    angles = np.arange(length, dtype=np.float32)[:, None] * frequency[None, :]
    used = entry < GROUP
    sign = np.where(entry % 2 == 0, -1.0, 1.0)
    cosine = np.cos(angles.astype(np.float64)) * used
    sine = np.sin(angles.astype(np.float64)) * (used * sign)
    return cosine.astype(np.float32), sine.astype(np.float32)


def place_tables(info, cosine, sine, cosine_held, sine_held):
    for i, k in enumerate(EVEN + ODD):
        here = rows((info[PLACE] ^ k) * 128, 128)
        cosine_held[128 * i : 128 * (i + 1)] = cosine[here, :]
        sine_held[128 * i : 128 * (i + 1)] = sine[here, :]


def prepare_body(
    info, hidden, attn, up, proj, down, v0, v1, v2, v3, v4, v5, v6, v7,
    mine, other, joined, early, wide,
):
    y = info[Y]
    mine[...] = hidden[y]
    other[...] = hidden[1 - y]
    late = down[48:96].astype(F32)
    early[...] = down[:48]
    parts = [v[...].astype(F32) for v in (v0, v1, v2, v3, v4, v5, v6, v7)]
    row = jnp.concatenate(parts + [jnp.zeros((1, 8), F32)], axis=1)
    small = jnp.concatenate(
        [row[:, 64 * i : 64 * (i + 1)] for i in range(5)] + [jnp.zeros((19, 64), F32)], axis=0
    )
    small = jnp.concatenate([small, jnp.zeros((24, 64), F32)], axis=1).astype(BF16)
    joined[:, :3072] = up[...]
    joined[:, 3072:3840] = proj[...]
    joined[:, 3840:4608] = late[:24].astype(BF16)
    joined[:, 4608:5376] = late[24:].astype(BF16)
    for k in range(4):
        wide[k, :, :2304] = attn[...]
        wide[k, :, 2304:] = small


def by_batch(info, pieces):
    z = info[Z]
    values = [p[...].astype(F32) for p in pieces]
    ordered = []
    for zz in range(4):
        k = zz ^ z
        low = jnp.where(k == 0, values[0], values[1])
        high = jnp.where(k == 2, values[2], values[3])
        ordered.append(jnp.where(k < 2, low, high))
    return ordered


def attn_column_body(info, pieces, out):
    column = jnp.concatenate([pieces[zz].astype(F32) for zz in range(4)], axis=0)
    small = [column[24 * zz + i : 24 * zz + i + 1, 2304:2368] for i in range(5) for zz in range(4)]
    small = jnp.concatenate(small + [jnp.zeros((76, 64), F32)], axis=0)
    for g in range(4):
        part = jnp.concatenate(
            [column[:, 768 * i + GROUP * g : 768 * i + GROUP * (g + 1)] for i in range(3)] + [small],
            axis=1,
        ).astype(BF16)
        out[g] = part
        out[4 + g] = part


def up_column_body(info, p0, p1, p2, p3, keep, sent, rest, held):
    core = info[CORE]
    pieces = by_batch(info, (p0, p1, p2, p3))
    column = jnp.concatenate(pieces, axis=0).astype(BF16)
    held[...] = column[:, :3072]
    rest[:96] = column[:, 3072:3840]
    for zz in range(4):
        rest[96 + 48 * zz : 144 + 48 * zz] = jnp.concatenate(
            [pieces[zz][:, 3840:4608], pieces[zz][:, 4608:]], axis=0
        ).astype(BF16)
    for which, out in ((core, keep), (1 - core, sent)):
        for q in range(4):
            out[96 * (q // 2) : 96 * (q // 2 + 1), 384 * (q % 2) : 384 * (q % 2 + 1)] = held[
                :, lanes(768 * q + 384 * which, 384)
            ]


def up_join_body(info, keep, came, rest, out):
    out[0:96] = keep[:96]
    out[96:192] = came[:96]
    out[192:288] = keep[96:]
    out[288:384] = came[96:]
    out[384:672] = rest[...]


def early_body(info, p0, px, py, pd, out):
    for j, p in enumerate((p0, px, py, pd)):
        out[48 * j : 48 * (j + 1)] = p[...]


def attend_body(
    info, mine, r2, r4, r6, odd, given, cosine_all, sine_all,
    x_out, weight, qt_out, k_out, v_out, att_out, stats, even_low, odd_low, cosine, sine,
):
    place_tables(info, cosine_all, sine_all, cosine, sine)
    weight[:, :, GROUP:] = jnp.zeros((3, 768, WIDE - GROUP), BF16)
    for i in range(3):
        for s in range(8):
            weight[i, 96 * s : 96 * (s + 1), :GROUP] = given[s, :, GROUP * i : GROUP * (i + 1)]
    small = jnp.concatenate(
        [
            jnp.concatenate([given[s, 0:16, 576:640][4 * i : 4 * (i + 1)] for s in range(8)], axis=0)
            for i in range(2)
        ],
        axis=1,
    ).astype(F32)
    group = info[PLACE] & 3

    def bias_row(i):
        entry = 768 * i + GROUP * group + lax.broadcasted_iota(jnp.int32, (128, WIDE), 1)
        source = lax.broadcasted_iota(jnp.int32, (128, WIDE), 0)
        picked = dot(small.astype(BF16), jnp.where(source == entry % 72, 1.0, 0.0).astype(BF16))
        picked = jnp.where(source[:32] == entry[:32] // 72, picked, 0.0)
        used = lax.broadcasted_iota(jnp.int32, (1, WIDE), 1) < GROUP
        return jnp.where(used, column_sum(picked), 0.0)

    x_out[0:128] = mine[...]
    x_out[128:256] = r2[...]
    x_out[256:384] = r4[...]
    x_out[384:512] = r6[...]
    x_out[512:1024] = odd[...]
    tokens = x_out[...]
    lane = lax.broadcasted_iota(jnp.int32, (1024, WIDE), 1)
    is_even = lane % 2 == 0

    def part(i):
        return dot(tokens, weight[i]) + bias_row(i)

    def turned(value):
        left = pltpu.roll(value, WIDE - 1, 1)
        right = pltpu.roll(value, 1, 1)
        return value * cosine[...] + jnp.where(is_even, left, right) * sine[...]

    query = turned(part(0)).astype(BF16).astype(F32) * (HEAD_DIM**-0.5)
    query = jnp.where(lane == GROUP, 1.0, query).T.astype(BF16)
    qt_out[...] = query
    index = lax.broadcasted_iota(jnp.int32, (1024, WIDE), 0)
    block = index >> 7
    owner = info[PLACE] ^ (((block & 3) << 1) | (block >> 2))
    valid = owner * 128 + (index & 127) < info[LEN_MINE]
    padding = jnp.where(valid, 0.0, NEG_BIG)
    key = jnp.where(lane == GROUP, padding, turned(part(1))).astype(BF16)
    k_out[...] = key
    value = part(2).astype(BF16)
    v_out[...] = value
    value_t = value.astype(F32).T
    ones = jnp.ones((16, 1024), BF16)
    row = lax.broadcasted_iota(jnp.int32, (WIDE, WIDE), 0)
    for h in range(HERE):
        here = (row // HEAD_DIM == h) | (row == GROUP)
        value_h = jnp.concatenate(
            [value_t[HEAD_DIM * h : HEAD_DIM * (h + 1)].astype(BF16), ones], axis=0
        )
        for b in range(4):
            block = qt_out[:, WIDE * b : WIDE * (b + 1)].astype(F32)
            scores = dot(key, jnp.where(here, block, 0.0).astype(BF16))
            top = jnp.max(scores, axis=0, keepdims=True)
            weights = jnp.exp(scores - top).astype(BF16)
            summed = dot(value_h, weights)
            total = summed[HEAD_DIM : HEAD_DIM + 1]
            att_out[HEAD_DIM * h : HEAD_DIM * (h + 1), WIDE * b : WIDE * (b + 1)] = (
                summed[:HEAD_DIM] / total
            )
            stats[h : h + 1, WIDE * b : WIDE * (b + 1)] = top
            stats[4 + h : 5 + h, WIDE * b : WIDE * (b + 1)] = total
    low = att_out[...].T.astype(BF16)
    for i in range(4):
        even_low[i] = low[128 * i : 128 * (i + 1)]
        odd_low[i] = low[512 + 128 * i : 640 + 128 * i]


def small_body(info, given, vectors, up_bias):
    core = info[CORE]
    values = jnp.concatenate(
        [
            jnp.concatenate([given[s, 0:32, 576:640][4 * i : 4 * (i + 1)] for s in range(8)], axis=0)
            for i in range(5)
        ],
        axis=1,
    ).astype(F32)
    entry = lax.broadcasted_iota(jnp.int32, (32, 768), 1)
    source = lax.broadcasted_iota(jnp.int32, (32, 768), 0)
    spread = jnp.where(source == entry % 24, 1.0, 0.0).astype(BF16)
    here = source == entry // 24
    padding = jnp.zeros((32, 8), F32)
    for i in range(6):
        part = jnp.concatenate([values[:, 72 + 24 * i : 96 + 24 * i], padding], axis=1)
        vectors[i : i + 1] = column_sum(jnp.where(here, dot(part.astype(BF16), spread), 0.0))
    entry = lax.broadcasted_iota(jnp.int32, (128, 1536), 1)
    entry = entry // 384 * 768 + core * 384 + entry % 384
    source = lax.broadcasted_iota(jnp.int32, (128, 1536), 0)
    spread = jnp.where(source == entry % 96, 1.0, 0.0).astype(BF16)
    part = jnp.concatenate([values[:, 216:312], jnp.zeros((32, 32), F32)], axis=1)
    part = dot(part.astype(BF16), spread)
    up_bias[...] = column_sum(jnp.where(source[:32] == entry[:32] // 96, part, 0.0))


def pair_body(info, own, came, p0, p1, p2, p3):
    for i, out in enumerate((p0, p1, p2, p3)):
        out[...] = jnp.concatenate(
            [own[i].astype(F32), came[i].astype(F32)], axis=1
        ).astype(BF16)


def proj_rows_body(info, d0, dx, dy, dd, out):
    for i, d in enumerate((d0, dx, dy, dd)):
        out[i] = d[384:480]


def attn_order(info):
    x, core = info[X], info[CORE]
    return ((x, core), (x, 1 - core), (1 - x, core), (1 - x, 1 - core))


def mix_body(
    info, p0, r2, r4, r6, d0, dx, dy, dd, proj_came, mine, other, vectors,
    normed_out, low_out, hat_out, rstd_out, rows_out, proj, held,
):
    core = info[CORE]
    for j, (yy, xx) in enumerate(chips(info)):
        held[rows((yy * 4 + xx * 2 + core) * 96, 96), :] = (d0, dx, dy, dd)[j][384:480]
        held[rows((yy * 4 + xx * 2 + 1 - core) * 96, 96), :] = proj_came[j]
    for i, (xx, cc) in enumerate(attn_order(info)):
        proj[GROUP * i : GROUP * (i + 1)] = held[rows((xx * 2 + cc) * GROUP, GROUP), :]
    rows_out[0:128, 0:384] = p0[...]
    rows_out[0:128, 384:768] = r2[...]
    rows_out[128:256, 0:384] = r4[...]
    rows_out[128:256, 384:768] = r6[...]
    tokens = jnp.concatenate([mine[...], other[...]], axis=0).astype(F32)
    resid = tokens + dot(rows_out[...], proj[...]) + vectors[0:1, :]
    centred = resid - jnp.mean(resid, axis=1, keepdims=True)
    rstd = lax.rsqrt(jnp.mean(centred * centred, axis=1, keepdims=True) + EPSILON)
    hat = centred * rstd
    normed = hat * vectors[1:2, :] + vectors[2:3, :]
    hat_out[...] = hat
    rstd_out[...] = jnp.broadcast_to(rstd, (256, 128))
    normed_out[...] = normed
    low_out[...] = normed.astype(BF16)


def whole_up(info, blocks, held):
    core = info[CORE]
    for block, (yy, xx) in zip(blocks, chips(info)):
        for half in range(2):
            span = slice(768 * half, 768 * (half + 1))
            for i, cc in enumerate((core, 1 - core)):
                held[rows((yy * 4 + xx * 2 + cc) * 96, 96), span] = block[
                    192 * half + 96 * i : 192 * half + 96 * (i + 1)
                ]


def whole_down(info, blocks, early, held):
    z = info[Z]
    for j, (yy, xx) in enumerate(chips(info)):
        base = (yy * 2 + xx) * 384
        for zz in range(4):
            held[rows(base + 96 * zz + 48, 48), :] = blocks[j][480 + 48 * zz : 528 + 48 * zz]
        for k, piece in enumerate(early):
            held[rows(base + 96 * (z ^ k), 48), :] = piece[48 * j : 48 * (j + 1)]


def gelu_parts(upward):
    gauss = jnp.exp(-0.5 * upward * upward)
    t = 1.0 / (1.0 + (0.3275911 * 2.0**-0.5) * jnp.abs(upward))
    poly = t * (
        0.127414796
        + t * (-0.142248368 + t * (0.7107068705 + t * (-0.7265760135 + t * 0.5307027145)))
    )
    tail = poly * gauss
    below = jnp.where(upward < 0, tail, 1.0 - tail)
    return upward * below, below + upward * gauss * 0.3989422804014327


def up_body(
    info, low_mine, low_other, u0, ux, uy, ud, d0, d1, d2, d3, bias,
    part_mine, part_other, active_out, slope_out, up_held, down_held,
):
    whole_up(info, (u0, ux, uy, ud), up_held)
    whole_down(info, (u0, ux, uy, ud), (d0, d1, d2, d3), down_held)
    for i, low in enumerate((low_mine, low_other)):
        upward = dot(low[...], up_held[...]) + bias[...]
        active, slope = gelu_parts(upward)
        active = active.astype(BF16)
        active_out[256 * i : 256 * (i + 1)] = active
        slope_out[256 * i : 256 * (i + 1)] = slope.astype(BF16)
        part = dot(active, down_held[...])
        if i == 0:
            part_mine[...] = part
        else:
            part_other[...] = part.astype(BF16)


def back_norm(d_hat, hat, rstd):
    return rstd * (
        d_hat
        - jnp.mean(d_hat, axis=1, keepdims=True)
        - hat * jnp.mean(d_hat * hat, axis=1, keepdims=True)
    )


def column_sum(value):
    return jnp.sum(value, axis=0, keepdims=True)


def norm_two_body(
    info, part_mine, came, normed, vectors, grad, out, d_resid_out, d_low, sums,
):
    y = info[Y]
    resid = normed[...] + (part_mine[...] + came[...].astype(F32) + vectors[3:4, :])
    centred = resid - jnp.mean(resid, axis=1, keepdims=True)
    rstd = lax.rsqrt(jnp.mean(centred * centred, axis=1, keepdims=True) + EPSILON)
    hat = centred * rstd
    result = (hat * vectors[4:5, :] + vectors[5:6, :]).astype(BF16)
    out[y] = result[:128]
    out[1 - y] = result[128:]
    position = info[PLACE] * 128 + lax.broadcasted_iota(jnp.int32, (128, 768), 0)
    first = jnp.where(position < info[LEN_MINE], grad[y].astype(F32), 0.0)
    second = jnp.where(position < info[LEN_OTHER], grad[1 - y].astype(F32), 0.0)
    cotangent = jnp.concatenate([first, second], axis=0)
    d_resid = back_norm(cotangent * vectors[4:5, :], hat, rstd)
    d_resid_out[...] = d_resid
    low = d_resid.astype(BF16)
    d_low[...] = low
    sums[0:1] = column_sum(low.astype(F32))
    sums[1:2] = column_sum(cotangent * hat)
    sums[2:3] = column_sum(cotangent)


def down_grad_body(info, active, d_mine, d_other, g0, gx, gy, da, db, held):
    d_low = jnp.concatenate([d_mine[...], d_other[...]], axis=0)
    for i in range(4):
        held[384 * i : 384 * (i + 1)] = dot(
            active[:, 384 * i : 384 * (i + 1)], d_low, TN
        ).astype(BF16)
    outs = ((g0,), (gx,), (gy,), (da, db))
    for out, (yy, xx) in zip(outs, chips(info)):
        base = (yy * 2 + xx) * 384
        if len(out) == 1:
            out[0][...] = held[rows(base, 384), :]
        else:
            out[0][...] = held[rows(base, 192), :]
            out[1][...] = held[rows(base + 192, 192), :]


def up_grad_body(
    info, d_mine, d_other, slope, low_mine, low_other, u0, ux, uy, ud, d0, d1, d2, d3,
    part_mine, part_other, g0, gx, gy, gd, z0, z1, z2, z3, sums, up_held, down_held, held,
):
    core = info[CORE]
    whole_up(info, (u0, ux, uy, ud), up_held)
    whole_down(info, (u0, ux, uy, ud), (d0, d1, d2, d3), down_held)
    d_ups = []
    total = jnp.zeros((1, 1536), F32)
    for i, d_low in enumerate((d_mine, d_other)):
        d_active = dot(d_low[...], down_held[...], NT)
        d_up = (slope[256 * i : 256 * (i + 1)].astype(F32) * d_active).astype(BF16)
        total = total + column_sum(d_up.astype(F32))
        d_ups.append(d_up)
        part = dot(d_up, up_held[...], NT)
        if i == 0:
            part_mine[...] = part
        else:
            part_other[...] = part.astype(BF16)
    sums[...] = total
    d_up = jnp.concatenate(d_ups, axis=0)
    low = jnp.concatenate([low_mine[...], low_other[...]], axis=0)
    held[...] = dot(low, d_up, TN)
    z = info[Z]
    for j, (yy, xx) in enumerate(chips(info)):
        for i, cc in enumerate((core, 1 - core)):
            base = (yy * 4 + xx * 2 + cc) * 96
            (g0, gx, gy, gd)[j][96 * i : 96 * (i + 1)] = held[rows(base, 96), :768].astype(BF16)
    for k, out in enumerate((z0, z1, z2, z3)):
        for j, (yy, xx) in enumerate(chips(info)):
            block = [
                held[rows((yy * 4 + xx * 2 + cc) * 96 + (z ^ k) * 24, 24, 8), 768:]
                for cc in (core, 1 - core)
            ]
            out[48 * j : 48 * (j + 1)] = jnp.concatenate(block, axis=0).astype(BF16)


def norm_one_body(
    info, d_resid_two, part_mine, came, hat, rstd, vectors, rows_here, proj,
    d_resid_out, e0, e2, e4, e6, proj_own, proj_sent, sums, held,
):
    core = info[CORE]
    d_normed = d_resid_two[...] + part_mine[...] + came[...].astype(F32)
    sums[0:1] = column_sum(d_normed * hat[...])
    sums[1:2] = column_sum(d_normed)
    d_resid = back_norm(d_normed * vectors[1:2, :], hat[...], rstd[:, 0:1])
    d_resid_out[...] = d_resid
    low = d_resid.astype(BF16)
    sums[2:3] = column_sum(low.astype(F32))
    d_att = dot(low, proj[...], NT).astype(BF16)
    e0[...] = d_att[:128, :384]
    e2[...] = d_att[:128, 384:]
    e4[...] = d_att[128:, :384]
    e6[...] = d_att[128:, 384:]
    d_weight = dot(rows_here[...], low, TN).astype(BF16)
    for i, (xx, cc) in enumerate(attn_order(info)):
        held[rows((xx * 2 + cc) * GROUP, GROUP), :] = d_weight[GROUP * i : GROUP * (i + 1)]
    for j, (yy, xx) in enumerate(chips(info)):
        proj_own[j] = held[rows((yy * 4 + xx * 2 + core) * 96, 96), :]
        proj_sent[j] = held[rows((yy * 4 + xx * 2 + 1 - core) * 96, 96), :]


def split_core_body(info, e0, e2, e4, e6, out):
    for i, e in enumerate((e0, e2, e4, e6)):
        out[128 * i : 128 * (i + 1)] = e[...].astype(F32)[:, GROUP:].astype(BF16)


def attend_back_body(
    info, e0, e2, e4, e6, came, qt, key, value, att, stats, cosine_all, sine_all,
    d_proj, sums, guide, weights_held, d_scores_held, dq_held, dk_held, dv_held, cosine, sine,
):
    place_tables(info, cosine_all, sine_all, cosine, sine)
    d_att = jnp.concatenate(
        [e[...].astype(F32)[:, :GROUP] for e in (e0, e2, e4, e6)] + [came[...].astype(F32)], axis=0
    )
    d_att_t = d_att.T
    product = d_att_t * att[...]
    pieces = []
    deltas = []
    for h in range(HERE):
        here = slice(HEAD_DIM * h, HEAD_DIM * (h + 1))
        total = stats[4 + h : 5 + h, :]
        pieces.append(d_att_t[here] / total)
        deltas.append(column_sum(product[here]) / total)
    pieces.append(jnp.zeros((WIDE - GROUP, 1024), F32))
    guide[...] = jnp.concatenate(pieces, axis=0).astype(BF16)
    key_t = key[...].astype(F32).T
    row = lax.broadcasted_iota(jnp.int32, (WIDE, WIDE), 0)
    dk_held[...] = jnp.zeros((1024, WIDE), F32)
    dv_held[...] = jnp.zeros((1024, WIDE), F32)
    dq_held[GROUP:] = jnp.zeros((WIDE - GROUP, 1024), F32)
    wide_row = lax.broadcasted_iota(jnp.int32, (WIDE, 1024), 0)
    for h in range(HERE):
        mine = row // HEAD_DIM == h
        with_pad = mine | (row == GROUP)
        key_h = key_t[HEAD_DIM * h : HEAD_DIM * (h + 1)].astype(BF16)
        for b in range(4):
            span = slice(WIDE * b, WIDE * (b + 1))
            q_block = jnp.where(with_pad, qt[:, span].astype(F32), 0.0).astype(BF16)
            g_block = jnp.where(mine, guide[:, span].astype(F32), 0.0).astype(BF16)
            scores = dot(key[...], q_block)
            weights = jnp.exp(scores - stats[h : h + 1, span])
            d_weights = dot(value[...], g_block)
            d_scores = (weights * (d_weights - deltas[h][:, span])).astype(BF16)
            weights_held[:, span] = weights.astype(BF16)
            d_scores_held[:, span] = d_scores
            dq_held[HEAD_DIM * h : HEAD_DIM * (h + 1), span] = dot(key_h, d_scores)
        here = wide_row // HEAD_DIM == h
        q_all = jnp.where(here, qt[...].astype(F32), 0.0).astype(BF16)
        g_all = jnp.where(here, guide[...].astype(F32), 0.0).astype(BF16)
        dk_held[...] += dot(d_scores_held[...], q_all, NT)
        dv_held[...] += dot(weights_held[...], g_all, NT)
    lane = lax.broadcasted_iota(jnp.int32, (1024, WIDE), 1)
    is_even = lane % 2 == 0

    def turned_back(value):
        left = pltpu.roll(value, WIDE - 1, 1)
        right = pltpu.roll(value, 1, 1)
        return value * cosine[...] - jnp.where(is_even, left, right) * sine[...]

    d_query = turned_back(dq_held[...].T * (HEAD_DIM**-0.5)).astype(BF16)
    d_key = turned_back(dk_held[...]).astype(BF16)
    d_value = dv_held[...].astype(BF16)
    for i, part in enumerate((d_query, d_key, d_value)):
        d_proj[i] = part
        sums[i : i + 1] = column_sum(part.astype(F32))


def attn_grad_body(info, tokens, d_proj, small, out):
    parts = [dot(tokens[...], d_proj[i], TN)[:, :GROUP] for i in range(3)]
    whole = jnp.concatenate(parts, axis=1)
    for s in range(8):
        beside = jnp.concatenate([small[s], jnp.zeros((56, 64), F32)], axis=0)
        out[s] = jnp.concatenate([whole[96 * s : 96 * (s + 1)], beside], axis=1).astype(BF16)


def sum_four_body(info, first, r1, r2, r3, out):
    out[...] = (
        first[...] + r1[...].astype(F32) + r2[...].astype(F32) + r3[...].astype(F32)
    )


def hidden_grad_body(info, d_proj, weight, even_out, odd_out):
    total = jnp.zeros((1024, 768), F32)
    for i in range(3):
        total = total + dot(d_proj[i], weight[i], NT)
    even_out[...] = total[:512]
    odd_out[...] = total[512:].astype(BF16)


def first_sums_body(info, jx, cy, jy, cx, down, x_out, y_out, first, s1, s2, s3, held):
    x_out[:144] = jx[:144]
    x_out[144:] = (jx[144:].astype(F32) + cy[384:].astype(F32)).astype(BF16)
    y_out[:144] = (jy[:144].astype(F32) + cx[384:].astype(F32)).astype(BF16)
    y_out[144:] = jy[144:]
    z = info[Z]
    held[...] = down[...].astype(F32) + cx[:384].astype(F32) + cy[:384].astype(F32)
    for k, out in enumerate((first, s1, s2, s3)):
        out[...] = held[rows((z ^ k) * 96, 96), :].astype(out.dtype)


def second_sums_body(info, even, came, u0, u1, u2, u3, own, half_first, x_out, y_out, across):
    hidden = even[...] + came[...].astype(F32)
    up = u0[...].astype(F32) + u1[...].astype(F32) + u2[...].astype(F32) + u3[...].astype(F32)
    own[...] = hidden[:128]
    half_first[...] = up[:48]
    for i, out in enumerate((x_out, y_out, across)):
        out[:48] = up[48 * (i + 1) : 48 * (i + 2)].astype(BF16)
        out[48:] = hidden[128 * (i + 1) : 128 * (i + 2)].astype(BF16)


def small_grads_body(info, attn, one, two, up, out):
    core = info[CORE]
    group = info[PLACE] & 3

    def split(value, place):
        n = value.shape[1]
        entry = lax.broadcasted_iota(jnp.int32, (1, n), 1)
        return jnp.where(
            lax.broadcasted_iota(jnp.int32, (32, n), 0) == place(entry), value, 0.0
        )

    def gather(value, width):
        n = value.shape[1]
        entry = lax.broadcasted_iota(jnp.int32, (n, 1), 0) % width
        chosen = jnp.where(lax.broadcasted_iota(jnp.int32, (n, 128), 1) == entry, 1.0, 0.0)
        return lax.dot_general(
            value, chosen, NN, precision=lax.Precision.HIGHEST, preferred_element_type=F32
        )

    inside = lax.broadcasted_iota(jnp.int32, (1, WIDE), 1) < GROUP
    own = [jnp.where(inside, attn[i : i + 1], 0.0) for i in range(3)]
    pairs = gather(
        split(own[0], lambda n: 4 * group + n // 48)
        + split(own[1], lambda n: 16 + 4 * group + n // 48),
        48,
    )
    values = gather(split(own[2], lambda n: 8 * group + n // 24), 24)
    six = (one[2:3], one[0:1], one[1:2], two[0:1], two[1:2], two[2:3])
    six = gather(jnp.concatenate([split(v, lambda n: n // 24) for v in six], axis=0), 24)
    ups = gather(split(up[...], lambda n: n // 96 + 4 * (n // 384) + 4 * core), 96)
    parts = [pairs[:, :48], values[:, :24]]
    parts += [six[32 * i : 32 * (i + 1), :24] for i in range(6)]
    parts += [ups[:, :96], jnp.zeros((32, 8), F32)]
    row = jnp.concatenate(parts, axis=1)
    high = row.astype(BF16).astype(F32)
    for s in range(8):
        here = slice(4 * s, 4 * (s + 1))
        out[s] = jnp.concatenate(
            [v[here, 64 * i : 64 * (i + 1)] for v in (high, row - high) for i in range(5)], axis=0
        )


def last_blocks_body(info, own, a, b, came, first, s1, s2, s3, up_held, attn_held, small_held):
    z = info[Z]
    up_held[...] = own[...].astype(F32) + a[...].astype(F32) + b[...].astype(F32)
    for g in range(4):
        attn_held[g] = came[g].astype(F32) + came[4 + g].astype(F32)
    small = sum(attn_held[g, :40, 576:] for g in range(4))
    small = small[:20] + small[20:]
    pad = jnp.zeros((1, 64), F32)
    for zz in range(4):
        small_held[zz] = jnp.concatenate(
            [small[4 * i + zz : 4 * i + zz + 1] for i in range(5)] + [pad], axis=1
        )
    for k, out in enumerate((first, s1, s2, s3)):
        parts = [up_held[rows(96 * i + (z ^ k) * 24, 24, 8), :] for i in range(3)]
        blocks = [attn_held[g, rows((z ^ k) * 24, 24, 8), :] for g in range(4)]
        for i in range(3):
            parts.append(
                jnp.concatenate([b[:, GROUP * i : GROUP * (i + 1)] for b in blocks], axis=1)
            )
        row = small_held[z ^ k]
        high = row.astype(BF16).astype(F32)
        parts.append(jnp.concatenate([high, row - high], axis=1))
        parts.append(jnp.zeros((7, 768), F32))
        out[...] = jnp.concatenate(parts, axis=0).astype(out.dtype)


def last_sum_body(info, first, r1, r2, r3, half, proj_out, attn_out, small):
    total = first[...] + r1[...].astype(F32) + r2[...].astype(F32) + r3[...].astype(F32)
    half[...] = total[:48]
    proj_out[...] = total[48:72]
    for i in range(3):
        attn_out[:, 768 * i : 768 * (i + 1)] = total[72 + 24 * i : 96 + 24 * i]
    small[...] = total[144:145, :384] + total[144:145, 384:]


def end_sum_body(info, half, other_half, d_resid, hidden, r2, r4, r6, own, sent, out):
    y = info[Y]
    other = other_half[...] + r2[:48].astype(F32) + r4[:48].astype(F32) + r6[:48].astype(F32)
    own[...] = jnp.concatenate([half[:24], other[:24]], axis=1)
    sent[...] = jnp.concatenate([half[24:], other[24:]], axis=1).astype(BF16)
    out[y] = d_resid[:128] + hidden[...] + r2[48:].astype(F32)
    out[1 - y] = d_resid[128:] + r4[48:].astype(F32) + r6[48:].astype(F32)


def up_end_body(info, own, came, up_out):
    core = info[CORE]
    for which, source in ((core, own), (1 - core, came)):
        for q in range(4):
            up_out[:, lanes(768 * q + 384 * which, 384)] = source[
                :, 384 * q : 384 * (q + 1)
            ].astype(F32)


def join_body(
    info, g0, gx, gy, gd, p_own, p_came, dx, d_from_y, dy, d_from_x, j0, jx, jy, mx, my
):
    proj = [(p_own[j].astype(F32) + p_came[j].astype(F32)).astype(BF16) for j in range(4)]
    for j, (g, out) in enumerate(((g0, j0), (gx, jx), (gy, jy))):
        out[:192] = g[...]
        out[192:] = proj[j]
    mx[:192] = dx[:192]
    mx[192:384] = (dx[192:].astype(F32) + d_from_y[...].astype(F32)).astype(BF16)
    my[:192] = (dy[:192].astype(F32) + d_from_x[...].astype(F32)).astype(BF16)
    my[192:384] = dy[192:]
    mx[384:] = gd[:144]
    my[384:432] = gd[144:]
    my[432:] = proj[3]
def split_layer(
    hidden_in,
    lengths,
    attn_weight,
    attn_bias,
    proj_weight,
    proj_bias,
    first_gain,
    first_shift,
    up_weight,
    up_bias,
    down_weight,
    down_bias,
    second_gain,
    second_shift,
    grad_out,
):
    both_axes = ("seq", "batch")
    info = lengths

    small_vectors = (
        attn_bias, proj_bias, first_gain, first_shift, down_bias, second_gain, second_shift, up_bias
    )
    mine, other, joined, early, attn_wide = call(
        prepare_body,
        [
            shape((128, 768)), shape((128, 768)), shape((24, 5376)), shape((48, 768)),
            shape((4, 24, 2432)),
        ],
        info, hidden_in, attn_weight, up_weight, proj_weight, down_weight,
        *[v[None] for v in small_vectors], name="prepare", alone=True,
    )
    cosine, sine = (jnp.asarray(table) for table in rotary_tables(8 * 128))
    attn_wide = lax.all_to_all(attn_wide, "batch", 0, 0, tiled=True)
    far = [swap_batch(joined, k) for k in (1, 2, 3)]
    r2, r4, r6 = swap_seq(mine, 2), swap_seq(other, 4), swap_seq(other, 6)
    odd = swap_seq(jnp.concatenate([mine, r2, r4, r6], axis=0), 1)
    early_far = [swap_seq(early, k) for k in (2, 4, 6)]
    (early_plane,) = call(early_body, [shape((192, 768))], info, early, *early_far, name="early")
    (weight_sent,) = call(
        attn_column_body, [shape((8, 96, 640))], info, after(attn_wide, far[0], far[1], *early_far),
        name="attn_column",
    )
    weight_given = lax.all_to_all(weight_sent, "seq", 0, 0, tiled=True)
    up_keep, up_sent, rest = call(
        up_column_body, [shape((192, 768)), shape((192, 768)), shape((288, 768))],
        info, joined, *far, scratch=[shape((96, 3072))], name="up_column",
    )
    (up_column,) = call(
        up_join_body, [shape((672, 768))], info, up_keep, swap_seq(up_sent, 1), rest,
        name="up_join",
    )
    up_column, early_plane, odd, weight_given = fence(up_column, early_plane, odd, weight_given)

    up_x, up_y = swap_seq(up_column, 2), swap_seq(up_column, 4)
    early_far = [swap_batch(early_plane, k) for k in (1, 2, 3)]

    tokens_here, weight_here, query_t, key, value, attended, stats, even_low, odd_low = call(
        attend_body,
        [
            shape((1024, 768)), shape((3, 768, WIDE)),
            shape((WIDE, 1024)), shape((1024, WIDE)), shape((1024, WIDE)),
            shape((GROUP, 1024), F32), shape((8, 1024), F32),
            shape((4, 128, GROUP)), shape((4, 128, GROUP)),
        ],
        info, mine, r2, r4, r6, odd, weight_given, cosine, sine,
        scratch=[shape((1024, WIDE), F32)] * 2, flops=8_000_000_000, name="attend", alone=True,
    )
    even_low, odd_low, up_x, up_y, weight_given = fence(even_low, odd_low, up_x, up_y, weight_given)

    p0, p1, p2, p3 = call(
        pair_body, [shape((128, 384))] * 4, info, even_low, swap_seq(odd_low, 1), name="pair"
    )
    p0, p1, p2, p3, up_x, up_y, early_far = fence(p0, p1, p2, p3, up_x, up_y, early_far)

    a2, a4, a6 = swap_seq(p1, 2), swap_seq(p2, 4), swap_seq(p3, 6)
    up_da, up_db = swap_seq(up_y[:336], 2), swap_seq(up_x[336:], 4)
    vectors, up_bias_here = call(
        small_body, [shape((8, 768), F32), shape((1, 1536), F32)], info, after(weight_given, p0), name="small"
    )
    a2, a4, a6, up_da, up_db, vectors, up_bias_here = fence(
        a2, a4, a6, up_da, up_db, vectors, up_bias_here
    )
    up_blocks = (up_column, up_x, up_y, jnp.concatenate([up_da, up_db], axis=0))
    down_blocks = (early_plane, *early_far)
    (proj_rows,) = call(proj_rows_body, [shape((4, 96, 768))], info, *up_blocks, name="proj_rows")
    proj_came = swap_seq(proj_rows, 1)
    normed, low_mine, hat_one, rstd_one, rows_here, proj_here = call(
        mix_body,
        [
            shape((256, 768), F32), shape((256, 768)), shape((256, 768), F32),
            shape((256, 128), F32), shape((256, 768)), shape((768, 768)),
        ],
        info, p0, a2, a4, a6, *up_blocks, proj_came, mine, other, vectors,
        scratch=[shape((768, 768))], flops=300_000_000, name="mix",
    )
    low_other = swap_seq(low_mine, 1)
    part_mine, part_other, active, slope = call(
        up_body,
        [shape((256, 768), F32), shape((256, 768)), shape((512, 1536)), shape((512, 1536))],
        info, low_mine, low_other, *up_blocks, *down_blocks, up_bias_here,
        scratch=[shape((768, 1536)), shape((1536, 768))], flops=2_400_000_000, name="up",
    )
    layer_out, d_resid_two, d_low, sums_two = call(
        norm_two_body,
        [shape((2, 128, 768)), shape((256, 768), F32), shape((256, 768)), shape((8, 768), F32)],
        info, part_mine, swap_seq(part_other, 1), normed, vectors, grad_out, name="norm_two",
    )
    d_came = swap_seq(d_low, 1)
    g_down, gx_down, gy_down, gda, gdb = call(
        down_grad_body, [shape((384, 768))] * 3 + [shape((192, 768))] * 2,
        info, active, d_low, d_came,
        scratch=[shape((1536, 768))], flops=1_200_000_000, name="down_grad",
    )
    gx_down, gy_down, gda, gdb, d_low, d_came = fence(gx_down, gy_down, gda, gdb, d_low, d_came)

    gda, gdb = swap_seq(gda, 2), swap_seq(gdb, 4)
    part_mine, part_other, g0, gx, gy, gd, z0, z1, z2, z3, up_sums = call(
        up_grad_body,
        [shape((256, 768), F32), shape((256, 768))] + [shape((192, 768))] * 8
        + [shape((1, 1536), F32)],
        info, d_low, d_came, slope, low_mine, low_other, *up_blocks, *down_blocks,
        scratch=[shape((768, 1536)), shape((1536, 768)), shape((768, 1536), F32)],
        flops=3_600_000_000, name="up_grad",
    )
    gda, gdb, part_mine, part_other = fence(gda, gdb, part_mine, part_other)
    d_resid_one, e0, e2, e4, e6, proj_own, proj_sent, sums_one = call(
        norm_one_body,
        [shape((256, 768), F32)] + [shape((128, 384))] * 4 + [shape((4, 96, 768))] * 2
        + [shape((8, 768), F32)],
        info, d_resid_two, part_mine, swap_seq(part_other, 1), hat_one, rstd_one, vectors,
        rows_here, proj_here,
        scratch=[shape((768, 768))], flops=600_000_000, name="norm_one",
    )
    e0, e2, e4, e6, proj_sent = fence(e0, e2, e4, e6, proj_sent)

    e2, e4, e6 = swap_seq(e2, 2), swap_seq(e4, 4), swap_seq(e6, 6)
    proj_came = swap_seq(proj_sent, 1)
    j0, jx, jy, mx, my = call(
        join_body, [shape((288, 768))] * 3 + [shape((528, 768))] * 2,
        info, g0, gx, gy, gd, proj_own, proj_came, gx_down, gdb, gy_down, gda, name="join",
    )
    e2, e4, e6, j0, jx, jy, mx, my = fence(e2, e4, e6, j0, jx, jy, mx, my)
    (split,) = call(split_core_body, [shape((512, GROUP))], info, e0, e2, e4, e6, name="split")
    e_came = swap_seq(split, 1)
    e_came, mx, my, z1, z2, z3 = fence(e_came, mx, my, z1, z2, z3)

    mx, my = swap_seq(mx, 2), swap_seq(my, 4)
    z_came = [swap_batch(part, k) for k, part in zip((1, 2, 3), (z1, z2, z3))]
    d_proj, sums_attn = call(
        attend_back_body,
        [shape((3, 1024, WIDE)), shape((8, WIDE), F32)],
        info, e0, e2, e4, e6, e_came, query_t, key, value, attended, stats, cosine, sine,
        scratch=[
            shape((WIDE, 1024)), shape((1024, 1024)), shape((1024, 1024)),
            shape((WIDE, 1024), F32), *[shape((1024, WIDE), F32)] * 4,
        ],
        flops=8_000_000_000, name="attend_back",
    )
    (small_grads,) = call(
        small_grads_body, [shape((8, 40, 64), F32)], info, sums_attn, sums_one, sums_two, up_sums,
        name="small_grads",
    )
    (w_sent,) = call(
        attn_grad_body, [shape((8, 96, 640))], info, tokens_here, d_proj, small_grads,
        flops=1_200_000_000, name="attn_grad",
    )
    even, odd_sent = call(
        hidden_grad_body, [shape((512, 768), F32), shape((512, 768))], info, d_proj, weight_here,
        flops=1_200_000_000, name="hidden_grad",
    )
    w_came = lax.all_to_all(w_sent, "seq", 0, 0, tiled=True)
    mx, my, z_came, odd_sent, _ = fence(mx, my, z_came, odd_sent, w_sent)

    jx, jy, first, b1, b2, b3 = call(
        first_sums_body,
        [shape((288, 768))] * 2 + [shape((96, 768), F32)] + [shape((96, 768))] * 3,
        info, jx, my, jy, mx, g_down, scratch=[shape((384, 768), F32)], name="first_sums",
        alone=True,
    )
    jx, jy = swap_seq(jx, 2), swap_seq(jy, 4)
    b1, b2, b3 = [swap_batch(b, k) for k, b in ((1, b1), (2, b2), (3, b3))]
    own, half_first, s2, s4, s6 = call(
        second_sums_body,
        [shape((128, 768), F32), shape((48, 768), F32)] + [shape((176, 768))] * 3,
        info, even, swap_seq(odd_sent, 1), z0, *z_came, name="second_sums", alone=True,
    )
    jx, jy, s2, s4, s6, w_came, b1, b2, b3 = fence(jx, jy, s2, s4, s6, w_came, b1, b2, b3)

    last_first, *last_sends = call(
        last_blocks_body, [shape((152, 768), F32)] + [shape((152, 768))] * 3,
        info, j0, jx, jy, w_came,
        scratch=[shape((288, 768), F32), shape((4, 96, 640), F32), shape((4, 1, 384), F32)],
        name="last_blocks", alone=True,
    )
    last_came = [swap_batch(part, k) for k, part in zip((1, 2, 3), last_sends)]
    s2, s4, s6 = swap_seq(s2, 2), swap_seq(s4, 4), swap_seq(s6, 6)
    (grad_down_weight,) = call(
        sum_four_body, [shape((96, 768), F32)], info, first, b1, b2, b3, name="down_end"
    )
    up_half, grad_proj_weight, grad_attn_weight, d_small = call(
        last_sum_body,
        [shape((48, 768), F32), shape((24, 768), F32), shape((24, 2304), F32), shape((1, 384), F32)],
        info, last_first, *last_came, name="last_sum",
    )
    up_own, up_sent, grad_hidden = call(
        end_sum_body,
        [shape((24, 1536), F32), shape((24, 1536)), shape((2, 128, 768), F32)],
        info, up_half, half_first, d_resid_one, own, s2, s4, s6, name="end_sum",
    )
    (grad_up_weight,) = call(
        up_end_body, [shape((24, 3072), F32)], info, up_own, swap_seq(up_sent, 1), name="up_end"
    )

    d_small = d_small[0]
    d_vectors = [d_small[72 + 24 * i : 96 + 24 * i] for i in range(6)]
    return (
        layer_out,
        grad_hidden,
        grad_attn_weight,
        d_small[:48],
        d_small[48:72],
        grad_proj_weight,
        d_vectors[0],
        d_vectors[1],
        d_vectors[2],
        grad_up_weight,
        d_small[216:312],
        grad_down_weight,
        d_vectors[3],
        d_vectors[4],
        d_vectors[5],
    )


def solution(mesh):
    in_specs = (
        P("batch", "seq", None),
        P("batch"),
        P(("seq", "batch"), None),
        P(("seq", "batch")),
        P(("seq", "batch"), None),
        P(("seq", "batch")),
        P(("seq", "batch")),
        P(("seq", "batch")),
        P(("seq", "batch"), None),
        P(("seq", "batch")),
        P(("seq", "batch"), None),
        P(("seq", "batch")),
        P(("seq", "batch")),
        P(("seq", "batch")),
        P("batch", "seq", None),
    )
    out_specs = (
        P("batch", "seq", None),
        P("batch", "seq", None),
        P(("seq", "batch"), None),
        P(("seq", "batch")),
        P(("seq", "batch")),
        P(("seq", "batch"), None),
        P(("seq", "batch")),
        P(("seq", "batch")),
        P(("seq", "batch")),
        P(("seq", "batch"), None),
        P(("seq", "batch")),
        P(("seq", "batch"), None),
        P(("seq", "batch")),
        P(("seq", "batch")),
        P(("seq", "batch")),
    )
    fits = mesh.shape["seq"] == SEQ_SIDE and mesh.shape["batch"] == BATCH_SIDE
    return jax.shard_map(
        split_layer if fits else on_device, mesh=mesh, in_specs=in_specs, out_specs=out_specs, check_vma=False
    )
```

```python
import math

import jax
import jax.numpy as jnp
import numpy as np
from jax import lax
from jax.experimental import pallas as pl
from jax.experimental.pallas import tpu as pltpu
from jax.sharding import PartitionSpec as P

HEADS = 12
HEAD_DIM = 64


EPSILON = 1e-12
NEG_BIG = -1e30


def passed_along(value, axis, steps):
    count = lax.axis_size(axis)
    pairs = [(source, (source + steps) % count) for source in range(count)]
    return lax.ppermute(value, axis, pairs)


def rotate(vectors, positions):
    half_dim = vectors.shape[-1] // 2
    frequency = 10000.0 ** (-2.0 * jnp.arange(half_dim, dtype=jnp.float32) / vectors.shape[-1])
    angles = positions[:, None] * frequency[None, :]
    cosine = jnp.cos(angles)[:, None, :]
    sine_part = jnp.sin(angles)[:, None, :]
    split_pairs = vectors.reshape(vectors.shape[:-1] + (half_dim, 2))
    even_part = split_pairs[..., 0]
    odd_part = split_pairs[..., 1]
    turned = jnp.stack(
        [even_part * cosine - odd_part * sine_part, odd_part * cosine + even_part * sine_part],
        axis=-1,
    )
    return turned.reshape(vectors.shape)


def layer_norm(residual, scale_gain, shift_bias):
    row_mean = jnp.mean(residual, axis=-1, keepdims=True)
    centered = residual - row_mean
    variance = jnp.mean(centered * centered, axis=-1, keepdims=True)
    return centered * lax.rsqrt(variance + EPSILON) * scale_gain + shift_bias


def gelu_exact(upward):
    return jax.nn.gelu(upward, approximate=False)


def run_blocks(step_fn, carry_now, key_piece, first_row, block_keys):
    row_count = key_piece.shape[1]
    width_now = block_keys if row_count % block_keys == 0 else row_count

    def one_turn(index, carry_in):
        begin_at = index * width_now
        sub_piece = lax.dynamic_slice_in_dim(key_piece, begin_at, width_now, 1)
        return step_fn(carry_in, sub_piece, first_row + begin_at)

    return lax.fori_loop(0, row_count // width_now, one_turn, carry_now)


def on_device(
    hidden_in,
    lengths,
    attn_weight,
    attn_bias,
    proj_weight,
    proj_bias,
    first_gain,
    first_shift,
    up_weight,
    up_bias,
    down_weight,
    down_bias,
    second_gain,
    second_shift,
    grad_out,
):
    seq_count, span_rows, model_width = hidden_in.shape
    token_count = seq_count * span_rows
    seq_devices = lax.axis_size("seq")
    my_index = lax.axis_index("seq")
    block_keys = max(span_rows, 512)
    score_scale = HEAD_DIM ** (-0.5)
    offset = my_index * span_rows
    row_index = offset + jnp.arange(span_rows, dtype=jnp.int32)
    positions = row_index.astype(jnp.float32)
    attn_full, attn_bias_full, proj_full, proj_bias_full, gain_one, shift_one = (
        lax.all_gather(attn_weight, ("seq", "batch"), axis=0, tiled=True),
        lax.all_gather(attn_bias, ("seq", "batch"), axis=0, tiled=True),
        lax.all_gather(proj_weight, ("seq", "batch"), axis=0, tiled=True),
        lax.all_gather(proj_bias, ("seq", "batch"), axis=0, tiled=True),
        lax.all_gather(first_gain, ("seq", "batch"), axis=0, tiled=True),
        lax.all_gather(first_shift, ("seq", "batch"), axis=0, tiled=True),
    )
    up_full, up_bias_full, down_full, down_bias_full, gain_two, shift_two = (
        lax.all_gather(up_weight, ("seq", "batch"), axis=0, tiled=True),
        lax.all_gather(up_bias, ("seq", "batch"), axis=0, tiled=True),
        lax.all_gather(down_weight, ("seq", "batch"), axis=0, tiled=True),
        lax.all_gather(down_bias, ("seq", "batch"), axis=0, tiled=True),
        lax.all_gather(second_gain, ("seq", "batch"), axis=0, tiled=True),
        lax.all_gather(second_shift, ("seq", "batch"), axis=0, tiled=True),
    )
    tokens_flat = hidden_in.reshape(token_count, model_width)
    projected = jnp.dot(
        tokens_flat, attn_full, preferred_element_type=jnp.float32
    ) + attn_bias_full.astype(jnp.float32)
    projected = projected.reshape(seq_count, span_rows, 3, HEADS, HEAD_DIM)
    queries = rotate(projected[:, :, 0], positions).astype(jnp.bfloat16)
    keys_low = rotate(projected[:, :, 1], positions).astype(jnp.bfloat16)
    values_low = projected[:, :, 2].astype(jnp.bfloat16)
    key_values = jnp.concatenate(
        [
            keys_low.reshape(seq_count, span_rows, model_width),
            values_low.reshape(seq_count, span_rows, model_width),
        ],
        axis=-1,
    )

    def key_mask(first_row, row_count):
        key_rows = first_row + jnp.arange(row_count, dtype=jnp.int32)
        return (key_rows[None, :] < lengths[:, None])[:, None, None, :]

    def split_pairs(key_piece):
        row_count = key_piece.shape[1]
        keys_part = key_piece[:, :, :model_width].reshape(seq_count, row_count, HEADS, HEAD_DIM)
        values_part = key_piece[:, :, model_width:].reshape(seq_count, row_count, HEADS, HEAD_DIM)
        return (keys_part, values_part)

    def attend_step(carry_in, key_piece, first_row):
        row_max, row_sum, accum = carry_in
        keys_part, values_part = split_pairs(key_piece)
        masked = key_mask(first_row, key_piece.shape[1])
        scores = score_scale * jnp.einsum(
            "sqhd,skhd->shqk", queries, keys_part, preferred_element_type=jnp.float32
        )
        scores = jnp.where(masked, scores, NEG_BIG)
        new_max = jnp.maximum(row_max, jnp.max(scores, axis=-1))
        weights = jnp.where(masked, jnp.exp(scores - new_max[..., None]), 0.0)
        factor = jnp.exp(row_max - new_max)
        row_sum = row_sum * factor + jnp.sum(weights, axis=-1)
        accum = accum * jnp.transpose(factor, (0, 2, 1))[..., None] + jnp.einsum(
            "shqk,skhd->sqhd",
            weights.astype(jnp.bfloat16),
            values_part,
            preferred_element_type=jnp.float32,
        )
        return (new_max, row_sum, accum)

    start_state = (
        jnp.full((seq_count, HEADS, span_rows), NEG_BIG, jnp.float32),
        jnp.zeros((seq_count, HEADS, span_rows), jnp.float32),
        jnp.zeros((seq_count, span_rows, HEADS, HEAD_DIM), jnp.float32),
    )
    row_max, row_sum, accum = run_blocks(
        attend_step,
        start_state,
        lax.all_gather(key_values, "seq", axis=1, tiled=True),
        jnp.int32(0),
        block_keys,
    )
    sum_view = jnp.transpose(row_sum, (0, 2, 1))[..., None]
    attended = accum / sum_view
    attn_rows = attended.reshape(token_count, model_width).astype(jnp.bfloat16)
    mixed = jnp.dot(
        attn_rows, proj_full, preferred_element_type=jnp.float32
    ) + proj_bias_full.astype(jnp.float32)
    normed, norm_back_one = jax.vjp(
        layer_norm,
        tokens_flat.astype(jnp.float32) + mixed,
        gain_one.astype(jnp.float32),
        shift_one.astype(jnp.float32),
    )
    normed_low = normed.astype(jnp.bfloat16)
    upward = jnp.dot(normed_low, up_full, preferred_element_type=jnp.float32) + up_bias_full.astype(
        jnp.float32
    )
    active, gelu_back = jax.vjp(gelu_exact, upward)
    active_low = active.astype(jnp.bfloat16)
    downward = jnp.dot(
        active_low, down_full, preferred_element_type=jnp.float32
    ) + down_bias_full.astype(jnp.float32)
    output_rows, norm_back_two = jax.vjp(
        layer_norm, normed + downward, gain_two.astype(jnp.float32), shift_two.astype(jnp.float32)
    )
    layer_out = output_rows.reshape(seq_count, span_rows, model_width).astype(jnp.bfloat16)
    row_valid = (row_index[None, :] < lengths[:, None]).astype(jnp.float32)
    cotangent = (grad_out.astype(jnp.float32) * row_valid[:, :, None]).reshape(
        token_count, model_width
    )
    d_resid_two, d_gain_two, d_shift_two = norm_back_two(cotangent)
    d_down = d_resid_two.astype(jnp.bfloat16)
    d_down_bias = jnp.sum(d_down.astype(jnp.float32), axis=0)
    d_down_weight = jnp.einsum("tf,td->fd", active_low, d_down, preferred_element_type=jnp.float32)
    d_active = jnp.dot(d_down, down_full.T, preferred_element_type=jnp.float32)
    (d_upward,) = gelu_back(d_active)
    d_up = d_upward.astype(jnp.bfloat16)
    d_up_bias = jnp.sum(d_up.astype(jnp.float32), axis=0)
    d_up_weight = jnp.einsum("td,tf->df", normed_low, d_up, preferred_element_type=jnp.float32)
    d_normed = d_resid_two + jnp.dot(d_up, up_full.T, preferred_element_type=jnp.float32)
    ffn_parts = (
        lax.psum_scatter(d_up_weight, ("seq", "batch"), scatter_dimension=0, tiled=True),
        lax.psum_scatter(d_up_bias, ("seq", "batch"), scatter_dimension=0, tiled=True),
        lax.psum_scatter(d_down_weight, ("seq", "batch"), scatter_dimension=0, tiled=True),
        lax.psum_scatter(d_down_bias, ("seq", "batch"), scatter_dimension=0, tiled=True),
        lax.psum_scatter(d_gain_two, ("seq", "batch"), scatter_dimension=0, tiled=True),
        lax.psum_scatter(d_shift_two, ("seq", "batch"), scatter_dimension=0, tiled=True),
    )
    d_resid_one, d_gain_one, d_shift_one = norm_back_one(d_normed)
    d_mixed = d_resid_one.astype(jnp.bfloat16)
    d_proj_bias = jnp.sum(d_mixed.astype(jnp.float32), axis=0)
    d_proj_weight = jnp.einsum("td,te->de", attn_rows, d_mixed, preferred_element_type=jnp.float32)
    d_attended = jnp.dot(d_mixed, proj_full.T, preferred_element_type=jnp.float32).astype(
        jnp.bfloat16
    )
    d_attended = d_attended.astype(jnp.float32).reshape(seq_count, span_rows, HEADS, HEAD_DIM)
    delta = jnp.transpose(jnp.sum(d_attended * attended, axis=-1), (0, 2, 1))
    delta_scaled = delta / row_sum
    guide = (d_attended / sum_view).astype(jnp.bfloat16)

    def back_step(carry_in, key_piece, first_row):
        d_queries, buffer = carry_in
        keys_part, values_part = split_pairs(key_piece)
        row_count = key_piece.shape[1]
        masked = key_mask(first_row, row_count)
        scores = score_scale * jnp.einsum(
            "sqhd,skhd->shqk", queries, keys_part, preferred_element_type=jnp.float32
        )
        scores = jnp.where(masked, scores, NEG_BIG)
        weights = jnp.where(masked, jnp.exp(scores - row_max[..., None]), 0.0)
        d_weights = jnp.einsum(
            "sqhd,skhd->shqk", guide, values_part, preferred_element_type=jnp.float32
        )
        d_scores = (weights * (d_weights - delta_scaled[..., None])).astype(jnp.bfloat16)
        d_queries = d_queries + score_scale * jnp.einsum(
            "shqk,skhd->sqhd", d_scores, keys_part, preferred_element_type=jnp.float32
        )
        d_keys = score_scale * jnp.einsum(
            "shqk,sqhd->skhd", d_scores, queries, preferred_element_type=jnp.float32
        )
        d_values = jnp.einsum(
            "shqk,sqhd->skhd",
            weights.astype(jnp.bfloat16),
            guide,
            preferred_element_type=jnp.float32,
        )
        new_terms = jnp.concatenate(
            [
                d_keys.reshape(seq_count, row_count, model_width),
                d_values.reshape(seq_count, row_count, model_width),
            ],
            axis=-1,
        )
        current = buffer
        buffer = current + new_terms
        return (d_queries, buffer)

    zero_queries = jnp.zeros((seq_count, span_rows, HEADS, HEAD_DIM), jnp.float32)

    def cycle_turn(turn, carry_in):
        d_queries, pair_piece, grad_piece = carry_in
        owner = (my_index - turn) % seq_devices
        base_row = owner * span_rows

        def owner_step(inner, key_piece, first_row):
            return back_step(inner, key_piece, first_row)

        d_queries, grad_piece = run_blocks(
            owner_step, (d_queries, grad_piece), pair_piece, base_row, block_keys
        )
        grad_piece = passed_along(grad_piece.astype(jnp.bfloat16), "seq", 1).astype(
            grad_piece.dtype
        )
        pair_piece = passed_along(pair_piece, "seq", 1)
        return (d_queries, pair_piece, grad_piece)

    start_cycle = (
        zero_queries,
        key_values,
        jnp.zeros((seq_count, span_rows, 2 * model_width), jnp.float32),
    )
    d_queries, pair_spent, d_pairs = lax.fori_loop(0, seq_devices, cycle_turn, start_cycle)
    d_keys_own = d_pairs[:, :, :model_width].reshape(seq_count, span_rows, HEADS, HEAD_DIM)
    d_values_own = d_pairs[:, :, model_width:].reshape(seq_count, span_rows, HEADS, HEAD_DIM)
    d_projected = jnp.stack(
        [rotate(d_queries, -positions), rotate(d_keys_own, -positions), d_values_own], axis=2
    )
    d_projected = d_projected.reshape(token_count, 3 * model_width).astype(jnp.bfloat16)
    d_attn_bias = jnp.sum(d_projected.astype(jnp.float32), axis=0)
    d_pair_bias = d_attn_bias[: 2 * model_width]
    d_value_bias = d_attn_bias[2 * model_width :]
    d_attn_weight = jnp.einsum(
        "td,tf->df", tokens_flat, d_projected, preferred_element_type=jnp.float32
    )
    grad_hidden = d_resid_one + jnp.dot(
        d_projected, attn_full.T, preferred_element_type=jnp.float32
    )
    attn_parts = (
        lax.psum_scatter(d_attn_weight, ("seq", "batch"), scatter_dimension=0, tiled=True),
        lax.psum_scatter(d_pair_bias, ("seq", "batch"), scatter_dimension=0, tiled=True),
        lax.psum_scatter(d_value_bias, ("seq", "batch"), scatter_dimension=0, tiled=True),
        lax.psum_scatter(d_proj_weight, ("seq", "batch"), scatter_dimension=0, tiled=True),
        lax.psum_scatter(d_proj_bias, ("seq", "batch"), scatter_dimension=0, tiled=True),
        lax.psum_scatter(d_gain_one, ("seq", "batch"), scatter_dimension=0, tiled=True),
        lax.psum_scatter(d_shift_one, ("seq", "batch"), scatter_dimension=0, tiled=True),
    )
    return (
        layer_out,
        grad_hidden.reshape(seq_count, span_rows, model_width),
        attn_parts[0],
        attn_parts[1],
        attn_parts[2],
        attn_parts[3],
        attn_parts[4],
        attn_parts[5],
        attn_parts[6],
        ffn_parts[0],
        ffn_parts[1],
        ffn_parts[2],
        ffn_parts[3],
        ffn_parts[4],
        ffn_parts[5],
    )


SEQ_SIDE = 8
BATCH_SIDE = 4
GROUP = 192
WIDE = 256
HERE = 3
EVEN = (0, 2, 4, 6)
ODD = (1, 3, 5, 7)
CORE, X, Y, Z, PLACE, LEN_MINE, LEN_OTHER = range(7)
F32, BF16 = jnp.float32, jnp.bfloat16
NN = (((1,), (0,)), ((), ()))
NT = (((1,), (1,)), ((), ()))
TN = (((0,), (0,)), ((), ()))


def swap_seq(value, mask):
    return lax.ppermute(value, "seq", [(i, i ^ mask) for i in range(SEQ_SIDE)])


def swap_batch(value, mask):
    return lax.ppermute(value, "batch", [(i, i ^ mask) for i in range(BATCH_SIDE)])


def after(value, *done):
    return lax.optimization_barrier((value,) + done)[0]


def fence(*values):
    return lax.optimization_barrier(values)


def shape(dims, dtype=BF16):
    return jax.ShapeDtypeStruct(dims, dtype)


def call(body, outs, info, *args, scratch=(), flops=0, name=None, alone=False):
    moved = sum(a.size * a.dtype.itemsize for a in args)
    moved += sum(math.prod(o.shape) * o.dtype.itemsize for o in outs)
    held = sum(math.prod(m.shape) * m.dtype.itemsize for m in scratch)
    return pl.pallas_call(
        lambda lengths, *refs: body(Spot(lengths), *refs),
        out_shape=outs,
        in_specs=[pl.BlockSpec(memory_space=pltpu.SMEM)]
        + [pl.BlockSpec(memory_space=pltpu.VMEM)] * len(args),
        out_specs=[pl.BlockSpec(memory_space=pltpu.VMEM)] * len(outs),
        scratch_shapes=[pltpu.VMEM(m.shape, m.dtype) for m in scratch],
        compiler_params=pltpu.CompilerParams(
            vmem_limit_bytes=60 << 20 if alone else min(56 << 20, moved + held + (10 << 20))
        ),
        cost_estimate=pl.CostEstimate(flops=1, bytes_accessed=1, transcendentals=0),
        name=name,
    )(info, *args)


def dot(left, right, dims=NN):
    return lax.dot_general(left, right, dims, preferred_element_type=F32)


class Spot:
    def __init__(self, lengths):
        self.lengths = lengths

    def __getitem__(self, what):
        place = lax.axis_index("seq")
        if what == Z:
            return lax.axis_index("batch")
        if what == LEN_MINE:
            return self.lengths[place >> 2]
        if what == LEN_OTHER:
            return self.lengths[1 - (place >> 2)]
        return {CORE: place & 1, X: (place >> 1) & 1, Y: place >> 2, PLACE: place}[what]


def chips(info):
    x, y = info[X], info[Y]
    return ((y, x), (y, 1 - x), (1 - y, x), (1 - y, 1 - x))


def lanes(start, size):
    return pl.ds(pl.multiple_of(start, 128), size)


def rows(start, size, unit=16):
    return pl.ds(pl.multiple_of(start, unit), size)


def rotary_tables(length):
    entry = np.arange(WIDE)
    frequency = (10000.0 ** (-2.0 * ((entry % HEAD_DIM) // 2) / HEAD_DIM)).astype(np.float32)
    angles = np.arange(length, dtype=np.float32)[:, None] * frequency[None, :]
    used = entry < GROUP
    sign = np.where(entry % 2 == 0, -1.0, 1.0)
    cosine = np.cos(angles.astype(np.float64)) * used
    sine = np.sin(angles.astype(np.float64)) * (used * sign)
    return cosine.astype(np.float32), sine.astype(np.float32)


def place_tables(info, cosine, sine, cosine_held, sine_held):
    for i, k in enumerate(EVEN + ODD):
        here = rows((info[PLACE] ^ k) * 128, 128)
        cosine_held[128 * i : 128 * (i + 1)] = cosine[here, :]
        sine_held[128 * i : 128 * (i + 1)] = sine[here, :]


def prepare_body(
    info, hidden, attn, up, proj, down, v0, v1, v2, v3, v4, v5, v6, v7,
    mine, other, joined, early, wide,
):
    y = info[Y]
    mine[...] = hidden[y]
    other[...] = hidden[1 - y]
    late = down[48:96].astype(F32)
    early[...] = down[:48]
    parts = [v[...].astype(F32) for v in (v0, v1, v2, v3, v4, v5, v6, v7)]
    row = jnp.concatenate(parts + [jnp.zeros((1, 8), F32)], axis=1)
    small = jnp.concatenate(
        [row[:, 64 * i : 64 * (i + 1)] for i in range(5)] + [jnp.zeros((19, 64), F32)], axis=0
    )
    small = jnp.concatenate([small, jnp.zeros((24, 64), F32)], axis=1).astype(BF16)
    joined[:, :3072] = up[...]
    joined[:, 3072:3840] = proj[...]
    joined[:, 3840:4608] = late[:24].astype(BF16)
    joined[:, 4608:5376] = late[24:].astype(BF16)
    for k in range(4):
        wide[k, :, :2304] = attn[...]
        wide[k, :, 2304:] = small


def by_batch(info, pieces):
    z = info[Z]
    values = [p[...].astype(F32) for p in pieces]
    ordered = []
    for zz in range(4):
        k = zz ^ z
        low = jnp.where(k == 0, values[0], values[1])
        high = jnp.where(k == 2, values[2], values[3])
        ordered.append(jnp.where(k < 2, low, high))
    return ordered


def attn_column_body(info, pieces, out):
    column = jnp.concatenate([pieces[zz].astype(F32) for zz in range(4)], axis=0)
    small = [column[24 * zz + i : 24 * zz + i + 1, 2304:2368] for i in range(5) for zz in range(4)]
    small = jnp.concatenate(small + [jnp.zeros((76, 64), F32)], axis=0)
    for g in range(4):
        part = jnp.concatenate(
            [column[:, 768 * i + GROUP * g : 768 * i + GROUP * (g + 1)] for i in range(3)] + [small],
            axis=1,
        ).astype(BF16)
        out[g] = part
        out[4 + g] = part


def up_column_body(info, p0, p1, p2, p3, keep, sent, rest, held):
    core = info[CORE]
    pieces = by_batch(info, (p0, p1, p2, p3))
    column = jnp.concatenate(pieces, axis=0).astype(BF16)
    held[...] = column[:, :3072]
    rest[:96] = column[:, 3072:3840]
    for zz in range(4):
        rest[96 + 48 * zz : 144 + 48 * zz] = jnp.concatenate(
            [pieces[zz][:, 3840:4608], pieces[zz][:, 4608:]], axis=0
        ).astype(BF16)
    for which, out in ((core, keep), (1 - core, sent)):
        for q in range(4):
            out[96 * (q // 2) : 96 * (q // 2 + 1), 384 * (q % 2) : 384 * (q % 2 + 1)] = held[
                :, lanes(768 * q + 384 * which, 384)
            ]


def up_join_body(info, keep, came, rest, out):
    out[0:96] = keep[:96]
    out[96:192] = came[:96]
    out[192:288] = keep[96:]
    out[288:384] = came[96:]
    out[384:672] = rest[...]


def early_body(info, p0, px, py, pd, out):
    for j, p in enumerate((p0, px, py, pd)):
        out[48 * j : 48 * (j + 1)] = p[...]


def attend_body(
    info, mine, r2, r4, r6, odd, given, cosine_all, sine_all,
    x_out, weight, qt_out, k_out, v_out, att_out, stats, even_low, odd_low, cosine, sine,
):
    place_tables(info, cosine_all, sine_all, cosine, sine)
    weight[:, :, GROUP:] = jnp.zeros((3, 768, WIDE - GROUP), BF16)
    for i in range(3):
        for s in range(8):
            weight[i, 96 * s : 96 * (s + 1), :GROUP] = given[s, :, GROUP * i : GROUP * (i + 1)]
    small = jnp.concatenate(
        [
            jnp.concatenate([given[s, 0:16, 576:640][4 * i : 4 * (i + 1)] for s in range(8)], axis=0)
            for i in range(2)
        ],
        axis=1,
    ).astype(F32)
    group = info[PLACE] & 3

    def bias_row(i):
        entry = 768 * i + GROUP * group + lax.broadcasted_iota(jnp.int32, (128, WIDE), 1)
        source = lax.broadcasted_iota(jnp.int32, (128, WIDE), 0)
        picked = dot(small.astype(BF16), jnp.where(source == entry % 72, 1.0, 0.0).astype(BF16))
        picked = jnp.where(source[:32] == entry[:32] // 72, picked, 0.0)
        used = lax.broadcasted_iota(jnp.int32, (1, WIDE), 1) < GROUP
        return jnp.where(used, column_sum(picked), 0.0)

    x_out[0:128] = mine[...]
    x_out[128:256] = r2[...]
    x_out[256:384] = r4[...]
    x_out[384:512] = r6[...]
    x_out[512:1024] = odd[...]
    tokens = x_out[...]
    lane = lax.broadcasted_iota(jnp.int32, (1024, WIDE), 1)
    is_even = lane % 2 == 0

    def part(i):
        return dot(tokens, weight[i]) + bias_row(i)

    def turned(value):
        left = pltpu.roll(value, WIDE - 1, 1)
        right = pltpu.roll(value, 1, 1)
        return value * cosine[...] + jnp.where(is_even, left, right) * sine[...]

    query = turned(part(0)).astype(BF16).astype(F32) * (HEAD_DIM**-0.5)
    query = jnp.where(lane == GROUP, 1.0, query).T.astype(BF16)
    qt_out[...] = query
    index = lax.broadcasted_iota(jnp.int32, (1024, WIDE), 0)
    block = index >> 7
    owner = info[PLACE] ^ (((block & 3) << 1) | (block >> 2))
    valid = owner * 128 + (index & 127) < info[LEN_MINE]
    padding = jnp.where(valid, 0.0, NEG_BIG)
    key = jnp.where(lane == GROUP, padding, turned(part(1))).astype(BF16)
    k_out[...] = key
    value = part(2).astype(BF16)
    v_out[...] = value
    value_t = value.astype(F32).T
    ones = jnp.ones((16, 1024), BF16)
    row = lax.broadcasted_iota(jnp.int32, (WIDE, WIDE), 0)
    for h in range(HERE):
        here = (row // HEAD_DIM == h) | (row == GROUP)
        value_h = jnp.concatenate(
            [value_t[HEAD_DIM * h : HEAD_DIM * (h + 1)].astype(BF16), ones], axis=0
        )
        for b in range(4):
            block = qt_out[:, WIDE * b : WIDE * (b + 1)].astype(F32)
            scores = dot(key, jnp.where(here, block, 0.0).astype(BF16))
            top = jnp.max(scores, axis=0, keepdims=True)
            weights = jnp.exp(scores - top).astype(BF16)
            summed = dot(value_h, weights)
            total = summed[HEAD_DIM : HEAD_DIM + 1]
            att_out[HEAD_DIM * h : HEAD_DIM * (h + 1), WIDE * b : WIDE * (b + 1)] = (
                summed[:HEAD_DIM] / total
            )
            stats[h : h + 1, WIDE * b : WIDE * (b + 1)] = top
            stats[4 + h : 5 + h, WIDE * b : WIDE * (b + 1)] = total
    low = att_out[...].T.astype(BF16)
    for i in range(4):
        even_low[i] = low[128 * i : 128 * (i + 1)]
        odd_low[i] = low[512 + 128 * i : 640 + 128 * i]


def small_body(info, given, vectors, up_bias):
    core = info[CORE]
    values = jnp.concatenate(
        [
            jnp.concatenate([given[s, 0:32, 576:640][4 * i : 4 * (i + 1)] for s in range(8)], axis=0)
            for i in range(5)
        ],
        axis=1,
    ).astype(F32)
    entry = lax.broadcasted_iota(jnp.int32, (32, 768), 1)
    source = lax.broadcasted_iota(jnp.int32, (32, 768), 0)
    spread = jnp.where(source == entry % 24, 1.0, 0.0).astype(BF16)
    here = source == entry // 24
    padding = jnp.zeros((32, 8), F32)
    for i in range(6):
        part = jnp.concatenate([values[:, 72 + 24 * i : 96 + 24 * i], padding], axis=1)
        vectors[i : i + 1] = column_sum(jnp.where(here, dot(part.astype(BF16), spread), 0.0))
    entry = lax.broadcasted_iota(jnp.int32, (128, 1536), 1)
    entry = entry // 384 * 768 + core * 384 + entry % 384
    source = lax.broadcasted_iota(jnp.int32, (128, 1536), 0)
    spread = jnp.where(source == entry % 96, 1.0, 0.0).astype(BF16)
    part = jnp.concatenate([values[:, 216:312], jnp.zeros((32, 32), F32)], axis=1)
    part = dot(part.astype(BF16), spread)
    up_bias[...] = column_sum(jnp.where(source[:32] == entry[:32] // 96, part, 0.0))


def pair_body(info, own, came, up_x, up_y, p0, x_out, y_out, p3):
    both = [
        jnp.concatenate([own[i].astype(F32), came[i].astype(F32)], axis=1) for i in range(4)
    ]
    p0[...] = both[0].astype(BF16)
    p3[...] = both[3].astype(BF16)
    x_out[:336] = up_y[:336]
    x_out[336:] = jnp.concatenate([both[1][:64], both[1][64:]], axis=1).astype(BF16)
    y_out[:336] = up_x[336:]
    y_out[336:] = jnp.concatenate([both[2][:64], both[2][64:]], axis=1).astype(BF16)


def proj_rows_body(info, d0, dx, dy, dd, out):
    for i, d in enumerate((d0, dx, dy, dd)):
        out[i] = d[384:480]


def attn_order(info):
    x, core = info[X], info[CORE]
    return ((x, core), (x, 1 - core), (1 - x, core), (1 - x, 1 - core))


def mix_body(
    info, p0, r2, r4, r6, d0, dx, dy, dd, proj_came, mine, other, vectors,
    normed_out, low_out, hat_out, rstd_out, rows_out, proj, held,
):
    core = info[CORE]
    for j, (yy, xx) in enumerate(chips(info)):
        held[rows((yy * 4 + xx * 2 + core) * 96, 96), :] = (d0, dx, dy, dd)[j][384:480]
        held[rows((yy * 4 + xx * 2 + 1 - core) * 96, 96), :] = proj_came[j]
    for i, (xx, cc) in enumerate(attn_order(info)):
        proj[GROUP * i : GROUP * (i + 1)] = held[rows((xx * 2 + cc) * GROUP, GROUP), :]
    rows_out[0:128, 0:384] = p0[...]
    for half in range(2):
        span = slice(384 * half, 384 * (half + 1))
        rows_out[64 * half : 64 * (half + 1), 384:768] = r2[336:, span]
        rows_out[128 + 64 * half : 192 + 64 * half, 0:384] = r4[336:, span]
    rows_out[128:256, 384:768] = r6[...]
    tokens = jnp.concatenate([mine[...], other[...]], axis=0).astype(F32)
    resid = tokens + dot(rows_out[...], proj[...]) + vectors[0:1, :]
    centred = resid - jnp.mean(resid, axis=1, keepdims=True)
    rstd = lax.rsqrt(jnp.mean(centred * centred, axis=1, keepdims=True) + EPSILON)
    hat = centred * rstd
    normed = hat * vectors[1:2, :] + vectors[2:3, :]
    hat_out[...] = hat
    rstd_out[...] = jnp.broadcast_to(rstd, (256, 128))
    normed_out[...] = normed
    low_out[...] = normed.astype(BF16)


def whole_up(info, blocks, held):
    core = info[CORE]
    for block, (yy, xx) in zip(blocks, chips(info)):
        for half in range(2):
            span = slice(768 * half, 768 * (half + 1))
            for i, cc in enumerate((core, 1 - core)):
                held[rows((yy * 4 + xx * 2 + cc) * 96, 96), span] = block[
                    192 * half + 96 * i : 192 * half + 96 * (i + 1)
                ]


def whole_down(info, blocks, early, held):
    z = info[Z]
    for j, (yy, xx) in enumerate(chips(info)):
        base = (yy * 2 + xx) * 384
        for zz in range(4):
            held[rows(base + 96 * zz + 48, 48), :] = blocks[j][480 + 48 * zz : 528 + 48 * zz]
        for k, piece in enumerate(early):
            held[rows(base + 96 * (z ^ k), 48), :] = piece[48 * j : 48 * (j + 1)]


def gelu_parts(upward):
    gauss = jnp.exp(-0.5 * upward * upward)
    t = 1.0 / (1.0 + (0.3275911 * 2.0**-0.5) * jnp.abs(upward))
    poly = t * (
        0.127414796
        + t * (-0.142248368 + t * (0.7107068705 + t * (-0.7265760135 + t * 0.5307027145)))
    )
    tail = poly * gauss
    below = jnp.where(upward < 0, tail, 1.0 - tail)
    return upward * below, below + upward * gauss * 0.3989422804014327


def up_body(
    info, low_mine, low_other, u0, ux, uy, ud, d0, d1, d2, d3, bias,
    part_mine, part_other, active_out, slope_out, up_held, down_held,
):
    whole_up(info, (u0, ux, uy, ud), up_held)
    whole_down(info, (u0, ux, uy, ud), (d0, d1, d2, d3), down_held)
    for i, low in enumerate((low_mine, low_other)):
        upward = dot(low[...], up_held[...]) + bias[...]
        active, slope = gelu_parts(upward)
        active = active.astype(BF16)
        active_out[256 * i : 256 * (i + 1)] = active
        slope_out[256 * i : 256 * (i + 1)] = slope.astype(BF16)
        part = dot(active, down_held[...])
        if i == 0:
            part_mine[...] = part
        else:
            part_other[...] = part.astype(BF16)


def back_norm(d_hat, hat, rstd):
    return rstd * (
        d_hat
        - jnp.mean(d_hat, axis=1, keepdims=True)
        - hat * jnp.mean(d_hat * hat, axis=1, keepdims=True)
    )


def column_sum(value):
    return jnp.sum(value, axis=0, keepdims=True)


def norm_two_body(
    info, part_mine, came, normed, vectors, grad, out, d_resid_out, d_low, sums,
):
    y = info[Y]
    resid = normed[...] + (part_mine[...] + came[...].astype(F32) + vectors[3:4, :])
    centred = resid - jnp.mean(resid, axis=1, keepdims=True)
    rstd = lax.rsqrt(jnp.mean(centred * centred, axis=1, keepdims=True) + EPSILON)
    hat = centred * rstd
    result = (hat * vectors[4:5, :] + vectors[5:6, :]).astype(BF16)
    out[y] = result[:128]
    out[1 - y] = result[128:]
    position = info[PLACE] * 128 + lax.broadcasted_iota(jnp.int32, (128, 768), 0)
    first = jnp.where(position < info[LEN_MINE], grad[y].astype(F32), 0.0)
    second = jnp.where(position < info[LEN_OTHER], grad[1 - y].astype(F32), 0.0)
    cotangent = jnp.concatenate([first, second], axis=0)
    d_resid = back_norm(cotangent * vectors[4:5, :], hat, rstd)
    d_resid_out[...] = d_resid
    low = d_resid.astype(BF16)
    d_low[...] = low
    sums[0:1] = column_sum(low.astype(F32))
    sums[1:2] = column_sum(cotangent * hat)
    sums[2:3] = column_sum(cotangent)


def down_grad_body(info, active, d_mine, d_other, g0, gx, gy, da, db, held):
    d_low = jnp.concatenate([d_mine[...], d_other[...]], axis=0)
    for i in range(4):
        held[384 * i : 384 * (i + 1)] = dot(
            active[:, 384 * i : 384 * (i + 1)], d_low, TN
        ).astype(BF16)
    outs = ((g0,), (gx,), (gy,), (da, db))
    for out, (yy, xx) in zip(outs, chips(info)):
        base = (yy * 2 + xx) * 384
        if len(out) == 1:
            out[0][...] = held[rows(base, 384), :]
        else:
            out[0][...] = held[rows(base, 192), :]
            out[1][...] = held[rows(base + 192, 192), :]


def up_grad_body(
    info, d_mine, d_other, slope, low_mine, low_other, u0, ux, uy, ud, d0, d1, d2, d3,
    part_mine, part_other, g0, gx, gy, gd, z0, z1, z2, z3, sums, up_held, down_held, held,
):
    core = info[CORE]
    whole_up(info, (u0, ux, uy, ud), up_held)
    whole_down(info, (u0, ux, uy, ud), (d0, d1, d2, d3), down_held)
    d_ups = []
    total = jnp.zeros((1, 1536), F32)
    for i, d_low in enumerate((d_mine, d_other)):
        d_active = dot(d_low[...], down_held[...], NT)
        d_up = (slope[256 * i : 256 * (i + 1)].astype(F32) * d_active).astype(BF16)
        total = total + column_sum(d_up.astype(F32))
        d_ups.append(d_up)
        part = dot(d_up, up_held[...], NT)
        if i == 0:
            part_mine[...] = part
        else:
            part_other[...] = part.astype(BF16)
    sums[...] = total
    d_up = jnp.concatenate(d_ups, axis=0)
    low = jnp.concatenate([low_mine[...], low_other[...]], axis=0)
    held[...] = dot(low, d_up, TN)
    z = info[Z]
    for j, (yy, xx) in enumerate(chips(info)):
        for i, cc in enumerate((core, 1 - core)):
            base = (yy * 4 + xx * 2 + cc) * 96
            (g0, gx, gy, gd)[j][96 * i : 96 * (i + 1)] = held[rows(base, 96), :768].astype(BF16)
    for k, out in enumerate((z0, z1, z2, z3)):
        for j, (yy, xx) in enumerate(chips(info)):
            block = [
                held[rows((yy * 4 + xx * 2 + cc) * 96 + (z ^ k) * 24, 24, 8), 768:]
                for cc in (core, 1 - core)
            ]
            out[48 * j : 48 * (j + 1)] = jnp.concatenate(block, axis=0).astype(BF16)


def norm_one_body(
    info, d_resid_two, part_mine, came, hat, rstd, vectors, rows_here, proj,
    d_resid_out, e0, e2, e4, e6, proj_own, proj_sent, sums, held,
):
    core = info[CORE]
    d_normed = d_resid_two[...] + part_mine[...] + came[...].astype(F32)
    sums[0:1] = column_sum(d_normed * hat[...])
    sums[1:2] = column_sum(d_normed)
    d_resid = back_norm(d_normed * vectors[1:2, :], hat[...], rstd[:, 0:1])
    d_resid_out[...] = d_resid
    low = d_resid.astype(BF16)
    sums[2:3] = column_sum(low.astype(F32))
    d_att = dot(low, proj[...], NT).astype(BF16)
    e0[...] = d_att[:128, :384]
    e2[...] = d_att[:128, 384:]
    e4[...] = d_att[128:, :384]
    e6[...] = d_att[128:, 384:]
    d_weight = dot(rows_here[...], low, TN).astype(BF16)
    for i, (xx, cc) in enumerate(attn_order(info)):
        held[rows((xx * 2 + cc) * GROUP, GROUP), :] = d_weight[GROUP * i : GROUP * (i + 1)]
    for j, (yy, xx) in enumerate(chips(info)):
        proj_own[j] = held[rows((yy * 4 + xx * 2 + core) * 96, 96), :]
        proj_sent[j] = held[rows((yy * 4 + xx * 2 + 1 - core) * 96, 96), :]


def split_core_body(info, e0, e2, e4, e6, out):
    for i, e in enumerate((e0, e2, e4, e6)):
        out[128 * i : 128 * (i + 1)] = e[...].astype(F32)[:, GROUP:].astype(BF16)


def attend_back_body(
    info, e0, e2, e4, e6, came, qt, key, value, att, stats, cosine_all, sine_all,
    d_proj, sums, guide, weights_held, d_scores_held, dq_held, dk_held, dv_held, cosine, sine,
):
    place_tables(info, cosine_all, sine_all, cosine, sine)
    d_att = jnp.concatenate(
        [e[...].astype(F32)[:, :GROUP] for e in (e0, e2, e4, e6)] + [came[...].astype(F32)], axis=0
    )
    d_att_t = d_att.T
    product = d_att_t * att[...]
    pieces = []
    deltas = []
    for h in range(HERE):
        here = slice(HEAD_DIM * h, HEAD_DIM * (h + 1))
        total = stats[4 + h : 5 + h, :]
        pieces.append(d_att_t[here] / total)
        deltas.append(column_sum(product[here]) / total)
    pieces.append(jnp.zeros((WIDE - GROUP, 1024), F32))
    guide[...] = jnp.concatenate(pieces, axis=0).astype(BF16)
    key_t = key[...].astype(F32).T
    row = lax.broadcasted_iota(jnp.int32, (WIDE, WIDE), 0)
    dk_held[...] = jnp.zeros((1024, WIDE), F32)
    dv_held[...] = jnp.zeros((1024, WIDE), F32)
    dq_held[GROUP:] = jnp.zeros((WIDE - GROUP, 1024), F32)
    wide_row = lax.broadcasted_iota(jnp.int32, (WIDE, 1024), 0)
    for h in range(HERE):
        mine = row // HEAD_DIM == h
        with_pad = mine | (row == GROUP)
        key_h = key_t[HEAD_DIM * h : HEAD_DIM * (h + 1)].astype(BF16)
        for b in range(4):
            span = slice(WIDE * b, WIDE * (b + 1))
            q_block = jnp.where(with_pad, qt[:, span].astype(F32), 0.0).astype(BF16)
            g_block = jnp.where(mine, guide[:, span].astype(F32), 0.0).astype(BF16)
            scores = dot(key[...], q_block)
            weights = jnp.exp(scores - stats[h : h + 1, span])
            d_weights = dot(value[...], g_block)
            d_scores = (weights * (d_weights - deltas[h][:, span])).astype(BF16)
            weights_held[:, span] = weights.astype(BF16)
            d_scores_held[:, span] = d_scores
            dq_held[HEAD_DIM * h : HEAD_DIM * (h + 1), span] = dot(key_h, d_scores)
        here = wide_row // HEAD_DIM == h
        q_all = jnp.where(here, qt[...].astype(F32), 0.0).astype(BF16)
        g_all = jnp.where(here, guide[...].astype(F32), 0.0).astype(BF16)
        dk_held[...] += dot(d_scores_held[...], q_all, NT)
        dv_held[...] += dot(weights_held[...], g_all, NT)
    lane = lax.broadcasted_iota(jnp.int32, (1024, WIDE), 1)
    is_even = lane % 2 == 0

    def turned_back(value):
        left = pltpu.roll(value, WIDE - 1, 1)
        right = pltpu.roll(value, 1, 1)
        return value * cosine[...] - jnp.where(is_even, left, right) * sine[...]

    d_query = turned_back(dq_held[...].T * (HEAD_DIM**-0.5)).astype(BF16)
    d_key = turned_back(dk_held[...]).astype(BF16)
    d_value = dv_held[...].astype(BF16)
    for i, part in enumerate((d_query, d_key, d_value)):
        d_proj[i] = part
        sums[i : i + 1] = column_sum(part.astype(F32))


def attn_grad_body(info, tokens, d_proj, small, out):
    parts = [dot(tokens[...], d_proj[i], TN)[:, :GROUP] for i in range(3)]
    whole = jnp.concatenate(parts, axis=1)
    for s in range(8):
        beside = jnp.concatenate([small[s], jnp.zeros((56, 64), F32)], axis=0)
        out[s] = jnp.concatenate([whole[96 * s : 96 * (s + 1)], beside], axis=1).astype(BF16)


def sum_four_body(info, first, r1, r2, r3, out):
    out[...] = (
        first[...] + r1[...].astype(F32) + r2[...].astype(F32) + r3[...].astype(F32)
    )


def hidden_grad_body(info, d_proj, weight, even_out, odd_out):
    total = jnp.zeros((1024, 768), F32)
    for i in range(3):
        total = total + dot(d_proj[i], weight[i], NT)
    even_out[...] = total[:512]
    odd_out[...] = total[512:].astype(BF16)


def first_sums_body(info, jx, cy, jy, cx, down, x_out, y_out, first, s1, s2, s3, held):
    x_out[:144] = jx[:144]
    x_out[144:] = (jx[144:].astype(F32) + cy[384:].astype(F32)).astype(BF16)
    y_out[:144] = (jy[:144].astype(F32) + cx[384:].astype(F32)).astype(BF16)
    y_out[144:] = jy[144:]
    z = info[Z]
    held[...] = down[...].astype(F32) + cx[:384].astype(F32) + cy[:384].astype(F32)
    for k, out in enumerate((first, s1, s2, s3)):
        out[...] = held[rows((z ^ k) * 96, 96), :].astype(out.dtype)


def second_sums_body(info, even, came, u0, u1, u2, u3, own, half_first, x_out, y_out, across):
    hidden = even[...] + came[...].astype(F32)
    up = u0[...].astype(F32) + u1[...].astype(F32) + u2[...].astype(F32) + u3[...].astype(F32)
    own[...] = hidden[:128]
    half_first[...] = up[:48]
    for i, out in enumerate((x_out, y_out, across)):
        out[:48] = up[48 * (i + 1) : 48 * (i + 2)].astype(BF16)
        out[48:] = hidden[128 * (i + 1) : 128 * (i + 2)].astype(BF16)


def small_grads_body(info, attn, one, two, up, out):
    core = info[CORE]
    group = info[PLACE] & 3

    def split(value, place):
        n = value.shape[1]
        entry = lax.broadcasted_iota(jnp.int32, (1, n), 1)
        return jnp.where(
            lax.broadcasted_iota(jnp.int32, (32, n), 0) == place(entry), value, 0.0
        )

    def gather(value, width):
        n = value.shape[1]
        entry = lax.broadcasted_iota(jnp.int32, (n, 1), 0) % width
        chosen = jnp.where(lax.broadcasted_iota(jnp.int32, (n, 128), 1) == entry, 1.0, 0.0)
        chosen = chosen.astype(BF16)
        high = value.astype(BF16)
        return dot(high, chosen) + dot((value - high.astype(F32)).astype(BF16), chosen)

    inside = lax.broadcasted_iota(jnp.int32, (1, WIDE), 1) < GROUP
    own = [jnp.where(inside, attn[i : i + 1], 0.0) for i in range(3)]
    pairs = gather(
        split(own[0], lambda n: 4 * group + n // 48)
        + split(own[1], lambda n: 16 + 4 * group + n // 48),
        48,
    )
    values = gather(split(own[2], lambda n: 8 * group + n // 24), 24)
    six = (one[2:3], one[0:1], one[1:2], two[0:1], two[1:2], two[2:3])
    six = gather(jnp.concatenate([split(v, lambda n: n // 24) for v in six], axis=0), 24)
    ups = gather(split(up[...], lambda n: n // 96 + 4 * (n // 384) + 4 * core), 96)
    parts = [pairs[:, :48], values[:, :24]]
    parts += [six[32 * i : 32 * (i + 1), :24] for i in range(6)]
    parts += [ups[:, :96], jnp.zeros((32, 8), F32)]
    row = jnp.concatenate(parts, axis=1)
    high = row.astype(BF16).astype(F32)
    for s in range(8):
        here = slice(4 * s, 4 * (s + 1))
        out[s] = jnp.concatenate(
            [v[here, 64 * i : 64 * (i + 1)] for v in (high, row - high) for i in range(5)], axis=0
        )


def last_blocks_body(info, own, a, b, came, first, s1, s2, s3, up_held, attn_held, small_held):
    z = info[Z]
    up_held[...] = own[...].astype(F32) + a[...].astype(F32) + b[...].astype(F32)
    for g in range(4):
        attn_held[g] = came[g].astype(F32) + came[4 + g].astype(F32)
    small = sum(attn_held[g, :40, 576:] for g in range(4))
    small = small[:20] + small[20:]
    pad = jnp.zeros((1, 64), F32)
    for zz in range(4):
        small_held[zz] = jnp.concatenate(
            [small[4 * i + zz : 4 * i + zz + 1] for i in range(5)] + [pad], axis=1
        )
    for k, out in enumerate((first, s1, s2, s3)):
        parts = [up_held[rows(96 * i + (z ^ k) * 24, 24, 8), :] for i in range(3)]
        blocks = [attn_held[g, rows((z ^ k) * 24, 24, 8), :] for g in range(4)]
        for i in range(3):
            parts.append(
                jnp.concatenate([b[:, GROUP * i : GROUP * (i + 1)] for b in blocks], axis=1)
            )
        row = small_held[z ^ k]
        high = row.astype(BF16).astype(F32)
        parts.append(jnp.concatenate([high, row - high], axis=1))
        parts.append(jnp.zeros((7, 768), F32))
        out[...] = jnp.concatenate(parts, axis=0).astype(out.dtype)


def last_sum_body(info, first, r1, r2, r3, half, proj_out, attn_out, small):
    total = first[...] + r1[...].astype(F32) + r2[...].astype(F32) + r3[...].astype(F32)
    half[...] = total[:48]
    proj_out[...] = total[48:72]
    for i in range(3):
        attn_out[:, 768 * i : 768 * (i + 1)] = total[72 + 24 * i : 96 + 24 * i]
    small[...] = total[144:145, :384] + total[144:145, 384:]


def end_sum_body(info, half, other_half, d_resid, hidden, r2, r4, r6, own, sent, out):
    y = info[Y]
    other = other_half[...] + r2[:48].astype(F32) + r4[:48].astype(F32) + r6[:48].astype(F32)
    own[...] = jnp.concatenate([half[:24], other[:24]], axis=1)
    sent[...] = jnp.concatenate([half[24:], other[24:]], axis=1).astype(BF16)
    out[y] = d_resid[:128] + hidden[...] + r2[48:].astype(F32)
    out[1 - y] = d_resid[128:] + r4[48:].astype(F32) + r6[48:].astype(F32)


def up_end_body(info, own, came, up_out):
    core = info[CORE]
    for which, source in ((core, own), (1 - core, came)):
        for q in range(4):
            up_out[:, lanes(768 * q + 384 * which, 384)] = source[
                :, 384 * q : 384 * (q + 1)
            ].astype(F32)


def join_body(
    info, g0, gx, gy, gd, p_own, p_came, dx, d_from_y, dy, d_from_x, j0, jx, jy, mx, my
):
    proj = [(p_own[j].astype(F32) + p_came[j].astype(F32)).astype(BF16) for j in range(4)]
    for j, (g, out) in enumerate(((g0, j0), (gx, jx), (gy, jy))):
        out[:192] = g[...]
        out[192:] = proj[j]
    mx[:192] = dx[:192]
    mx[192:384] = (dx[192:].astype(F32) + d_from_y[...].astype(F32)).astype(BF16)
    my[:192] = (dy[:192].astype(F32) + d_from_x[...].astype(F32)).astype(BF16)
    my[192:384] = dy[192:]
    mx[384:] = gd[:144]
    my[384:432] = gd[144:]
    my[432:] = proj[3]
def split_layer(
    hidden_in,
    lengths,
    attn_weight,
    attn_bias,
    proj_weight,
    proj_bias,
    first_gain,
    first_shift,
    up_weight,
    up_bias,
    down_weight,
    down_bias,
    second_gain,
    second_shift,
    grad_out,
):
    both_axes = ("seq", "batch")
    info = lengths

    small_vectors = (
        attn_bias, proj_bias, first_gain, first_shift, down_bias, second_gain, second_shift, up_bias
    )
    mine, other, joined, early, attn_wide = call(
        prepare_body,
        [
            shape((128, 768)), shape((128, 768)), shape((24, 5376)), shape((48, 768)),
            shape((4, 24, 2432)),
        ],
        info, hidden_in, attn_weight, up_weight, proj_weight, down_weight,
        *[v[None] for v in small_vectors], name="prepare", alone=True,
    )
    cosine, sine = (jnp.asarray(table) for table in rotary_tables(8 * 128))
    attn_wide = lax.all_to_all(attn_wide, "batch", 0, 0, tiled=True)
    far = [swap_batch(joined, k) for k in (1, 2, 3)]
    r2, r4, r6 = swap_seq(mine, 2), swap_seq(other, 4), swap_seq(other, 6)
    odd = swap_seq(jnp.concatenate([mine, r2, r4, r6], axis=0), 1)
    early_far = [swap_seq(early, k) for k in (2, 4, 6)]
    (early_plane,) = call(early_body, [shape((192, 768))], info, early, *early_far, name="early")
    (weight_sent,) = call(
        attn_column_body, [shape((8, 96, 640))], info, after(attn_wide, far[0], far[1], *early_far),
        name="attn_column",
    )
    weight_given = lax.all_to_all(weight_sent, "seq", 0, 0, tiled=True)
    up_keep, up_sent, rest = call(
        up_column_body, [shape((192, 768)), shape((192, 768)), shape((288, 768))],
        info, joined, *far, scratch=[shape((96, 3072))], name="up_column",
    )
    (up_column,) = call(
        up_join_body, [shape((672, 768))], info, up_keep, swap_seq(up_sent, 1), rest,
        name="up_join",
    )
    up_column, early_plane, odd, weight_given = fence(up_column, early_plane, odd, weight_given)

    up_x, up_y = swap_seq(up_column, 2), swap_seq(up_column, 4)
    early_far = [swap_batch(early_plane, k) for k in (1, 2, 3)]

    tokens_here, weight_here, query_t, key, value, attended, stats, even_low, odd_low = call(
        attend_body,
        [
            shape((1024, 768)), shape((3, 768, WIDE)),
            shape((WIDE, 1024)), shape((1024, WIDE)), shape((1024, WIDE)),
            shape((GROUP, 1024), F32), shape((8, 1024), F32),
            shape((4, 128, GROUP)), shape((4, 128, GROUP)),
        ],
        info, mine, r2, r4, r6, odd, weight_given, cosine, sine,
        scratch=[shape((1024, WIDE), F32)] * 2, flops=8_000_000_000, name="attend", alone=True,
    )
    even_low, odd_low, up_x, up_y, weight_given = fence(even_low, odd_low, up_x, up_y, weight_given)

    p0, to_x, to_y, p3 = call(
        pair_body, [shape((128, 384)), shape((400, 768)), shape((400, 768)), shape((128, 384))],
        info, even_low, swap_seq(odd_low, 1), up_x, up_y, name="pair",
    )
    p0, to_x, to_y, p3, early_far = fence(p0, to_x, to_y, p3, early_far)

    a2, a4, a6 = swap_seq(to_x, 2), swap_seq(to_y, 4), swap_seq(p3, 6)
    vectors, up_bias_here = call(
        small_body, [shape((8, 768), F32), shape((1, 1536), F32)], info, after(weight_given, p0), name="small"
    )
    a2, a4, a6, vectors, up_bias_here = fence(a2, a4, a6, vectors, up_bias_here)
    up_blocks = (up_column, up_x, up_y, jnp.concatenate([a2[:336], a4[:336]], axis=0))
    down_blocks = (early_plane, *early_far)
    (proj_rows,) = call(proj_rows_body, [shape((4, 96, 768))], info, *up_blocks, name="proj_rows")
    proj_came = swap_seq(proj_rows, 1)
    normed, low_mine, hat_one, rstd_one, rows_here, proj_here = call(
        mix_body,
        [
            shape((256, 768), F32), shape((256, 768)), shape((256, 768), F32),
            shape((256, 128), F32), shape((256, 768)), shape((768, 768)),
        ],
        info, p0, a2, a4, a6, *up_blocks, proj_came, mine, other, vectors,
        scratch=[shape((768, 768))], flops=300_000_000, name="mix",
    )
    low_other = swap_seq(low_mine, 1)
    part_mine, part_other, active, slope = call(
        up_body,
        [shape((256, 768), F32), shape((256, 768)), shape((512, 1536)), shape((512, 1536))],
        info, low_mine, low_other, *up_blocks, *down_blocks, up_bias_here,
        scratch=[shape((768, 1536)), shape((1536, 768))], flops=2_400_000_000, name="up",
    )
    layer_out, d_resid_two, d_low, sums_two = call(
        norm_two_body,
        [shape((2, 128, 768)), shape((256, 768), F32), shape((256, 768)), shape((8, 768), F32)],
        info, part_mine, swap_seq(part_other, 1), normed, vectors, grad_out, name="norm_two",
    )
    d_came = swap_seq(d_low, 1)
    g_down, gx_down, gy_down, gda, gdb = call(
        down_grad_body, [shape((384, 768))] * 3 + [shape((192, 768))] * 2,
        info, active, d_low, d_came,
        scratch=[shape((1536, 768))], flops=1_200_000_000, name="down_grad",
    )
    gx_down, gy_down, gda, gdb, d_low, d_came = fence(gx_down, gy_down, gda, gdb, d_low, d_came)

    gda, gdb = swap_seq(gda, 2), swap_seq(gdb, 4)
    part_mine, part_other, g0, gx, gy, gd, z0, z1, z2, z3, up_sums = call(
        up_grad_body,
        [shape((256, 768), F32), shape((256, 768))] + [shape((192, 768))] * 8
        + [shape((1, 1536), F32)],
        info, d_low, d_came, slope, low_mine, low_other, *up_blocks, *down_blocks,
        scratch=[shape((768, 1536)), shape((1536, 768)), shape((768, 1536), F32)],
        flops=3_600_000_000, name="up_grad",
    )
    gda, gdb, part_mine, part_other = fence(gda, gdb, part_mine, part_other)
    d_resid_one, e0, e2, e4, e6, proj_own, proj_sent, sums_one = call(
        norm_one_body,
        [shape((256, 768), F32)] + [shape((128, 384))] * 4 + [shape((4, 96, 768))] * 2
        + [shape((8, 768), F32)],
        info, d_resid_two, part_mine, swap_seq(part_other, 1), hat_one, rstd_one, vectors,
        rows_here, proj_here,
        scratch=[shape((768, 768))], flops=600_000_000, name="norm_one",
    )
    e0, e2, e4, e6, proj_sent = fence(e0, e2, e4, e6, proj_sent)

    e2, e4, e6 = swap_seq(e2, 2), swap_seq(e4, 4), swap_seq(e6, 6)
    proj_came = swap_seq(proj_sent, 1)
    j0, jx, jy, mx, my = call(
        join_body, [shape((288, 768))] * 3 + [shape((528, 768))] * 2,
        info, g0, gx, gy, gd, proj_own, proj_came, gx_down, gdb, gy_down, gda, name="join",
    )
    e2, e4, e6, j0, jx, jy, mx, my = fence(e2, e4, e6, j0, jx, jy, mx, my)
    (split,) = call(split_core_body, [shape((512, GROUP))], info, e0, e2, e4, e6, name="split")
    e_came = swap_seq(split, 1)
    e_came, mx, my, z1, z2, z3 = fence(e_came, mx, my, z1, z2, z3)

    mx, my = swap_seq(mx, 2), swap_seq(my, 4)
    z_came = [swap_batch(part, k) for k, part in zip((1, 2, 3), (z1, z2, z3))]
    d_proj, sums_attn = call(
        attend_back_body,
        [shape((3, 1024, WIDE)), shape((8, WIDE), F32)],
        info, e0, e2, e4, e6, e_came, query_t, key, value, attended, stats, cosine, sine,
        scratch=[
            shape((WIDE, 1024)), shape((1024, 1024)), shape((1024, 1024)),
            shape((WIDE, 1024), F32), *[shape((1024, WIDE), F32)] * 4,
        ],
        flops=8_000_000_000, name="attend_back",
    )
    (small_grads,) = call(
        small_grads_body, [shape((8, 40, 64), F32)], info, sums_attn, sums_one, sums_two, up_sums,
        name="small_grads",
    )
    (w_sent,) = call(
        attn_grad_body, [shape((8, 96, 640))], info, tokens_here, d_proj, small_grads,
        flops=1_200_000_000, name="attn_grad",
    )
    even, odd_sent = call(
        hidden_grad_body, [shape((512, 768), F32), shape((512, 768))], info, d_proj, weight_here,
        flops=1_200_000_000, name="hidden_grad",
    )
    w_came = lax.all_to_all(w_sent, "seq", 0, 0, tiled=True)
    mx, my, z_came, odd_sent, _ = fence(mx, my, z_came, odd_sent, w_sent)

    jx, jy, first, b1, b2, b3 = call(
        first_sums_body,
        [shape((288, 768))] * 2 + [shape((96, 768), F32)] + [shape((96, 768))] * 3,
        info, jx, my, jy, mx, g_down, scratch=[shape((384, 768), F32)], name="first_sums",
        alone=True,
    )
    jx, jy = swap_seq(jx, 2), swap_seq(jy, 4)
    b1, b2, b3 = [swap_batch(b, k) for k, b in ((1, b1), (2, b2), (3, b3))]
    own, half_first, s2, s4, s6 = call(
        second_sums_body,
        [shape((128, 768), F32), shape((48, 768), F32)] + [shape((176, 768))] * 3,
        info, even, swap_seq(odd_sent, 1), z0, *z_came, name="second_sums",
    )
    jx, jy, s2, s4, s6, w_came, b1, b2, b3 = fence(jx, jy, s2, s4, s6, w_came, b1, b2, b3)

    last_first, *last_sends = call(
        last_blocks_body, [shape((152, 768), F32)] + [shape((152, 768))] * 3,
        info, j0, jx, jy, w_came,
        scratch=[shape((288, 768), F32), shape((4, 96, 640), F32), shape((4, 1, 384), F32)],
        name="last_blocks",
    )
    last_came = [swap_batch(part, k) for k, part in zip((1, 2, 3), last_sends)]
    s2, s4, s6 = swap_seq(s2, 2), swap_seq(s4, 4), swap_seq(s6, 6)
    (grad_down_weight,) = call(
        sum_four_body, [shape((96, 768), F32)], info, first, b1, b2, b3, name="down_end"
    )
    up_half, grad_proj_weight, grad_attn_weight, d_small = call(
        last_sum_body,
        [shape((48, 768), F32), shape((24, 768), F32), shape((24, 2304), F32), shape((1, 384), F32)],
        info, last_first, *last_came, name="last_sum",
    )
    up_own, up_sent, grad_hidden = call(
        end_sum_body,
        [shape((24, 1536), F32), shape((24, 1536)), shape((2, 128, 768), F32)],
        info, up_half, half_first, d_resid_one, own, s2, s4, s6, name="end_sum",
    )
    (grad_up_weight,) = call(
        up_end_body, [shape((24, 3072), F32)], info, up_own, swap_seq(up_sent, 1), name="up_end"
    )

    d_small = d_small[0]
    d_vectors = [d_small[72 + 24 * i : 96 + 24 * i] for i in range(6)]
    return (
        layer_out,
        grad_hidden,
        grad_attn_weight,
        d_small[:48],
        d_small[48:72],
        grad_proj_weight,
        d_vectors[0],
        d_vectors[1],
        d_vectors[2],
        grad_up_weight,
        d_small[216:312],
        grad_down_weight,
        d_vectors[3],
        d_vectors[4],
        d_vectors[5],
    )


def solution(mesh):
    in_specs = (
        P("batch", "seq", None),
        P("batch"),
        P(("seq", "batch"), None),
        P(("seq", "batch")),
        P(("seq", "batch"), None),
        P(("seq", "batch")),
        P(("seq", "batch")),
        P(("seq", "batch")),
        P(("seq", "batch"), None),
        P(("seq", "batch")),
        P(("seq", "batch"), None),
        P(("seq", "batch")),
        P(("seq", "batch")),
        P(("seq", "batch")),
        P("batch", "seq", None),
    )
    out_specs = (
        P("batch", "seq", None),
        P("batch", "seq", None),
        P(("seq", "batch"), None),
        P(("seq", "batch")),
        P(("seq", "batch")),
        P(("seq", "batch"), None),
        P(("seq", "batch")),
        P(("seq", "batch")),
        P(("seq", "batch")),
        P(("seq", "batch"), None),
        P(("seq", "batch")),
        P(("seq", "batch"), None),
        P(("seq", "batch")),
        P(("seq", "batch")),
        P(("seq", "batch")),
    )
    fits = mesh.shape["seq"] == SEQ_SIDE and mesh.shape["batch"] == BATCH_SIDE
    return jax.shard_map(
        split_layer if fits else on_device, mesh=mesh, in_specs=in_specs, out_specs=out_specs, check_vma=False
    )
```
